32 devices in a mesh: head: 8 (over z, y), ctx: 4 (over x, core).
Axes of the slice: x: 2, y: 2, z: 4, core: 2. Of those that a mesh axis runs over, the one named last changes fastest.
Arguments:
- latent: bfloat16 [4, 16, 512], P('ctx', 'head'), may hold values from -6 to 6
- gain: float32 [512], replicated, may hold values from 0.1 to 1.9
- cotangent: bfloat16 [4, 16, 64, 256], P('ctx', None, 'head'), may hold values from -1 to 1
- weight: bfloat16 [512, 64, 256], P('ctx', 'head'), may hold values from -0.25 to 0.25
Outputs:
- latent_gradient: float32 [4, 16, 512], P('ctx', 'head')
- weight_grad: float32 [512, 64, 256], P('ctx', 'head')
The draws below stay inside these ranges and needn't reach their ends.
All inputs are finite; a program needn't handle non-finite values.
Results may differ from the reference program's by a relative error of at most 0.0029.
Values may be sent and summed in bfloat16 or wider, within the bound.
No kernel may reach another device: no remote copies, remote signals or barrier semaphores. Data moves between devices by JAX's collectives and lax.ppermute only.
A program may use at most 64 MiB of HBM per device.

```python
import jax
import jax.numpy as jnp
from jax import lax

HEADS = 64
LATENT = 512
KV = 256
CTX_TOK = 16
SHARDS = 4


def spiked(values, key, source, target, parts, factor):
    def block_of(dim):
        return (jnp.arange(values.shape[dim]) // (values.shape[dim] // parts)).reshape((-1,) + (1,) * (values.ndim - 1 - dim))

    first = jax.random.permutation(key, parts)[block_of(target)]
    far = (block_of(target) + parts // 2) % parts
    return jnp.where((block_of(source) == first) | (block_of(source) == far), factor * values, values)


def shard_levels(key, extent, cuts, low, high):
    def one(axis_at, parts):
        steps = jax.random.uniform(jax.random.fold_in(jax.random.fold_in(key, 6), axis_at), (parts,), jnp.float32, low / len(cuts), high / len(cuts))
        return jnp.repeat(jnp.exp(steps), extent[axis_at] // parts).reshape((-1,) + (1,) * (len(extent) - axis_at - 1))

    loudness = one(*cuts[0])
    for cut in cuts[1:]:
        loudness = loudness * one(*cut)
    return loudness


def gaussian(rng, shape, deviation, most, cuts=(), held_as=jnp.bfloat16):
    factor_of = shard_levels(rng, shape, cuts, -0.22, 0.18) if cuts else 1.0
    array = jax.random.normal(rng, shape, jnp.float32) * deviation * factor_of
    return jnp.minimum(jnp.maximum(array, -most), most).astype(held_as)


def bell_draw_with(own_key, extent, spread, bound, cuts, heavy, kind=jnp.bfloat16):
    result = spread * jax.random.normal(own_key, extent, jnp.float32)
    if cuts:
        result = result * shard_levels(own_key, extent, cuts, -0.22, 0.18)
    return jnp.clip(spiked(result, jax.random.fold_in(own_key, 3), *heavy), -bound, bound).astype(kind)


def setup_inputs(seed: int = 0) -> dict:
    seeds = jax.random.split(jax.random.key(seed), 5)
    latent = gaussian(seeds[0], (SHARDS, CTX_TOK, LATENT), 1.0, 6.0, ((0, 4), (1, 8)))
    gain = jnp.clip(1.0 + 0.18 * jax.random.normal(seeds[1], (LATENT,), jnp.float32), 0.1, 1.9)
    cotangent = bell_draw_with(seeds[2], (SHARDS, CTX_TOK, HEADS, KV), 0.125, 1.0, ((0, 4), (2, 8)), (2, 1, 8, 2.0))
    weight = gaussian(seeds[3], (LATENT, HEADS, KV), LATENT ** -0.5, 0.25, ((0, 4), (1, 8)))
    return dict(latent=latent, gain=gain, cotangent=cotangent, weight=weight)


def reference(latent, gain, cotangent, weight):
    raw_latent = latent.astype(jnp.float32).reshape(-1, LATENT)
    root_mean_square = lax.rsqrt(lax.optimization_barrier(jnp.mean(raw_latent * raw_latent, axis=1, keepdims=True)) + 1e-06)
    latent_hat = raw_latent * root_mean_square
    normed_latent = (latent_hat * gain).astype(jnp.bfloat16)
    flat = cotangent.reshape(-1, HEADS * KV)
    weight_flat = weight.reshape(LATENT, HEADS * KV)
    grad_normed = lax.dot_general(flat, weight_flat, (((1,), (1,)), ((), ())), preferred_element_type=jnp.float32)
    weight_grad = lax.dot_general(normed_latent, flat, (((0,), (0,)), ((), ())), preferred_element_type=jnp.float32)
    scaled_latent = grad_normed * gain
    inner_product = lax.optimization_barrier(jnp.mean(scaled_latent * latent_hat, axis=1, keepdims=True))
    latent_gradient = root_mean_square * (scaled_latent - latent_hat * inner_product)
    return (latent_gradient.reshape(latent.shape), weight_grad.reshape(LATENT, HEADS, KV))
```

```python
import functools

import jax
import jax.numpy as jnp
from jax import lax
from jax.experimental import pallas as pl
from jax.experimental.pallas import tpu as pltpu
from jax.sharding import PartitionSpec as P


F32 = jnp.float32
BF16 = jnp.bfloat16


def iota(shape, axis):
    return lax.broadcasted_iota(jnp.int32, shape, axis)


def one_hot(condition):
    return jnp.where(condition, 1.0, 0.0).astype(BF16)


def matmul(a, b, a_axis=1, b_axis=0):
    return lax.dot_general(a, b, (((a_axis,), (b_axis,)), ((), ())), preferred_element_type=F32)


def reverse_bits(value, count):
    out = 0
    for bit in range(count):
        out = out | (((value >> bit) & 1) << (count - 1 - bit))
    return out


def weight_kernel(heads, own_ref, other_ref, out_ref):
    core = lax.axis_index("ctx") & 1
    rows = own_ref.shape[0] // heads
    group = min(rows, max(256 // heads, 1))
    size = group * heads
    to, at = iota((size, size), 0), iota((size, size), 1)
    order = one_hot(at == (to % group) * heads + to // group)
    for ref, place in ((own_ref, core), (other_ref, 1 - core)):
        for start in range(0, rows, group):
            moved = matmul(order, ref[pl.ds(start * heads, size), :]).astype(BF16)
            first = pl.multiple_of(place * rows + start, group)
            for h in range(heads):
                out_ref[h, pl.ds(first, group), :] = moved[h * group : (h + 1) * group, :]


def partial_kernel(head_count, heads, owned, *refs):
    shard_refs, weight_ref, out_ref = refs[:-2], refs[-2], refs[-1]
    shards = len(shard_refs)
    me = lax.axis_index("head")
    bits = head_count.bit_length() - 1
    rows = head_count * owned
    stacked = jnp.concatenate([ref[...] for ref in shard_refs], axis=0)
    size = shards * rows * heads
    to, at = iota((size, size), 0), iota((size, size), 1)
    i, j = to % owned, (to // owned) % shards
    position = (to // (owned * shards)) % head_count
    token = (reverse_bits(position, bits) ^ me) * owned + i
    order = one_hot(at == (j * rows + token) * heads + to // (rows * shards))
    moved = matmul(order, stacked).astype(BF16)
    part = rows * shards
    total = matmul(moved[:part], weight_ref[0], 1, 1)
    for h in range(1, heads):
        total += matmul(moved[h * part : (h + 1) * part], weight_ref[h], 1, 1)
    out_ref[...] = total


def norm_kernel(columns, latent_ref, gain_ref, *out_refs):
    column = lax.axis_index("ctx") >> 1
    raw = latent_ref[...].astype(F32)
    rms = lax.rsqrt(jnp.mean(raw * raw, axis=1, keepdims=True) + 1e-06)
    normed = ((raw * rms) * gain_ref[...]).astype(BF16).astype(F32)
    width = normed.shape[1] // columns
    for j, ref in enumerate(out_refs):
        block = normed[:, :width]
        for b in range(1, columns):
            block = jnp.where((column ^ j) == b, normed[:, b * width : (b + 1) * width], block)
        ref[...] = block


def weight_grad_kernel(head_count, heads, owned, columns, normed_ref, *refs):
    shard_refs, out_ref, scratch_ref = refs[:-2], refs[-2], refs[-1]
    me = lax.axis_index("head")
    core = lax.axis_index("ctx") & 1
    rows = out_ref.shape[0] // heads
    tokens = head_count * owned
    normed = normed_ref[...].astype(BF16)
    size = columns * tokens * heads
    at, to = iota((normed.shape[0], size), 0), iota((normed.shape[0], size), 1)
    token, j = (to // heads) % tokens, to // (heads * tokens)
    cots = []
    for side in range(2):
        place = (((token // owned) ^ me) * 2 + (core ^ side)) * columns + j
        spread = one_hot(at == place * owned + token % owned)
        scratch_ref[side] = matmul(normed, spread, 0, 0)
        cots.append(jnp.concatenate([r[...] for r in shard_refs[side * columns : (side + 1) * columns]], axis=0))
    group = min(rows, max(256 // heads, 1))
    keep = (iota((1, heads, size), 2) % heads) == iota((1, heads, size), 1)
    for start in range(0, rows, group):
        total = None
        for side in range(2):
            block = scratch_ref[side, pl.ds(pl.multiple_of(core * rows + start, group), group), :]
            left = jnp.where(keep, block[:, None, :], 0.0).reshape(group * heads, size).astype(BF16)
            part = matmul(left, cots[side])
            total = part if total is None else total + part
        out_ref[start * heads : (start + group) * heads, :] = total


def latent_kernel(columns, latent_ref, gain_ref, *refs):
    block_refs, out_ref = refs[:-1], refs[-1]
    column = lax.axis_index("ctx") >> 1
    raw = latent_ref[...].astype(F32)
    rms = lax.rsqrt(jnp.mean(raw * raw, axis=1, keepdims=True) + 1e-06)
    hat = raw * rms
    blocks = []
    for b in range(columns):
        block = block_refs[0][...]
        for j in range(1, columns):
            block = jnp.where((column ^ j) == b, block_refs[j][...], block)
        blocks.append(block)
    scaled = jnp.concatenate(blocks, axis=1) * gain_ref[...]
    inner = jnp.mean(scaled * hat, axis=1, keepdims=True)
    out_ref[...] = rms * (scaled - hat * inner)


def per_device(head_count, ctx_count, latent, gain, cotangent, weight):
    columns = ctx_count // 2
    owned, width = latent.shape[1:]
    _, tokens, heads, channels = cotangent.shape
    rows = weight.shape[0]
    params = pltpu.CompilerParams(vmem_limit_bytes=48 * 1024 * 1024)

    def ctx_swap(value, mask):
        return lax.ppermute(value, "ctx", [(i, i ^ mask) for i in range(ctx_count)])

    def head_swap(value, mask):
        return lax.ppermute(value, "head", [(i, i ^ mask) for i in range(head_count)])

    def call(kernel, out, *args, scratch=(), flops=0):
        moved = sum(a.size * a.dtype.itemsize for a in args)
        return pl.pallas_call(
            kernel,
            out_shape=out,
            scratch_shapes=scratch,
            compiler_params=params,
            cost_estimate=pl.CostEstimate(flops=flops, bytes_accessed=moved, transcendentals=0),
        )(*args)

    flat = cotangent.reshape(tokens * heads, channels)
    shards = [flat]
    mask = 2
    while mask < ctx_count:
        shards += [ctx_swap(s, mask) for s in shards]
        mask *= 2
    weight_flat = weight.reshape(rows * heads, channels)
    weight_other = ctx_swap(weight_flat, 1)
    chip_weight = call(
        functools.partial(weight_kernel, heads),
        jax.ShapeDtypeStruct((heads, 2 * rows, channels), BF16),
        weight_flat,
        weight_other,
    )
    gain_row = gain.reshape(1, width)

    block = jax.ShapeDtypeStruct((owned, 2 * rows), F32)
    normed = list(call(functools.partial(norm_kernel, columns), [block] * columns, latent[0], gain_row))
    mask = 2
    while mask < ctx_count:
        for j in range(columns):
            if j & (mask >> 1):
                normed[j] = ctx_swap(normed[j], mask)
        mask *= 2
    mine = jnp.concatenate(normed, axis=0)
    theirs = ctx_swap(mine, 1)
    core = lax.axis_index("ctx") & 1
    normed = jnp.where(core == 0, jnp.concatenate([mine, theirs]), jnp.concatenate([theirs, mine]))

    sums = call(
        functools.partial(partial_kernel, head_count, heads, owned),
        jax.ShapeDtypeStruct((head_count * columns * owned, 2 * rows), F32),
        *shards,
        chip_weight,
    )
    mask = 1
    while mask < head_count:
        half = sums.shape[0] // 2
        got = head_swap(jnp.concatenate([sums[half:], normed], axis=0), mask)
        sums = sums[:half] + got[:half]
        normed = jnp.concatenate([normed, got[half:]], axis=0)
        mask *= 2

    blocks = [sums[j * owned : (j + 1) * owned] for j in range(columns)]
    mask = 2
    while mask < ctx_count:
        for j in range(columns):
            if j & (mask >> 1):
                blocks[j] = ctx_swap(blocks[j], mask)
        mask *= 2

    others = [ctx_swap(s, 1) for s in shards]
    weight_grad = call(
        functools.partial(weight_grad_kernel, head_count, heads, owned, columns),
        jax.ShapeDtypeStruct((rows * heads, channels), F32),
        normed,
        *shards,
        *others,
        scratch=[pltpu.VMEM((2, 2 * rows, columns * tokens * heads), F32)],
        flops=2 * rows * heads * channels * ctx_count * tokens * heads,
    )
    latent_gradient = call(
        functools.partial(latent_kernel, columns),
        jax.ShapeDtypeStruct((owned, width), F32),
        latent[0],
        gain_row,
        *blocks,
    )
    return latent_gradient[None], weight_grad.reshape(weight.shape)


def solution(mesh):
    return jax.shard_map(
        functools.partial(per_device, mesh.shape["head"], mesh.shape["ctx"]),
        mesh=mesh,
        in_specs=(
            P("ctx", "head", None),
            P(),
            P("ctx", None, "head", None),
            P("ctx", "head", None),
        ),
        out_specs=(P("ctx", "head", None), P("ctx", "head", None)),
        check_vma=False,
    )
```

```python
import functools

import jax
import jax.numpy as jnp
from jax import lax
from jax.experimental import pallas as pl
from jax.experimental.pallas import tpu as pltpu
from jax.sharding import PartitionSpec as P


F32 = jnp.float32
BF16 = jnp.bfloat16


def iota(shape, axis):
    return lax.broadcasted_iota(jnp.int32, shape, axis)


def one_hot(condition):
    return jnp.where(condition, 1.0, 0.0).astype(BF16)


def matmul(a, b, a_axis=1, b_axis=0):
    return lax.dot_general(a, b, (((a_axis,), (b_axis,)), ((), ())), preferred_element_type=F32)


def reverse_bits(value, count):
    out = 0
    for bit in range(count):
        out = out | (((value >> bit) & 1) << (count - 1 - bit))
    return out


def parity(value, count):
    out = value & 1
    for bit in range(1, count):
        out = out ^ ((value >> bit) & 1)
    return out


def weight_kernel(heads, own_ref, other_ref, out_ref):
    core = lax.axis_index("ctx") & 1
    rows = own_ref.shape[0] // heads
    group = min(rows, max(256 // heads, 1))
    size = group * heads
    to, at = iota((size, size), 0), iota((size, size), 1)
    order = one_hot(at == (to % group) * heads + to // group)
    for ref, place in ((own_ref, core), (other_ref, 1 - core)):
        for start in range(0, rows, group):
            moved = matmul(order, ref[pl.ds(start * heads, size), :]).astype(BF16)
            first = pl.multiple_of(place * rows + start, group)
            for h in range(heads):
                out_ref[h, pl.ds(first, group), :] = moved[h * group : (h + 1) * group, :]


def partial_kernel(head_count, heads, owned, own_ref, other_ref, *refs):
    shard_refs, weight_ref, out_ref = refs[:-2], refs[-2], refs[-1]
    shards = len(shard_refs) + 1
    me = lax.axis_index("head")
    bits = head_count.bit_length() - 1
    rows = head_count * owned
    first = jnp.where(parity(me, bits) == 0, own_ref[...], other_ref[...])
    stacked = jnp.concatenate([first] + [ref[...] for ref in shard_refs], axis=0)
    size = shards * rows * heads
    to, at = iota((size, size), 0), iota((size, size), 1)
    i, j = to % owned, (to // owned) % shards
    position = (to // (owned * shards)) % head_count
    token = (reverse_bits(position, bits) ^ me) * owned + i
    order = one_hot(at == (j * rows + token) * heads + to // (rows * shards))
    moved = matmul(order, stacked).astype(BF16)
    part = rows * shards
    total = matmul(moved[:part], weight_ref[0], 1, 1)
    for h in range(1, heads):
        total += matmul(moved[h * part : (h + 1) * part], weight_ref[h], 1, 1)
    out_ref[...] = total


def norm_kernel(columns, own_ref, other_ref, gain_ref, *out_refs):
    core, column = lax.axis_index("ctx") & 1, lax.axis_index("ctx") >> 1
    own, other = own_ref[...].astype(F32), other_ref[...].astype(F32)
    raw = jnp.concatenate([jnp.where(core == 0, own, other), jnp.where(core == 0, other, own)], axis=0)
    rms = lax.rsqrt(jnp.mean(raw * raw, axis=1, keepdims=True) + 1e-06)
    normed = ((raw * rms) * gain_ref[...]).astype(BF16).astype(F32)
    width = normed.shape[1] // columns
    for j, ref in enumerate(out_refs):
        block = normed[:, :width]
        for b in range(1, columns):
            block = jnp.where((column ^ j) == b, normed[:, b * width : (b + 1) * width], block)
        ref[...] = block


def weight_grad_kernel(head_count, heads, owned, columns, normed_ref, *refs):
    shard_refs, out_ref, scratch_ref = refs[:-2], refs[-2], refs[-1]
    me = lax.axis_index("head")
    core = lax.axis_index("ctx") & 1
    role = core ^ parity(me, head_count.bit_length() - 1)
    rows = out_ref.shape[0] // heads
    tokens = head_count * owned
    normed = normed_ref[...].astype(BF16)
    size = columns * tokens * heads
    at, to = iota((normed.shape[0], size), 0), iota((normed.shape[0], size), 1)
    token, j = (to // heads) % tokens, to // (heads * tokens)
    cots = []
    for side in range(2):
        place = (((token // owned) ^ me) * columns + j) * 2 + (jnp.where(j == 0, core, role) ^ side)
        spread = one_hot(at == place * owned + token % owned)
        scratch_ref[side] = matmul(normed, spread, 0, 0)
        cots.append(jnp.concatenate([r[...] for r in shard_refs[side * columns : (side + 1) * columns]], axis=0))
    group = min(rows, max(256 // heads, 1))
    keep = (iota((1, heads, size), 2) % heads) == iota((1, heads, size), 1)
    for start in range(0, rows, group):
        total = None
        for side in range(2):
            block = scratch_ref[side, start : start + group, :]
            left = jnp.where(keep, block[:, None, :], 0.0).reshape(group * heads, size).astype(BF16)
            part = matmul(left, cots[side])
            total = part if total is None else total + part
        out_ref[start * heads : (start + group) * heads, :] = total


def latent_kernel(head_count, columns, latent_ref, gain_ref, *refs):
    block_refs, other_refs, out_ref = refs[:columns], refs[columns:-1], refs[-1]
    column = lax.axis_index("ctx") >> 1
    odd = parity(lax.axis_index("head"), head_count.bit_length() - 1)
    raw = latent_ref[...].astype(F32)
    rms = lax.rsqrt(jnp.mean(raw * raw, axis=1, keepdims=True) + 1e-06)
    hat = raw * rms
    relative = [ref[...] for ref in block_refs]
    for j, ref in enumerate(other_refs):
        relative[2 * j] = jnp.where(odd == 0, relative[2 * j], ref[...])
    blocks = []
    for b in range(columns):
        block = relative[0]
        for j in range(1, columns):
            block = jnp.where((column ^ j) == b, relative[j], block)
        blocks.append(block)
    scaled = jnp.concatenate(blocks, axis=1) * gain_ref[...]
    inner = jnp.mean(scaled * hat, axis=1, keepdims=True)
    out_ref[...] = rms * (scaled - hat * inner)


def per_device(head_count, ctx_count, latent, gain, cotangent, weight):
    columns = ctx_count // 2
    owned, width = latent.shape[1:]
    _, tokens, heads, channels = cotangent.shape
    rows = weight.shape[0]
    bits = head_count.bit_length() - 1
    params = pltpu.CompilerParams(vmem_limit_bytes=48 * 1024 * 1024)

    def swap(value, partner):
        pairs = [
            (h * ctx_count + c, p * ctx_count + q)
            for h in range(head_count)
            for c in range(ctx_count)
            for p, q in [partner(h, c)]
        ]
        return lax.ppermute(value, ("head", "ctx"), pairs)

    def ctx_swap(value, mask):
        return swap(value, lambda h, c: (h, c ^ mask))

    def role_swap(value, mask):
        return swap(value, lambda h, c: (h, c ^ mask ^ parity(h, bits)))

    def head_swap(value, mask):
        return swap(value, lambda h, c: (h ^ mask, c ^ 1))

    def call(kernel, out, *args, scratch=(), flops=0):
        moved = sum(a.size * a.dtype.itemsize for a in args)
        return pl.pallas_call(
            kernel,
            out_shape=out,
            scratch_shapes=scratch,
            compiler_params=params,
            cost_estimate=pl.CostEstimate(flops=flops, bytes_accessed=moved, transcendentals=0),
        )(*args)

    own = cotangent.reshape(tokens * heads, channels)
    far = [role_swap(own, 2)]
    other = ctx_swap(own, 1)
    if columns > 2:
        first = jnp.where(parity(lax.axis_index("head"), bits) == 0, own, other)
        shards = [first] + far
        mask = 4
        while mask < ctx_count:
            shards += [ctx_swap(s, mask) for s in shards]
            mask *= 2
        far = shards[1:]
    weight_flat = weight.reshape(rows * heads, channels)
    weight_other = ctx_swap(weight_flat, 1)
    chip_weight = call(
        functools.partial(weight_kernel, heads),
        jax.ShapeDtypeStruct((heads, 2 * rows, channels), BF16),
        weight_flat,
        weight_other,
    )
    gain_row = gain.reshape(1, width)

    latent_other = ctx_swap(latent[0], 1)
    latent_own, latent_other, chip_weight = lax.optimization_barrier((latent[0], latent_other, chip_weight))
    block = jax.ShapeDtypeStruct((2 * owned, 2 * rows), F32)
    normed = list(call(functools.partial(norm_kernel, columns), [block] * columns, latent_own, latent_other, gain_row))
    mask = 2
    while mask < ctx_count:
        for j in range(columns):
            if j & (mask >> 1):
                normed[j] = ctx_swap(normed[j], mask | 1)
        mask *= 2
    normed = jnp.concatenate(normed, axis=0)

    sums = call(
        functools.partial(partial_kernel, head_count, heads, owned),
        jax.ShapeDtypeStruct((head_count * columns * owned, 2 * rows), F32),
        own,
        other,
        *far,
        chip_weight,
    )
    core = lax.axis_index("ctx") & 1
    mask = 1
    while mask < head_count:
        half = sums.shape[0] // 2
        if 2 * mask < head_count:
            got = head_swap(jnp.concatenate([sums[half:], normed], axis=0), mask)
            normed = jnp.concatenate([normed, got[half:]], axis=0)
        else:
            keep = jnp.where(core == 0, normed[:, :rows], normed[:, rows:])
            send = jnp.where(core == 0, normed[:, rows:], normed[:, :rows])
            count = send.shape[0] // 2
            send = jnp.concatenate([send[:count], send[count:]], axis=1)
            got = head_swap(jnp.concatenate([sums[half:], send], axis=0), mask)
            normed = jnp.concatenate([keep, got[half:, :rows], got[half:, rows:]], axis=0)
        sums = sums[:half] + got[:half]
        mask *= 2

    blocks = [sums[j * owned : (j + 1) * owned] for j in range(columns)]
    mask = ctx_count // 2
    while mask > 2:
        for j in range(columns):
            if j & (mask >> 1):
                blocks[j] = ctx_swap(blocks[j], mask)
        mask //= 2
    kept = [ctx_swap(blocks[j], 1) for j in range(0, columns, 2)]
    for j in range(1, columns, 2):
        blocks[j] = role_swap(blocks[j], 2)

    weight_grad = call(
        functools.partial(weight_grad_kernel, head_count, heads, owned, columns),
        jax.ShapeDtypeStruct((rows * heads, channels), F32),
        normed,
        own,
        *far,
        other,
        *[ctx_swap(s, 1) for s in far],
        scratch=[pltpu.VMEM((2, rows, columns * tokens * heads), F32)],
        flops=2 * rows * heads * channels * ctx_count * tokens * heads,
    )
    latent_gradient = call(
        functools.partial(latent_kernel, head_count, columns),
        jax.ShapeDtypeStruct((owned, width), F32),
        latent[0],
        gain_row,
        *blocks,
        *kept,
    )
    return latent_gradient[None], weight_grad.reshape(weight.shape)


def solution(mesh):
    return jax.shard_map(
        functools.partial(per_device, mesh.shape["head"], mesh.shape["ctx"]),
        mesh=mesh,
        in_specs=(
            P("ctx", "head", None),
            P(),
            P("ctx", None, "head", None),
            P("ctx", "head", None),
        ),
        out_specs=(P("ctx", "head", None), P("ctx", "head", None)),
        check_vma=False,
    )
```

```python
import functools

import jax
import jax.numpy as jnp
from jax import lax
from jax.experimental import pallas as pl
from jax.experimental.pallas import tpu as pltpu
from jax.sharding import PartitionSpec as P


F32 = jnp.float32
BF16 = jnp.bfloat16


def iota(shape, axis):
    return lax.broadcasted_iota(jnp.int32, shape, axis)


def one_hot(condition):
    return jnp.where(condition, 1.0, 0.0).astype(BF16)


def matmul(a, b, a_axis=1, b_axis=0):
    return lax.dot_general(a, b, (((a_axis,), (b_axis,)), ((), ())), preferred_element_type=F32)


def reverse_bits(value, count):
    out = 0
    for bit in range(count):
        out = out | (((value >> bit) & 1) << (count - 1 - bit))
    return out


def parity(value, count):
    out = value & 1
    for bit in range(1, count):
        out = out ^ ((value >> bit) & 1)
    return out


def weight_kernel(heads, own_ref, other_ref, out_ref):
    core = lax.axis_index("ctx") & 1
    rows = own_ref.shape[0] // heads
    group = min(rows, max(256 // heads, 1))
    size = group * heads
    to, at = iota((size, size), 0), iota((size, size), 1)
    order = one_hot(at == (to % group) * heads + to // group)
    for ref, place in ((own_ref, core), (other_ref, 1 - core)):
        for start in range(0, rows, group):
            moved = matmul(order, ref[pl.ds(start * heads, size), :]).astype(BF16)
            first = pl.multiple_of(place * rows + start, group)
            for h in range(heads):
                out_ref[h, pl.ds(first, group), :] = moved[h * group : (h + 1) * group, :]


def partial_kernel(head_count, heads, owned, own_ref, other_ref, *refs):
    shard_refs, weight_ref, out_ref = refs[:-2], refs[-2], refs[-1]
    shards = len(shard_refs) + 1
    me = lax.axis_index("head")
    bits = head_count.bit_length() - 1
    rows = head_count * owned
    first = jnp.where(parity(me, bits) == 0, own_ref[...], other_ref[...])
    stacked = jnp.concatenate([first] + [ref[...] for ref in shard_refs], axis=0)
    size = shards * rows * heads
    to, at = iota((size, size), 0), iota((size, size), 1)
    i, j = to % owned, (to // owned) % shards
    position = (to // (owned * shards)) % head_count
    token = (reverse_bits(position, bits) ^ me) * owned + i
    order = one_hot(at == (j * rows + token) * heads + to // (rows * shards))
    moved = matmul(order, stacked).astype(BF16)
    part = rows * shards
    total = matmul(moved[:part], weight_ref[0], 1, 1)
    for h in range(1, heads):
        total += matmul(moved[h * part : (h + 1) * part], weight_ref[h], 1, 1)
    out_ref[...] = total


def norm_kernel(columns, own_ref, other_ref, gain_ref, *out_refs):
    core, column = lax.axis_index("ctx") & 1, lax.axis_index("ctx") >> 1
    own, other = own_ref[...].astype(F32), other_ref[...].astype(F32)
    raw = jnp.concatenate([jnp.where(core == 0, own, other), jnp.where(core == 0, other, own)], axis=0)
    rms = lax.rsqrt(jnp.mean(raw * raw, axis=1, keepdims=True) + 1e-06)
    normed = ((raw * rms) * gain_ref[...]).astype(BF16).astype(F32)
    width = normed.shape[1] // columns
    for j, ref in enumerate(out_refs):
        block = normed[:, :width]
        for b in range(1, columns):
            block = jnp.where((column ^ j) == b, normed[:, b * width : (b + 1) * width], block)
        ref[...] = block


def weight_grad_kernel(head_count, heads, owned, columns, normed_ref, *refs):
    shard_refs, out_ref, scratch_ref = refs[:-2], refs[-2], refs[-1]
    me = lax.axis_index("head")
    core = lax.axis_index("ctx") & 1
    role = core ^ parity(me, head_count.bit_length() - 1)
    rows = out_ref.shape[0] // heads
    tokens = head_count * owned
    normed = normed_ref[...].astype(BF16)
    size = columns * tokens * heads
    at, to = iota((normed.shape[0], size), 0), iota((normed.shape[0], size), 1)
    token, j = (to // heads) % tokens, to // (heads * tokens)
    cots = []
    for side in range(2):
        place = (((token // owned) ^ me) * columns + j) * 2 + (jnp.where(j == 0, core, role) ^ side)
        spread = one_hot(at == place * owned + token % owned)
        scratch_ref[side] = matmul(normed, spread, 0, 0)
        cots.append(jnp.concatenate([r[...] for r in shard_refs[side * columns : (side + 1) * columns]], axis=0))
    group = min(rows, max(256 // heads, 1))
    keep = (iota((1, heads, size), 2) % heads) == iota((1, heads, size), 1)
    for start in range(0, rows, group):
        total = None
        for side in range(2):
            block = scratch_ref[side, start : start + group, :]
            left = jnp.where(keep, block[:, None, :], 0.0).reshape(group * heads, size).astype(BF16)
            part = matmul(left, cots[side])
            total = part if total is None else total + part
        out_ref[start * heads : (start + group) * heads, :] = total


def latent_kernel(head_count, columns, latent_ref, gain_ref, *refs):
    block_refs, other_refs, out_ref = refs[:columns], refs[columns:-1], refs[-1]
    column = lax.axis_index("ctx") >> 1
    odd = parity(lax.axis_index("head"), head_count.bit_length() - 1)
    raw = latent_ref[...].astype(F32)
    rms = lax.rsqrt(jnp.mean(raw * raw, axis=1, keepdims=True) + 1e-06)
    hat = raw * rms
    relative = [ref[...] for ref in block_refs]
    for j, ref in enumerate(other_refs):
        relative[2 * j] = jnp.where(odd == 0, relative[2 * j], ref[...])
    blocks = []
    for b in range(columns):
        block = relative[0]
        for j in range(1, columns):
            block = jnp.where((column ^ j) == b, relative[j], block)
        blocks.append(block)
    scaled = jnp.concatenate(blocks, axis=1) * gain_ref[...]
    inner = jnp.mean(scaled * hat, axis=1, keepdims=True)
    out_ref[...] = rms * (scaled - hat * inner)


def per_device(head_count, ctx_count, latent, gain, cotangent, weight):
    columns = ctx_count // 2
    owned, width = latent.shape[1:]
    _, tokens, heads, channels = cotangent.shape
    rows = weight.shape[0]
    bits = head_count.bit_length() - 1
    params = pltpu.CompilerParams(vmem_limit_bytes=48 * 1024 * 1024)

    def swap(value, partner):
        pairs = [
            (h * ctx_count + c, p * ctx_count + q)
            for h in range(head_count)
            for c in range(ctx_count)
            for p, q in [partner(h, c)]
        ]
        return lax.ppermute(value, ("head", "ctx"), pairs)

    def ctx_swap(value, mask):
        return swap(value, lambda h, c: (h, c ^ mask))

    def role_swap(value, mask):
        return swap(value, lambda h, c: (h, c ^ mask ^ parity(h, bits)))

    def head_swap(value, mask):
        return swap(value, lambda h, c: (h ^ mask, c ^ 1))

    def call(kernel, out, *args, scratch=(), flops=0):
        moved = sum(a.size * a.dtype.itemsize for a in args)
        return pl.pallas_call(
            kernel,
            out_shape=out,
            scratch_shapes=scratch,
            compiler_params=params,
            cost_estimate=pl.CostEstimate(flops=flops, bytes_accessed=moved, transcendentals=0),
        )(*args)

    own = cotangent.reshape(tokens * heads, channels)
    far = [role_swap(own, 2)]
    other = ctx_swap(own, 1)
    if columns > 2:
        first = jnp.where(parity(lax.axis_index("head"), bits) == 0, own, other)
        shards = [first] + far
        mask = 4
        while mask < ctx_count:
            shards += [ctx_swap(s, mask) for s in shards]
            mask *= 2
        far = shards[1:]
    latent_other = ctx_swap(latent[0], 1)
    gain_row = gain.reshape(1, width)
    block = jax.ShapeDtypeStruct((2 * owned, 2 * rows), F32)
    normed = list(call(functools.partial(norm_kernel, columns), [block] * columns, latent[0], latent_other, gain_row))

    weight_flat = weight.reshape(rows * heads, channels)
    weight_other = ctx_swap(weight_flat, 1)
    weight_flat, weight_other, *normed = lax.optimization_barrier((weight_flat, weight_other, *normed))
    chip_weight = call(
        functools.partial(weight_kernel, heads),
        jax.ShapeDtypeStruct((heads, 2 * rows, channels), BF16),
        weight_flat,
        weight_other,
    )

    mask = 2
    while mask < ctx_count:
        for j in range(columns):
            if j & (mask >> 1):
                normed[j] = ctx_swap(normed[j], mask | 1)
        mask *= 2
    normed = jnp.concatenate(normed, axis=0)

    sums = call(
        functools.partial(partial_kernel, head_count, heads, owned),
        jax.ShapeDtypeStruct((head_count * columns * owned, 2 * rows), F32),
        own,
        other,
        *far,
        chip_weight,
    )
    core = lax.axis_index("ctx") & 1
    mask = 1
    while mask < head_count:
        half = sums.shape[0] // 2
        if 2 * mask < head_count:
            got = head_swap(jnp.concatenate([sums[half:], normed], axis=0), mask)
            normed = jnp.concatenate([normed, got[half:]], axis=0)
        else:
            keep = jnp.where(core == 0, normed[:, :rows], normed[:, rows:])
            send = jnp.where(core == 0, normed[:, rows:], normed[:, :rows])
            count = send.shape[0] // 2
            send = jnp.concatenate([send[:count], send[count:]], axis=1)
            got = head_swap(jnp.concatenate([sums[half:], send], axis=0), mask)
            normed = jnp.concatenate([keep, got[half:, :rows], got[half:, rows:]], axis=0)
        sums = sums[:half] + got[:half]
        mask *= 2

    blocks = [sums[j * owned : (j + 1) * owned] for j in range(columns)]
    mask = ctx_count // 2
    while mask > 2:
        for j in range(columns):
            if j & (mask >> 1):
                blocks[j] = ctx_swap(blocks[j], mask)
        mask //= 2
    kept = [ctx_swap(blocks[j], 1) for j in range(0, columns, 2)]
    for j in range(1, columns, 2):
        blocks[j] = role_swap(blocks[j], 2)

    weight_grad = call(
        functools.partial(weight_grad_kernel, head_count, heads, owned, columns),
        jax.ShapeDtypeStruct((rows * heads, channels), F32),
        normed,
        own,
        *far,
        other,
        *[ctx_swap(s, 1) for s in far],
        scratch=[pltpu.VMEM((2, rows, columns * tokens * heads), F32)],
        flops=2 * rows * heads * channels * ctx_count * tokens * heads,
    )
    latent_gradient = call(
        functools.partial(latent_kernel, head_count, columns),
        jax.ShapeDtypeStruct((owned, width), F32),
        latent[0],
        gain_row,
        *blocks,
        *kept,
    )
    return latent_gradient[None], weight_grad.reshape(weight.shape)


def solution(mesh):
    return jax.shard_map(
        functools.partial(per_device, mesh.shape["head"], mesh.shape["ctx"]),
        mesh=mesh,
        in_specs=(
            P("ctx", "head", None),
            P(),
            P("ctx", None, "head", None),
            P("ctx", "head", None),
        ),
        out_specs=(P("ctx", "head", None), P("ctx", "head", None)),
        check_vma=False,
    )
```

```python
import functools

import jax
import jax.numpy as jnp
from jax import lax
from jax.experimental import pallas as pl
from jax.experimental.pallas import tpu as pltpu
from jax.sharding import PartitionSpec as P


F32 = jnp.float32
BF16 = jnp.bfloat16

def iota(shape, axis):
    return lax.broadcasted_iota(jnp.int32, shape, axis)

def one_hot(condition):
    return jnp.where(condition, 1.0, 0.0).astype(BF16)

def matmul(a, b, a_axis=1, b_axis=0):
    return lax.dot_general(a, b, (((a_axis,), (b_axis,)), ((), ())), preferred_element_type=F32)

def reverse_bits(value, count):
    out = 0
    for bit in range(count):
        out = out | (((value >> bit) & 1) << (count - 1 - bit))
    return out

def odd_head(value, count):
    out = value & 1
    for bit in range(1, count):
        out = out ^ ((value >> bit) & 1)
    return out

def row_order(rows, heads):
    group = min(rows, max(256 // heads, 1))
    size = group * heads
    to, at = iota((size, size), 0), iota((size, size), 1)
    return group, one_hot(at == (to % group) * heads + to // group)

def own_kernel(head_count, heads, owned, shards, weight_hbm, own_hbm, out_ref, own_ref, order_ref, weight_ref, sems):
    me = lax.axis_index("head")
    bits = head_count.bit_length() - 1
    rows = out_ref.shape[1]
    pieces = sems.shape[0] - 1
    span = rows * heads // pieces
    copies = [
        pltpu.make_async_copy(weight_hbm.at[pl.ds(n * span, span)], weight_ref.at[pl.ds(n * span, span)], sems.at[n])
        for n in range(pieces)
    ]
    copies.append(pltpu.make_async_copy(own_hbm, own_ref, sems.at[pieces]))
    for copy in copies:
        copy.start()
    tokens = head_count * owned
    size = shards * tokens * heads
    to, at = iota((size, size), 0), iota((size, size), 1)
    i, j = to % owned, (to // owned) % shards
    position = (to // (owned * shards)) % head_count
    token = (reverse_bits(position, bits) ^ me) * owned + i
    order_ref[...] = one_hot(at == (j * tokens + token) * heads + to // (tokens * shards))
    group, order = row_order(rows, heads)
    for n in range(pieces):
        copies[n].wait()
        for start in range(n * span // heads, (n + 1) * span // heads, group):
            moved = matmul(order, weight_ref[pl.ds(start * heads, group * heads), :]).astype(BF16)
            for h in range(heads):
                out_ref[h, pl.ds(start, group), :] = moved[h * group : (h + 1) * group, :]
    copies[pieces].wait()

def other_kernel(heads, weight_ref, out_ref):
    rows = out_ref.shape[1]
    group, order = row_order(rows, heads)
    for start in range(0, rows, group):
        moved = matmul(order, weight_ref[pl.ds(start * heads, group * heads), :]).astype(BF16)
        for h in range(heads):
            out_ref[h, pl.ds(start, group), :] = moved[h * group : (h + 1) * group, :]

def partial_kernel(head_count, order_ref, own_weight_ref, other_weight_ref, own_ref, other_ref, *refs):
    shard_refs, out_ref = refs[:-1], refs[-1]
    odd = odd_head(lax.axis_index("head"), head_count.bit_length() - 1) == 1
    first = jnp.where(odd, other_ref[...], own_ref[...])
    stacked = jnp.concatenate([first] + [ref[...] for ref in shard_refs], axis=0)
    moved = matmul(order_ref[...], stacked).astype(BF16)
    heads, part = own_weight_ref.shape[0], out_ref.shape[0]
    own = matmul(moved[:part], own_weight_ref[0], 1, 1)
    other = matmul(moved[:part], other_weight_ref[0], 1, 1)
    for h in range(1, heads):
        own += matmul(moved[h * part : (h + 1) * part], own_weight_ref[h], 1, 1)
        other += matmul(moved[h * part : (h + 1) * part], other_weight_ref[h], 1, 1)
    core = lax.axis_index("ctx") & 1
    out_ref[...] = jnp.concatenate([jnp.where(core == 0, own, other), jnp.where(core == 0, other, own)], axis=1)

def norm_kernel(columns, own_ref, other_ref, gain_ref, *out_refs):
    core, column = lax.axis_index("ctx") & 1, lax.axis_index("ctx") >> 1
    own, other = own_ref[...].astype(F32), other_ref[...].astype(F32)
    raw = jnp.concatenate([jnp.where(core == 0, own, other), jnp.where(core == 0, other, own)], axis=0)
    rms = lax.rsqrt(jnp.mean(raw * raw, axis=1, keepdims=True) + 1e-06)
    normed = ((raw * rms) * gain_ref[...]).astype(BF16).astype(F32)
    width = normed.shape[1] // columns
    for j, ref in enumerate(out_refs):
        block = normed[:, :width]
        for b in range(1, columns):
            block = jnp.where((column ^ j) == b, normed[:, b * width : (b + 1) * width], block)
        ref[...] = block

def weight_grad_kernel(head_count, heads, owned, columns, normed_ref, *refs):
    shard_refs, out_ref, scratch_ref = refs[:-2], refs[-2], refs[-1]
    me = lax.axis_index("head")
    core = lax.axis_index("ctx") & 1
    role = core ^ odd_head(me, head_count.bit_length() - 1)
    rows = out_ref.shape[0] // heads
    tokens = head_count * owned
    normed = normed_ref[...].astype(BF16)
    size = columns * tokens * heads
    at, to = iota((normed.shape[0], size), 0), iota((normed.shape[0], size), 1)
    token, j = (to // heads) % tokens, to // (heads * tokens)
    cots = []
    for side in range(2):
        place = (((token // owned) ^ me) * columns + j) * 2 + (jnp.where(j == 0, core, role) ^ side)
        spread = one_hot(at == place * owned + token % owned)
        scratch_ref[side] = matmul(normed, spread, 0, 0)
        cots.append(jnp.concatenate([r[...] for r in shard_refs[side * columns : (side + 1) * columns]], axis=0))
    group = min(rows, max(256 // heads, 1))
    keep = (iota((1, heads, size), 2) % heads) == iota((1, heads, size), 1)
    for start in range(0, rows, group):
        total = None
        for side in range(2):
            block = scratch_ref[side, start : start + group, :]
            left = jnp.where(keep, block[:, None, :], 0.0).reshape(group * heads, size).astype(BF16)
            part = matmul(left, cots[side])
            total = part if total is None else total + part
        out_ref[start * heads : (start + group) * heads, :] = total

def latent_kernel(head_count, columns, latent_ref, gain_ref, *refs):
    block_refs, other_refs, out_ref = refs[:columns], refs[columns:-1], refs[-1]
    column = lax.axis_index("ctx") >> 1
    odd = odd_head(lax.axis_index("head"), head_count.bit_length() - 1)
    raw = latent_ref[...].astype(F32)
    rms = lax.rsqrt(jnp.mean(raw * raw, axis=1, keepdims=True) + 1e-06)
    hat = raw * rms
    relative = [ref[...] for ref in block_refs]
    for j, ref in enumerate(other_refs):
        relative[2 * j] = jnp.where(odd == 0, relative[2 * j], ref[...])
    blocks = []
    for b in range(columns):
        block = relative[0]
        for j in range(1, columns):
            block = jnp.where((column ^ j) == b, relative[j], block)
        blocks.append(block)
    scaled = jnp.concatenate(blocks, axis=1) * gain_ref[...]
    inner = jnp.mean(scaled * hat, axis=1, keepdims=True)
    out_ref[...] = rms * (scaled - hat * inner)

def per_device(head_count, ctx_count, latent, gain, cotangent, weight):
    columns = ctx_count // 2
    owned, width = latent.shape[1:]
    _, tokens, heads, channels = cotangent.shape
    rows = weight.shape[0]
    bits = head_count.bit_length() - 1
    params = pltpu.CompilerParams(vmem_limit_bytes=48 * 1024 * 1024)

    def swap(value, partner):
        pairs = [
            (h * ctx_count + c, p * ctx_count + q)
            for h in range(head_count)
            for c in range(ctx_count)
            for p, q in [partner(h, c)]
        ]
        return lax.ppermute(value, ("head", "ctx"), pairs)

    def ctx_swap(value, mask):
        return swap(value, lambda h, c: (h, c ^ mask))

    def role_swap(value, mask):
        return swap(value, lambda h, c: (h, c ^ mask ^ odd_head(h, bits)))

    def head_swap(value, mask):
        return swap(value, lambda h, c: (h ^ mask, c ^ 1))

    def call(kernel, out, *args, scratch=(), flops=0, raw=0):
        moved = sum(a.size * a.dtype.itemsize for a in args)
        return pl.pallas_call(
            kernel,
            out_shape=out,
            in_specs=[pl.BlockSpec(memory_space=pltpu.HBM if n < raw else pltpu.VMEM) for n in range(len(args))],
            scratch_shapes=scratch,
            compiler_params=params,
            cost_estimate=pl.CostEstimate(flops=flops, bytes_accessed=moved, transcendentals=0),
        )(*[pltpu.with_memory_space_constraint(a, pltpu.HBM) if n < raw else a for n, a in enumerate(args)])

    own = cotangent.reshape(tokens * heads, channels)
    far = [role_swap(own, 2)]
    other = ctx_swap(own, 1)
    weight_flat = weight.reshape(rows * heads, channels)
    latent_other = ctx_swap(latent[0], 1)
    weight_other = ctx_swap(weight_flat, 1)
    gain_row = gain.reshape(1, width)

    ordered = jax.ShapeDtypeStruct((heads, rows, channels), BF16)
    size = columns * tokens * heads
    pieces = 4 if rows % 4 == 0 and rows // 4 * heads >= 256 else 1
    own_weight, own_copy, order = call(
        functools.partial(own_kernel, head_count, heads, owned, columns),
        [ordered, jax.ShapeDtypeStruct(own.shape, BF16), jax.ShapeDtypeStruct((size, size), BF16)],
        weight_flat,
        own,
        scratch=[
            pltpu.VMEM(weight_flat.shape, BF16),
            pltpu.SemaphoreType.DMA((pieces + 1,)),
        ],
        raw=2,
    )
    if columns > 2:
        mine = jnp.where(odd_head(lax.axis_index("head"), bits) == 1, other, own_copy)
        mask = 4
        while mask < ctx_count:
            far += [ctx_swap(s, mask) for s in [mine] + far]
            mask *= 2

    block = jax.ShapeDtypeStruct((2 * owned, 2 * rows), F32)

    normed = list(call(functools.partial(norm_kernel, columns), [block] * columns, latent[0], latent_other, gain_row))
    weight_other, *normed = lax.optimization_barrier((weight_other, *normed))
    other_weight = call(functools.partial(other_kernel, heads), ordered, weight_other)
    mask = 2
    while mask < ctx_count:
        for j in range(columns):
            if j & (mask >> 1):
                normed[j] = ctx_swap(normed[j], mask | 1)
        mask *= 2
    normed = jnp.concatenate(normed, axis=0)

    sums = call(
        functools.partial(partial_kernel, head_count),
        jax.ShapeDtypeStruct((head_count * columns * owned, 2 * rows), F32),
        order,
        own_weight,
        other_weight,
        own_copy,
        other,
        *far,
    )
    core = lax.axis_index("ctx") & 1
    mask = 1
    while mask < head_count:
        half = sums.shape[0] // 2
        if 2 * mask < head_count:
            got = head_swap(jnp.concatenate([sums[half:], normed], axis=0), mask)
            normed = jnp.concatenate([normed, got[half:]], axis=0)
        else:
            keep = jnp.where(core == 0, normed[:, :rows], normed[:, rows:])
            send = jnp.where(core == 0, normed[:, rows:], normed[:, :rows])
            count = send.shape[0] // 2
            send = jnp.concatenate([send[:count], send[count:]], axis=1)
            got = head_swap(jnp.concatenate([sums[half:], send], axis=0), mask)
            normed = jnp.concatenate([keep, got[half:, :rows], got[half:, rows:]], axis=0)
        sums = sums[:half] + got[:half]
        mask *= 2

    blocks = [sums[j * owned : (j + 1) * owned] for j in range(columns)]
    mask = ctx_count // 2
    while mask > 2:
        for j in range(columns):
            if j & (mask >> 1):
                blocks[j] = ctx_swap(blocks[j], mask)
        mask //= 2
    kept = [ctx_swap(blocks[j], 1) for j in range(0, columns, 2)]
    for j in range(1, columns, 2):
        blocks[j] = role_swap(blocks[j], 2)

    weight_grad = call(
        functools.partial(weight_grad_kernel, head_count, heads, owned, columns),
        jax.ShapeDtypeStruct((rows * heads, channels), F32),
        normed,
        own_copy,
        *far,
        other,
        *[ctx_swap(s, 1) for s in far],
        scratch=[pltpu.VMEM((2, rows, columns * tokens * heads), F32)],
        flops=2 * rows * heads * channels * ctx_count * tokens * heads,
    )
    latent_gradient = call(
        functools.partial(latent_kernel, head_count, columns),
        jax.ShapeDtypeStruct((owned, width), F32),
        latent[0],
        gain_row,
        *blocks,
        *kept,
    )
    return latent_gradient[None], weight_grad.reshape(weight.shape)

def solution(mesh):
    return jax.shard_map(
        functools.partial(per_device, mesh.shape["head"], mesh.shape["ctx"]),
        mesh=mesh,
        in_specs=(
            P("ctx", "head", None),
            P(),
            P("ctx", None, "head", None),
            P("ctx", "head", None),
        ),
        out_specs=(P("ctx", "head", None), P("ctx", "head", None)),
        check_vma=False,
    )
```

```python
import functools

import jax
import jax.numpy as jnp
from jax import lax
from jax.experimental import pallas as pl
from jax.experimental.pallas import tpu as pltpu
from jax.sharding import PartitionSpec as P


F32 = jnp.float32
BF16 = jnp.bfloat16


def iota(shape, axis):
    return lax.broadcasted_iota(jnp.int32, shape, axis)


def one_hot(condition):
    return jnp.where(condition, 1.0, 0.0).astype(BF16)


def matmul(a, b, a_axis=1, b_axis=0):
    return lax.dot_general(a, b, (((a_axis,), (b_axis,)), ((), ())), preferred_element_type=F32)


def reverse_bits(value, count):
    out = 0
    for bit in range(count):
        out = out | (((value >> bit) & 1) << (count - 1 - bit))
    return out


def parity(value, count):
    out = value & 1
    for bit in range(1, count):
        out = out ^ ((value >> bit) & 1)
    return out


def weight_kernel(heads, own_ref, other_ref, out_ref):
    core = lax.axis_index("ctx") & 1
    rows = own_ref.shape[0] // heads
    group = min(rows, max(256 // heads, 1))
    size = group * heads
    to, at = iota((size, size), 0), iota((size, size), 1)
    order = one_hot(at == (to % group) * heads + to // group)
    for ref, place in ((own_ref, core), (other_ref, 1 - core)):
        for start in range(0, rows, group):
            moved = matmul(order, ref[pl.ds(start * heads, size), :]).astype(BF16)
            first = pl.multiple_of(place * rows + start, group)
            for h in range(heads):
                out_ref[h, pl.ds(first, group), :] = moved[h * group : (h + 1) * group, :]


def partial_kernel(head_count, heads, owned, own_ref, other_ref, *refs):
    shard_refs, weight_ref, out_ref = refs[:-2], refs[-2], refs[-1]
    shards = len(shard_refs) + 1
    me = lax.axis_index("head")
    bits = head_count.bit_length() - 1
    rows = head_count * owned
    first = jnp.where(parity(me, bits) == 0, own_ref[...], other_ref[...])
    stacked = jnp.concatenate([first] + [ref[...] for ref in shard_refs], axis=0)
    size = shards * rows * heads
    to, at = iota((size, size), 0), iota((size, size), 1)
    i, j = to % owned, (to // owned) % shards
    position = (to // (owned * shards)) % head_count
    token = (reverse_bits(position, bits) ^ me) * owned + i
    order = one_hot(at == (j * rows + token) * heads + to // (rows * shards))
    moved = matmul(order, stacked).astype(BF16)
    part = rows * shards
    total = matmul(moved[:part], weight_ref[0], 1, 1)
    for h in range(1, heads):
        total += matmul(moved[h * part : (h + 1) * part], weight_ref[h], 1, 1)
    out_ref[...] = total


def norm_kernel(columns, own_ref, other_ref, gain_ref, *out_refs):
    core, column = lax.axis_index("ctx") & 1, lax.axis_index("ctx") >> 1
    own, other = own_ref[...].astype(F32), other_ref[...].astype(F32)
    raw = jnp.concatenate([jnp.where(core == 0, own, other), jnp.where(core == 0, other, own)], axis=0)
    rms = lax.rsqrt(jnp.mean(raw * raw, axis=1, keepdims=True) + 1e-06)
    normed = ((raw * rms) * gain_ref[...]).astype(BF16).astype(F32)
    width = normed.shape[1] // columns
    for j, ref in enumerate(out_refs):
        block = normed[:, :width]
        for b in range(1, columns):
            block = jnp.where((column ^ j) == b, normed[:, b * width : (b + 1) * width], block)
        ref[...] = block


def weight_grad_kernel(head_count, heads, owned, columns, normed_ref, *refs):
    shard_refs, out_ref, scratch_ref = refs[:-2], refs[-2], refs[-1]
    me = lax.axis_index("head")
    core = lax.axis_index("ctx") & 1
    role = core ^ parity(me, head_count.bit_length() - 1)
    rows = out_ref.shape[0] // heads
    tokens = head_count * owned
    normed = normed_ref[...].astype(BF16)
    size = columns * tokens * heads
    at, to = iota((normed.shape[0], size), 0), iota((normed.shape[0], size), 1)
    token, j = (to // heads) % tokens, to // (heads * tokens)
    cots = []
    for side in range(2):
        place = (((token // owned) ^ me) * columns + j) * 2 + (jnp.where(j == 0, core, role) ^ side)
        spread = one_hot(at == place * owned + token % owned)
        scratch_ref[side] = matmul(normed, spread, 0, 0)
        cots.append(jnp.concatenate([r[...] for r in shard_refs[side * columns : (side + 1) * columns]], axis=0))
    group = min(rows, max(256 // heads, 1))
    keep = (iota((1, heads, size), 2) % heads) == iota((1, heads, size), 1)
    for start in range(0, rows, group):
        total = None
        for side in range(2):
            block = scratch_ref[side, start : start + group, :]
            left = jnp.where(keep, block[:, None, :], 0.0).reshape(group * heads, size).astype(BF16)
            part = matmul(left, cots[side])
            total = part if total is None else total + part
        out_ref[start * heads : (start + group) * heads, :] = total


def latent_kernel(head_count, columns, latent_ref, gain_ref, *refs):
    block_refs, other_refs, out_ref = refs[:columns], refs[columns:-1], refs[-1]
    column = lax.axis_index("ctx") >> 1
    odd = parity(lax.axis_index("head"), head_count.bit_length() - 1)
    raw = latent_ref[...].astype(F32)
    rms = lax.rsqrt(jnp.mean(raw * raw, axis=1, keepdims=True) + 1e-06)
    hat = raw * rms
    relative = [ref[...] for ref in block_refs]
    for j, ref in enumerate(other_refs):
        relative[2 * j] = jnp.where(odd == 0, relative[2 * j], ref[...])
    blocks = []
    for b in range(columns):
        block = relative[0]
        for j in range(1, columns):
            block = jnp.where((column ^ j) == b, relative[j], block)
        blocks.append(block)
    scaled = jnp.concatenate(blocks, axis=1) * gain_ref[...]
    inner = jnp.mean(scaled * hat, axis=1, keepdims=True)
    out_ref[...] = rms * (scaled - hat * inner)


def per_device(head_count, ctx_count, latent, gain, cotangent, weight):
    columns = ctx_count // 2
    owned, width = latent.shape[1:]
    _, tokens, heads, channels = cotangent.shape
    rows = weight.shape[0]
    bits = head_count.bit_length() - 1
    params = pltpu.CompilerParams(vmem_limit_bytes=48 * 1024 * 1024)

    def swap(value, partner):
        pairs = [
            (h * ctx_count + c, p * ctx_count + q)
            for h in range(head_count)
            for c in range(ctx_count)
            for p, q in [partner(h, c)]
        ]
        return lax.ppermute(value, ("head", "ctx"), pairs)

    def ctx_swap(value, mask):
        return swap(value, lambda h, c: (h, c ^ mask))

    def role_swap(value, mask):
        return swap(value, lambda h, c: (h, c ^ mask ^ parity(h, bits)))

    def head_swap(value, mask):
        return swap(value, lambda h, c: (h ^ mask, c ^ 1))

    def call(kernel, out, *args, scratch=(), flops=0):
        moved = sum(a.size * a.dtype.itemsize for a in args)
        return pl.pallas_call(
            kernel,
            out_shape=out,
            scratch_shapes=scratch,
            compiler_params=params,
            cost_estimate=pl.CostEstimate(flops=flops, bytes_accessed=moved, transcendentals=0),
        )(*args)

    own = cotangent.reshape(tokens * heads, channels)
    far = [role_swap(own, 2)]
    other = ctx_swap(own, 1)
    if columns > 2:
        first = jnp.where(parity(lax.axis_index("head"), bits) == 0, own, other)
        shards = [first] + far
        mask = 4
        while mask < ctx_count:
            shards += [ctx_swap(s, mask) for s in shards]
            mask *= 2
        far = shards[1:]
    latent_other = ctx_swap(latent[0], 1)
    gain_row = gain.reshape(1, width)
    block = jax.ShapeDtypeStruct((2 * owned, 2 * rows), F32)
    normed = list(call(functools.partial(norm_kernel, columns), [block] * columns, latent[0], latent_other, gain_row, flops=4 * 10**8))

    weight_flat = weight.reshape(rows * heads, channels)
    weight_other = ctx_swap(weight_flat, 1)
    weight_flat, weight_other, *normed = lax.optimization_barrier((weight_flat, weight_other, *normed))
    chip_weight = call(
        functools.partial(weight_kernel, heads),
        jax.ShapeDtypeStruct((heads, 2 * rows, channels), BF16),
        weight_flat,
        weight_other,
    )

    mask = 2
    while mask < ctx_count:
        for j in range(columns):
            if j & (mask >> 1):
                normed[j] = ctx_swap(normed[j], mask | 1)
        mask *= 2
    normed = jnp.concatenate(normed, axis=0)

    sums = call(
        functools.partial(partial_kernel, head_count, heads, owned),
        jax.ShapeDtypeStruct((head_count * columns * owned, 2 * rows), F32),
        own,
        other,
        *far,
        chip_weight,
    )
    core = lax.axis_index("ctx") & 1
    mask = 1
    while mask < head_count:
        half = sums.shape[0] // 2
        if 2 * mask < head_count:
            got = head_swap(jnp.concatenate([sums[half:], normed], axis=0), mask)
            normed = jnp.concatenate([normed, got[half:]], axis=0)
        else:
            keep = jnp.where(core == 0, normed[:, :rows], normed[:, rows:])
            send = jnp.where(core == 0, normed[:, rows:], normed[:, :rows])
            count = send.shape[0] // 2
            send = jnp.concatenate([send[:count], send[count:]], axis=1)
            got = head_swap(jnp.concatenate([sums[half:], send], axis=0), mask)
            normed = jnp.concatenate([keep, got[half:, :rows], got[half:, rows:]], axis=0)
        sums = sums[:half] + got[:half]
        mask *= 2

    blocks = [sums[j * owned : (j + 1) * owned] for j in range(columns)]
    mask = ctx_count // 2
    while mask > 2:
        for j in range(columns):
            if j & (mask >> 1):
                blocks[j] = ctx_swap(blocks[j], mask)
        mask //= 2
    kept = [ctx_swap(blocks[j], 1) for j in range(0, columns, 2)]
    for j in range(1, columns, 2):
        blocks[j] = role_swap(blocks[j], 2)

    weight_grad = call(
        functools.partial(weight_grad_kernel, head_count, heads, owned, columns),
        jax.ShapeDtypeStruct((rows * heads, channels), F32),
        normed,
        own,
        *far,
        other,
        *[ctx_swap(s, 1) for s in far],
        scratch=[pltpu.VMEM((2, rows, columns * tokens * heads), F32)],
        flops=2 * rows * heads * channels * ctx_count * tokens * heads,
    )
    latent_gradient = call(
        functools.partial(latent_kernel, head_count, columns),
        jax.ShapeDtypeStruct((owned, width), F32),
        latent[0],
        gain_row,
        *blocks,
        *kept,
    )
    return latent_gradient[None], weight_grad.reshape(weight.shape)


def solution(mesh):
    return jax.shard_map(
        functools.partial(per_device, mesh.shape["head"], mesh.shape["ctx"]),
        mesh=mesh,
        in_specs=(
            P("ctx", "head", None),
            P(),
            P("ctx", None, "head", None),
            P("ctx", "head", None),
        ),
        out_specs=(P("ctx", "head", None), P("ctx", "head", None)),
        check_vma=False,
    )
```

```python
import functools

import jax
import jax.numpy as jnp
from jax import lax
from jax.experimental import pallas as pl
from jax.experimental.pallas import tpu as pltpu
from jax.sharding import PartitionSpec as P


F32 = jnp.float32
BF16 = jnp.bfloat16


def iota(shape, axis):
    return lax.broadcasted_iota(jnp.int32, shape, axis)


def one_hot(condition):
    return jnp.where(condition, 1.0, 0.0).astype(BF16)


def matmul(a, b, a_axis=1, b_axis=0):
    return lax.dot_general(a, b, (((a_axis,), (b_axis,)), ((), ())), preferred_element_type=F32)


def reverse_bits(value, count):
    out = 0
    for bit in range(count):
        out = out | (((value >> bit) & 1) << (count - 1 - bit))
    return out


def parity(value, count):
    out = value & 1
    for bit in range(1, count):
        out = out ^ ((value >> bit) & 1)
    return out


def weight_kernel(heads, own_ref, other_ref, out_ref):
    core = lax.axis_index("ctx") & 1
    rows = own_ref.shape[0] // heads
    group = min(rows, max(256 // heads, 1))
    size = group * heads
    to, at = iota((size, size), 0), iota((size, size), 1)
    order = one_hot(at == (to % group) * heads + to // group)
    for ref, place in ((own_ref, core), (other_ref, 1 - core)):
        for start in range(0, rows, group):
            moved = matmul(order, ref[pl.ds(start * heads, size), :]).astype(BF16)
            first = pl.multiple_of(place * rows + start, group)
            for h in range(heads):
                out_ref[h, pl.ds(first, group), :] = moved[h * group : (h + 1) * group, :]


def partial_kernel(head_count, heads, owned, own_ref, other_ref, *refs):
    shard_refs, weight_ref, out_ref = refs[:-2], refs[-2], refs[-1]
    shards = len(shard_refs) + 1
    me = lax.axis_index("head")
    bits = head_count.bit_length() - 1
    rows = head_count * owned
    first = jnp.where(parity(me, bits) == 0, own_ref[...], other_ref[...])
    stacked = jnp.concatenate([first] + [ref[...] for ref in shard_refs], axis=0)
    size = shards * rows * heads
    to, at = iota((size, size), 0), iota((size, size), 1)
    i, j = to % owned, (to // owned) % shards
    position = (to // (owned * shards)) % head_count
    token = (reverse_bits(position, bits) ^ me) * owned + i
    order = one_hot(at == (j * rows + token) * heads + to // (rows * shards))
    moved = matmul(order, stacked).astype(BF16)
    part = rows * shards
    total = matmul(moved[:part], weight_ref[0], 1, 1)
    for h in range(1, heads):
        total += matmul(moved[h * part : (h + 1) * part], weight_ref[h], 1, 1)
    out_ref[...] = total


def norm_kernel(columns, own_ref, other_ref, gain_ref, *out_refs):
    core, column = lax.axis_index("ctx") & 1, lax.axis_index("ctx") >> 1
    own, other = own_ref[...].astype(F32), other_ref[...].astype(F32)
    raw = jnp.concatenate([jnp.where(core == 0, own, other), jnp.where(core == 0, other, own)], axis=0)
    rms = lax.rsqrt(jnp.mean(raw * raw, axis=1, keepdims=True) + 1e-06)
    normed = ((raw * rms) * gain_ref[...]).astype(BF16).astype(F32)
    width = normed.shape[1] // columns
    for j, ref in enumerate(out_refs):
        block = normed[:, :width]
        for b in range(1, columns):
            block = jnp.where((column ^ j) == b, normed[:, b * width : (b + 1) * width], block)
        ref[...] = block


def weight_grad_kernel(head_count, heads, owned, columns, normed_ref, *refs):
    shard_refs, out_ref, scratch_ref = refs[:-2], refs[-2], refs[-1]
    me = lax.axis_index("head")
    core = lax.axis_index("ctx") & 1
    role = core ^ parity(me, head_count.bit_length() - 1)
    rows = out_ref.shape[0] // heads
    tokens = head_count * owned
    normed = normed_ref[...].astype(BF16)
    size = columns * tokens * heads
    at, to = iota((normed.shape[0], size), 0), iota((normed.shape[0], size), 1)
    token, j = (to // heads) % tokens, to // (heads * tokens)
    cots = []
    for side in range(2):
        place = (((token // owned) ^ me) * columns + j) * 2 + (jnp.where(j == 0, core, role) ^ side)
        spread = one_hot(at == place * owned + token % owned)
        scratch_ref[side] = matmul(normed, spread, 0, 0)
        cots.append(jnp.concatenate([r[...] for r in shard_refs[side * columns : (side + 1) * columns]], axis=0))
    group = min(rows, max(256 // heads, 1))
    keep = (iota((1, heads, size), 2) % heads) == iota((1, heads, size), 1)
    for start in range(0, rows, group):
        total = None
        for side in range(2):
            block = scratch_ref[side, start : start + group, :]
            left = jnp.where(keep, block[:, None, :], 0.0).reshape(group * heads, size).astype(BF16)
            part = matmul(left, cots[side])
            total = part if total is None else total + part
        out_ref[start * heads : (start + group) * heads, :] = total


def latent_kernel(head_count, columns, latent_ref, gain_ref, *refs):
    block_refs, other_refs, out_ref = refs[:columns], refs[columns:-1], refs[-1]
    column = lax.axis_index("ctx") >> 1
    odd = parity(lax.axis_index("head"), head_count.bit_length() - 1)
    raw = latent_ref[...].astype(F32)
    rms = lax.rsqrt(jnp.mean(raw * raw, axis=1, keepdims=True) + 1e-06)
    hat = raw * rms
    relative = [ref[...] for ref in block_refs]
    for j, ref in enumerate(other_refs):
        relative[2 * j] = jnp.where(odd == 0, relative[2 * j], ref[...])
    blocks = []
    for b in range(columns):
        block = relative[0]
        for j in range(1, columns):
            block = jnp.where((column ^ j) == b, relative[j], block)
        blocks.append(block)
    scaled = jnp.concatenate(blocks, axis=1) * gain_ref[...]
    inner = jnp.mean(scaled * hat, axis=1, keepdims=True)
    out_ref[...] = rms * (scaled - hat * inner)


def per_device(head_count, ctx_count, latent, gain, cotangent, weight):
    columns = ctx_count // 2
    owned, width = latent.shape[1:]
    _, tokens, heads, channels = cotangent.shape
    rows = weight.shape[0]
    bits = head_count.bit_length() - 1
    params = pltpu.CompilerParams(vmem_limit_bytes=48 * 1024 * 1024)

    def swap(value, partner):
        pairs = [
            (h * ctx_count + c, p * ctx_count + q)
            for h in range(head_count)
            for c in range(ctx_count)
            for p, q in [partner(h, c)]
        ]
        return lax.ppermute(value, ("head", "ctx"), pairs)

    def ctx_swap(value, mask):
        return swap(value, lambda h, c: (h, c ^ mask))

    def role_swap(value, mask):
        return swap(value, lambda h, c: (h, c ^ mask ^ parity(h, bits)))

    def head_swap(value, mask):
        return swap(value, lambda h, c: (h ^ mask, c ^ 1))

    def call(kernel, out, *args, scratch=(), flops=0):
        moved = sum(a.size * a.dtype.itemsize for a in args)
        return pl.pallas_call(
            kernel,
            out_shape=out,
            scratch_shapes=scratch,
            compiler_params=params,
            cost_estimate=pl.CostEstimate(flops=flops, bytes_accessed=moved, transcendentals=0),
        )(*args)

    own = cotangent.reshape(tokens * heads, channels)
    far = [role_swap(own, 2)]
    other = ctx_swap(own, 1)
    if columns > 2:
        first = jnp.where(parity(lax.axis_index("head"), bits) == 0, own, other)
        shards = [first] + far
        mask = 4
        while mask < ctx_count:
            shards += [ctx_swap(s, mask) for s in shards]
            mask *= 2
        far = shards[1:]
    latent_other = ctx_swap(latent[0], 1)
    gain_row = gain.reshape(1, width)
    block = jax.ShapeDtypeStruct((2 * owned, 2 * rows), F32)
    normed = list(call(functools.partial(norm_kernel, columns), [block] * columns, latent[0], latent_other, gain_row, flops=10**9))

    weight_flat = weight.reshape(rows * heads, channels)
    weight_other = ctx_swap(weight_flat, 1)
    weight_flat, weight_other, *normed = lax.optimization_barrier((weight_flat, weight_other, *normed))
    chip_weight = call(
        functools.partial(weight_kernel, heads),
        jax.ShapeDtypeStruct((heads, 2 * rows, channels), BF16),
        weight_flat,
        weight_other,
    )

    mask = 2
    while mask < ctx_count:
        for j in range(columns):
            if j & (mask >> 1):
                normed[j] = ctx_swap(normed[j], mask | 1)
        mask *= 2
    normed = jnp.concatenate(normed, axis=0)

    sums = call(
        functools.partial(partial_kernel, head_count, heads, owned),
        jax.ShapeDtypeStruct((head_count * columns * owned, 2 * rows), F32),
        own,
        other,
        *far,
        chip_weight,
    )
    core = lax.axis_index("ctx") & 1
    mask = 1
    while mask < head_count:
        half = sums.shape[0] // 2
        if 2 * mask < head_count:
            got = head_swap(jnp.concatenate([sums[half:], normed], axis=0), mask)
            normed = jnp.concatenate([normed, got[half:]], axis=0)
        else:
            keep = jnp.where(core == 0, normed[:, :rows], normed[:, rows:])
            send = jnp.where(core == 0, normed[:, rows:], normed[:, :rows])
            count = send.shape[0] // 2
            send = jnp.concatenate([send[:count], send[count:]], axis=1)
            got = head_swap(jnp.concatenate([sums[half:], send], axis=0), mask)
            normed = jnp.concatenate([keep, got[half:, :rows], got[half:, rows:]], axis=0)
        sums = sums[:half] + got[:half]
        mask *= 2

    blocks = [sums[j * owned : (j + 1) * owned] for j in range(columns)]
    mask = ctx_count // 2
    while mask > 2:
        for j in range(columns):
            if j & (mask >> 1):
                blocks[j] = ctx_swap(blocks[j], mask)
        mask //= 2
    kept = [ctx_swap(blocks[j], 1) for j in range(0, columns, 2)]
    for j in range(1, columns, 2):
        blocks[j] = role_swap(blocks[j], 2)

    weight_grad = call(
        functools.partial(weight_grad_kernel, head_count, heads, owned, columns),
        jax.ShapeDtypeStruct((rows * heads, channels), F32),
        normed,
        own,
        *far,
        other,
        *[ctx_swap(s, 1) for s in far],
        scratch=[pltpu.VMEM((2, rows, columns * tokens * heads), F32)],
        flops=2 * rows * heads * channels * ctx_count * tokens * heads,
    )
    latent_gradient = call(
        functools.partial(latent_kernel, head_count, columns),
        jax.ShapeDtypeStruct((owned, width), F32),
        latent[0],
        gain_row,
        *blocks,
        *kept,
    )
    return latent_gradient[None], weight_grad.reshape(weight.shape)


def solution(mesh):
    return jax.shard_map(
        functools.partial(per_device, mesh.shape["head"], mesh.shape["ctx"]),
        mesh=mesh,
        in_specs=(
            P("ctx", "head", None),
            P(),
            P("ctx", None, "head", None),
            P("ctx", "head", None),
        ),
        out_specs=(P("ctx", "head", None), P("ctx", "head", None)),
        check_vma=False,
    )
```

```python
import functools

import jax
import jax.numpy as jnp
from jax import lax
from jax.experimental import pallas as pl
from jax.experimental.pallas import tpu as pltpu
from jax.sharding import PartitionSpec as P


F32 = jnp.float32
BF16 = jnp.bfloat16


def iota(shape, axis):
    return lax.broadcasted_iota(jnp.int32, shape, axis)


def one_hot(condition):
    return jnp.where(condition, 1.0, 0.0).astype(BF16)


def matmul(a, b, a_axis=1, b_axis=0):
    return lax.dot_general(a, b, (((a_axis,), (b_axis,)), ((), ())), preferred_element_type=F32)


def reverse_bits(value, count):
    out = 0
    for bit in range(count):
        out = out | (((value >> bit) & 1) << (count - 1 - bit))
    return out


def parity(value, count):
    out = value & 1
    for bit in range(1, count):
        out = out ^ ((value >> bit) & 1)
    return out


def weight_kernel(heads, own_ref, other_ref, out_ref):
    core = lax.axis_index("ctx") & 1
    rows = own_ref.shape[0] // heads
    group = min(rows, max(256 // heads, 1))
    size = group * heads
    to, at = iota((size, size), 0), iota((size, size), 1)
    order = one_hot(at == (to % group) * heads + to // group)
    for ref, place in ((own_ref, core), (other_ref, 1 - core)):
        for start in range(0, rows, group):
            moved = matmul(order, ref[pl.ds(start * heads, size), :]).astype(BF16)
            first = pl.multiple_of(place * rows + start, group)
            for h in range(heads):
                out_ref[h, pl.ds(first, group), :] = moved[h * group : (h + 1) * group, :]


def partial_kernel(head_count, heads, owned, own_ref, other_ref, *refs):
    shard_refs, weight_ref, out_ref = refs[:-2], refs[-2], refs[-1]
    shards = len(shard_refs) + 1
    me = lax.axis_index("head")
    bits = head_count.bit_length() - 1
    rows = head_count * owned
    first = jnp.where(parity(me, bits) == 0, own_ref[...], other_ref[...])
    stacked = jnp.concatenate([first] + [ref[...] for ref in shard_refs], axis=0)
    size = shards * rows * heads
    to, at = iota((size, size), 0), iota((size, size), 1)
    i, j = to % owned, (to // owned) % shards
    position = (to // (owned * shards)) % head_count
    token = (reverse_bits(position, bits) ^ me) * owned + i
    order = one_hot(at == (j * rows + token) * heads + to // (rows * shards))
    moved = matmul(order, stacked).astype(BF16)
    part = rows * shards
    total = matmul(moved[:part], weight_ref[0], 1, 1)
    for h in range(1, heads):
        total += matmul(moved[h * part : (h + 1) * part], weight_ref[h], 1, 1)
    out_ref[...] = total


def norm_kernel(columns, latent_ref, gain_ref, *out_refs):
    column = lax.axis_index("ctx") >> 1
    raw = latent_ref[...].astype(F32)
    rms = lax.rsqrt(jnp.mean(raw * raw, axis=1, keepdims=True) + 1e-06)
    normed = ((raw * rms) * gain_ref[...]).astype(BF16).astype(F32)
    width = normed.shape[1] // columns
    for j, ref in enumerate(out_refs):
        block = normed[:, :width]
        for b in range(1, columns):
            block = jnp.where((column ^ j) == b, normed[:, b * width : (b + 1) * width], block)
        ref[...] = block


def weight_grad_kernel(head_count, heads, owned, columns, own_ref, other_ref, *refs):
    shard_refs, out_ref, scratch_ref = refs[:-2], refs[-2], refs[-1]
    me = lax.axis_index("head")
    core = lax.axis_index("ctx") & 1
    role = core ^ parity(me, head_count.bit_length() - 1)
    rows = out_ref.shape[0] // heads
    tokens = head_count * owned
    normed = jnp.concatenate([own_ref[...], other_ref[...]], axis=0).astype(BF16)
    size = columns * tokens * heads
    at, to = iota((normed.shape[0], size), 0), iota((normed.shape[0], size), 1)
    token, j = (to // heads) % tokens, to // (heads * tokens)
    distance = (token // owned) ^ me
    turned = parity(distance, head_count.bit_length() - 1) ^ (j & 1)
    cots = []
    for side in range(2):
        held = jnp.where(j == 0, core, role) ^ side ^ core ^ turned
        place = (held * head_count + distance) * columns + j
        spread = one_hot(at == place * owned + token % owned)
        scratch_ref[side] = matmul(normed, spread, 0, 0)
        cots.append(jnp.concatenate([r[...] for r in shard_refs[side * columns : (side + 1) * columns]], axis=0))
    group = min(rows, max(256 // heads, 1))
    keep = (iota((1, heads, size), 2) % heads) == iota((1, heads, size), 1)
    for start in range(0, rows, group):
        total = None
        for side in range(2):
            block = scratch_ref[side, start : start + group, :]
            left = jnp.where(keep, block[:, None, :], 0.0).reshape(group * heads, size).astype(BF16)
            part = matmul(left, cots[side])
            total = part if total is None else total + part
        out_ref[start * heads : (start + group) * heads, :] = total


def latent_kernel(head_count, columns, latent_ref, gain_ref, *refs):
    block_refs, other_refs, out_ref = refs[:columns], refs[columns:-1], refs[-1]
    column = lax.axis_index("ctx") >> 1
    odd = parity(lax.axis_index("head"), head_count.bit_length() - 1)
    raw = latent_ref[...].astype(F32)
    rms = lax.rsqrt(jnp.mean(raw * raw, axis=1, keepdims=True) + 1e-06)
    hat = raw * rms
    relative = [ref[...] for ref in block_refs]
    for j, ref in enumerate(other_refs):
        relative[2 * j] = jnp.where(odd == 0, relative[2 * j], ref[...])
    blocks = []
    for b in range(columns):
        block = relative[0]
        for j in range(1, columns):
            block = jnp.where((column ^ j) == b, relative[j], block)
        blocks.append(block)
    scaled = jnp.concatenate(blocks, axis=1) * gain_ref[...]
    inner = jnp.mean(scaled * hat, axis=1, keepdims=True)
    out_ref[...] = rms * (scaled - hat * inner)


def per_device(head_count, ctx_count, latent, gain, cotangent, weight):
    columns = ctx_count // 2
    owned, width = latent.shape[1:]
    _, tokens, heads, channels = cotangent.shape
    rows = weight.shape[0]
    bits = head_count.bit_length() - 1
    params = pltpu.CompilerParams(vmem_limit_bytes=48 * 1024 * 1024)

    def swap(value, partner):
        pairs = [
            (h * ctx_count + c, p * ctx_count + q)
            for h in range(head_count)
            for c in range(ctx_count)
            for p, q in [partner(h, c)]
        ]
        return lax.ppermute(value, ("head", "ctx"), pairs)

    def ctx_swap(value, mask):
        return swap(value, lambda h, c: (h, c ^ mask))

    def role_swap(value, mask):
        return swap(value, lambda h, c: (h, c ^ mask ^ parity(h, bits)))

    def head_swap(value, mask):
        return swap(value, lambda h, c: (h ^ mask, c ^ 1))

    def call(kernel, out, *args, scratch=(), flops=0):
        moved = sum(a.size * a.dtype.itemsize for a in args)
        return pl.pallas_call(
            kernel,
            out_shape=out,
            scratch_shapes=scratch,
            compiler_params=params,
            cost_estimate=pl.CostEstimate(flops=flops, bytes_accessed=moved, transcendentals=0),
        )(*args)

    own = cotangent.reshape(tokens * heads, channels)
    far = [role_swap(own, 2)]
    other = ctx_swap(own, 1)
    if columns > 2:
        first = jnp.where(parity(lax.axis_index("head"), bits) == 0, own, other)
        shards = [first] + far
        mask = 4
        while mask < ctx_count:
            shards += [ctx_swap(s, mask) for s in shards]
            mask *= 2
        far = shards[1:]
    gain_row = gain.reshape(1, width)
    block = jax.ShapeDtypeStruct((owned, 2 * rows), F32)
    normed = list(call(functools.partial(norm_kernel, columns), [block] * columns, latent[0], gain_row, flops=4 * 10**8))

    weight_flat = weight.reshape(rows * heads, channels)
    weight_other = ctx_swap(weight_flat, 1)
    weight_flat, weight_other, *normed = lax.optimization_barrier((weight_flat, weight_other, *normed))
    chip_weight = call(
        functools.partial(weight_kernel, heads),
        jax.ShapeDtypeStruct((heads, 2 * rows, channels), BF16),
        weight_flat,
        weight_other,
    )

    mask = 2
    while mask < ctx_count:
        for j in range(columns):
            if j & (mask >> 1):
                normed[j] = ctx_swap(normed[j], mask | (mask == 2))
        mask *= 2
    normed = jnp.concatenate(normed, axis=0)

    sums = call(
        functools.partial(partial_kernel, head_count, heads, owned),
        jax.ShapeDtypeStruct((head_count * columns * owned, 2 * rows), F32),
        own,
        other,
        *far,
        chip_weight,
    )
    core = lax.axis_index("ctx") & 1
    mask = 1
    while mask < head_count:
        half = sums.shape[0] // 2
        got = head_swap(jnp.concatenate([sums[half:], normed], axis=0), mask)
        normed = jnp.concatenate([normed, got[half:]], axis=0)
        sums = sums[:half] + got[:half]
        mask *= 2

    normed_own = jnp.where(core == 0, normed[:, :rows], normed[:, rows:])
    normed_other = ctx_swap(jnp.where(core == 0, normed[:, rows:], normed[:, :rows]), 1)

    blocks = [sums[j * owned : (j + 1) * owned] for j in range(columns)]
    mask = ctx_count // 2
    while mask > 2:
        for j in range(columns):
            if j & (mask >> 1):
                blocks[j] = ctx_swap(blocks[j], mask)
        mask //= 2
    kept = [ctx_swap(blocks[j], 1) for j in range(0, columns, 2)]
    for j in range(1, columns, 2):
        blocks[j] = role_swap(blocks[j], 2)

    weight_grad = call(
        functools.partial(weight_grad_kernel, head_count, heads, owned, columns),
        jax.ShapeDtypeStruct((rows * heads, channels), F32),
        normed_own,
        normed_other,
        own,
        *far,
        other,
        *[ctx_swap(s, 1) for s in far],
        scratch=[pltpu.VMEM((2, rows, columns * tokens * heads), F32)],
        flops=2 * rows * heads * channels * ctx_count * tokens * heads,
    )
    weight_grad, *blocks = lax.optimization_barrier((weight_grad, *blocks))
    latent_gradient = call(
        functools.partial(latent_kernel, head_count, columns),
        jax.ShapeDtypeStruct((owned, width), F32),
        latent[0],
        gain_row,
        *blocks,
        *kept,
    )
    return latent_gradient[None], weight_grad.reshape(weight.shape)


def solution(mesh):
    return jax.shard_map(
        functools.partial(per_device, mesh.shape["head"], mesh.shape["ctx"]),
        mesh=mesh,
        in_specs=(
            P("ctx", "head", None),
            P(),
            P("ctx", None, "head", None),
            P("ctx", "head", None),
        ),
        out_specs=(P("ctx", "head", None), P("ctx", "head", None)),
        check_vma=False,
    )
```

```python
import functools

import jax
import jax.numpy as jnp
from jax import lax
from jax.experimental import pallas as pl
from jax.experimental.pallas import tpu as pltpu
from jax.sharding import PartitionSpec as P


F32 = jnp.float32
BF16 = jnp.bfloat16


def iota(shape, axis):
    return lax.broadcasted_iota(jnp.int32, shape, axis)


def one_hot(condition):
    return jnp.where(condition, 1.0, 0.0).astype(BF16)


def matmul(a, b, a_axis=1, b_axis=0):
    return lax.dot_general(a, b, (((a_axis,), (b_axis,)), ((), ())), preferred_element_type=F32)


def reverse_bits(value, count):
    out = 0
    for bit in range(count):
        out = out | (((value >> bit) & 1) << (count - 1 - bit))
    return out


def even_bits(value, count):
    out = 1 ^ (value & 1)
    for bit in range(1, count):
        out = out ^ ((value >> bit) & 1)
    return out


def weight_kernel(heads, own_ref, other_ref, out_ref):
    core = lax.axis_index("ctx") & 1
    rows = own_ref.shape[0] // heads
    group = min(rows, max(256 // heads, 1))
    size = group * heads
    to, at = iota((size, size), 0), iota((size, size), 1)
    order = one_hot(at == (to % group) * heads + to // group)
    for ref, place in ((own_ref, core), (other_ref, 1 - core)):
        for start in range(0, rows, group):
            moved = matmul(order, ref[pl.ds(start * heads, size), :]).astype(BF16)
            first = pl.multiple_of(place * rows + start, group)
            for h in range(heads):
                out_ref[h, pl.ds(first, group), :] = moved[h * group : (h + 1) * group, :]


def partial_kernel(head_count, heads, owned, own_ref, other_ref, *refs):
    shard_refs, weight_ref, out_ref = refs[:-2], refs[-2], refs[-1]
    shards = len(shard_refs) + 1
    me = lax.axis_index("head")
    bits = head_count.bit_length() - 1
    rows = head_count * owned
    first = jnp.where(even_bits(me, bits) == 0, own_ref[...], other_ref[...])
    stacked = jnp.concatenate([first] + [ref[...] for ref in shard_refs], axis=0)
    size = shards * rows * heads
    to, at = iota((size, size), 0), iota((size, size), 1)
    i, j = to % owned, (to // owned) % shards
    position = (to // (owned * shards)) % head_count
    token = (reverse_bits(position, bits) ^ me) * owned + i
    order = one_hot(at == (j * rows + token) * heads + to // (rows * shards))
    moved = matmul(order, stacked).astype(BF16)
    part = rows * shards
    total = matmul(moved[:part], weight_ref[0], 1, 1)
    for h in range(1, heads):
        total += matmul(moved[h * part : (h + 1) * part], weight_ref[h], 1, 1)
    out_ref[...] = total


def norm_kernel(columns, latent_ref, gain_ref, *out_refs):
    column = lax.axis_index("ctx") >> 1
    raw = latent_ref[...].astype(F32)
    rms = lax.rsqrt(jnp.mean(raw * raw, axis=1, keepdims=True) + 1e-06)
    normed = ((raw * rms) * gain_ref[...]).astype(BF16).astype(F32)
    width = normed.shape[1] // columns
    for j, ref in enumerate(out_refs):
        block = normed[:, :width]
        for b in range(1, columns):
            block = jnp.where((column ^ j) == b, normed[:, b * width : (b + 1) * width], block)
        ref[...] = block


def weight_grad_kernel(head_count, heads, owned, columns, own_ref, other_ref, *refs):
    shard_refs, out_ref, scratch_ref = refs[:-2], refs[-2], refs[-1]
    me = lax.axis_index("head")
    core = lax.axis_index("ctx") & 1
    role = core ^ even_bits(me, head_count.bit_length() - 1)
    rows = out_ref.shape[0] // heads
    tokens = head_count * owned
    normed = jnp.concatenate([own_ref[...], other_ref[...]], axis=0).astype(BF16)
    size = columns * tokens * heads
    at, to = iota((normed.shape[0], size), 0), iota((normed.shape[0], size), 1)
    token, j = (to // heads) % tokens, to // (heads * tokens)
    distance = (token // owned) ^ me
    turned = 1 ^ even_bits(distance, head_count.bit_length() - 1) ^ (j & 1)
    cots = []
    for side in range(2):
        held = jnp.where(j == 0, core, role) ^ side ^ core ^ turned
        place = (held * head_count + distance) * columns + j
        spread = one_hot(at == place * owned + token % owned)
        scratch_ref[side] = matmul(normed, spread, 0, 0)
        cots.append(jnp.concatenate([r[...] for r in shard_refs[side * columns : (side + 1) * columns]], axis=0))
    group = min(rows, max(256 // heads, 1))
    keep = (iota((1, heads, size), 2) % heads) == iota((1, heads, size), 1)
    for start in range(0, rows, group):
        total = None
        for side in range(2):
            block = scratch_ref[side, start : start + group, :]
            left = jnp.where(keep, block[:, None, :], 0.0).reshape(group * heads, size).astype(BF16)
            part = matmul(left, cots[side])
            total = part if total is None else total + part
        out_ref[start * heads : (start + group) * heads, :] = total


def latent_kernel(head_count, columns, latent_ref, gain_ref, *refs):
    block_refs, other_refs, out_ref = refs[:columns], refs[columns:-1], refs[-1]
    column = lax.axis_index("ctx") >> 1
    crossed = even_bits(lax.axis_index("head"), head_count.bit_length() - 1)
    raw = latent_ref[...].astype(F32)
    rms = lax.rsqrt(jnp.mean(raw * raw, axis=1, keepdims=True) + 1e-06)
    hat = raw * rms
    relative = [ref[...] for ref in block_refs]
    for j, ref in enumerate(other_refs):
        relative[2 * j] = jnp.where(crossed == 0, relative[2 * j], ref[...])
    blocks = []
    for b in range(columns):
        block = relative[0]
        for j in range(1, columns):
            block = jnp.where((column ^ j) == b, relative[j], block)
        blocks.append(block)
    scaled = jnp.concatenate(blocks, axis=1) * gain_ref[...]
    inner = jnp.mean(scaled * hat, axis=1, keepdims=True)
    out_ref[...] = rms * (scaled - hat * inner)


def per_device(head_count, ctx_count, latent, gain, cotangent, weight):
    columns = ctx_count // 2
    owned, width = latent.shape[1:]
    _, tokens, heads, channels = cotangent.shape
    rows = weight.shape[0]
    bits = head_count.bit_length() - 1
    params = pltpu.CompilerParams(vmem_limit_bytes=48 * 1024 * 1024)

    def swap(value, partner):
        pairs = [
            (h * ctx_count + c, p * ctx_count + q)
            for h in range(head_count)
            for c in range(ctx_count)
            for p, q in [partner(h, c)]
        ]
        return lax.ppermute(value, ("head", "ctx"), pairs)

    def ctx_swap(value, mask):
        return swap(value, lambda h, c: (h, c ^ mask))

    def role_swap(value, mask):
        return swap(value, lambda h, c: (h, c ^ mask ^ even_bits(h, bits)))

    def head_swap(value, mask):
        return swap(value, lambda h, c: (h ^ mask, c ^ 1))

    def call(kernel, out, *args, scratch=(), flops=0):
        moved = sum(a.size * a.dtype.itemsize for a in args)
        return pl.pallas_call(
            kernel,
            out_shape=out,
            scratch_shapes=scratch,
            compiler_params=params,
            cost_estimate=pl.CostEstimate(flops=flops, bytes_accessed=moved, transcendentals=0),
        )(*args)

    own = cotangent.reshape(tokens * heads, channels)
    far = [role_swap(own, 2)]
    other = ctx_swap(own, 1)
    if columns > 2:
        first = jnp.where(even_bits(lax.axis_index("head"), bits) == 0, own, other)
        shards = [first] + far
        mask = 4
        while mask < ctx_count:
            shards += [ctx_swap(s, mask) for s in shards]
            mask *= 2
        far = shards[1:]
    gain_row = gain.reshape(1, width)
    block = jax.ShapeDtypeStruct((owned, 2 * rows), F32)
    normed = list(call(functools.partial(norm_kernel, columns), [block] * columns, latent[0], gain_row, flops=4 * 10**8))

    weight_flat = weight.reshape(rows * heads, channels)
    weight_other = ctx_swap(weight_flat, 1)
    weight_flat, weight_other, *normed = lax.optimization_barrier((weight_flat, weight_other, *normed))
    chip_weight = call(
        functools.partial(weight_kernel, heads),
        jax.ShapeDtypeStruct((heads, 2 * rows, channels), BF16),
        weight_flat,
        weight_other,
    )

    mask = 2
    while mask < ctx_count:
        for j in range(columns):
            if j & (mask >> 1):
                normed[j] = ctx_swap(normed[j], mask | (mask == 2))
        mask *= 2
    normed = jnp.concatenate(normed, axis=0)

    sums = call(
        functools.partial(partial_kernel, head_count, heads, owned),
        jax.ShapeDtypeStruct((head_count * columns * owned, 2 * rows), F32),
        own,
        other,
        *far,
        chip_weight,
    )
    core = lax.axis_index("ctx") & 1
    mask = 1
    while mask < head_count:
        half = sums.shape[0] // 2
        got = head_swap(jnp.concatenate([sums[half:], normed], axis=0), mask)
        normed = jnp.concatenate([normed, got[half:]], axis=0)
        sums = sums[:half] + got[:half]
        mask *= 2

    normed_own = jnp.where(core == 0, normed[:, :rows], normed[:, rows:])
    normed_other = ctx_swap(jnp.where(core == 0, normed[:, rows:], normed[:, :rows]), 1)

    blocks = [sums[j * owned : (j + 1) * owned] for j in range(columns)]
    mask = ctx_count // 2
    while mask > 2:
        for j in range(columns):
            if j & (mask >> 1):
                blocks[j] = ctx_swap(blocks[j], mask)
        mask //= 2
    kept = [ctx_swap(blocks[j], 1) for j in range(0, columns, 2)]
    for j in range(1, columns, 2):
        blocks[j] = role_swap(blocks[j], 2)

    weight_grad = call(
        functools.partial(weight_grad_kernel, head_count, heads, owned, columns),
        jax.ShapeDtypeStruct((rows * heads, channels), F32),
        normed_own,
        normed_other,
        own,
        *far,
        other,
        *[ctx_swap(s, 1) for s in far],
        scratch=[pltpu.VMEM((2, rows, columns * tokens * heads), F32)],
        flops=2 * rows * heads * channels * ctx_count * tokens * heads,
    )
    weight_grad, *blocks = lax.optimization_barrier((weight_grad, *blocks))
    latent_gradient = call(
        functools.partial(latent_kernel, head_count, columns),
        jax.ShapeDtypeStruct((owned, width), F32),
        latent[0],
        gain_row,
        *blocks,
        *kept,
    )
    return latent_gradient[None], weight_grad.reshape(weight.shape)


def solution(mesh):
    return jax.shard_map(
        functools.partial(per_device, mesh.shape["head"], mesh.shape["ctx"]),
        mesh=mesh,
        in_specs=(
            P("ctx", "head", None),
            P(),
            P("ctx", None, "head", None),
            P("ctx", "head", None),
        ),
        out_specs=(P("ctx", "head", None), P("ctx", "head", None)),
        check_vma=False,
    )
```

```python
import functools

import jax
import jax.numpy as jnp
from jax import lax
from jax.experimental import pallas as pl
from jax.experimental.pallas import tpu as pltpu
from jax.sharding import PartitionSpec as P


F32 = jnp.float32
BF16 = jnp.bfloat16


def iota(shape, axis):
    return lax.broadcasted_iota(jnp.int32, shape, axis)


def one_hot(condition):
    return jnp.where(condition, 1.0, 0.0).astype(BF16)


def matmul(a, b, a_axis=1, b_axis=0):
    return lax.dot_general(a, b, (((a_axis,), (b_axis,)), ((), ())), preferred_element_type=F32)


def whole(value, step):
    return value >> (step.bit_length() - 1) if step & (step - 1) == 0 else value // step


def rest(value, step):
    return value & (step - 1) if step & (step - 1) == 0 else value % step


def reverse_bits(value, count):
    out = 0
    for bit in range(count):
        out = out | (((value >> bit) & 1) << (count - 1 - bit))
    return out


def even_bits(value, count):
    out = 1 ^ (value & 1)
    for bit in range(1, count):
        out = out ^ ((value >> bit) & 1)
    return out


def weight_kernel(heads, own_ref, other_ref, out_ref):
    core = lax.axis_index("ctx") & 1
    rows = own_ref.shape[0] // heads
    group = min(rows, max(256 // heads, 1))
    size = group * heads
    to, at = iota((size, size), 0), iota((size, size), 1)
    order = one_hot(at == rest(to, group) * heads + whole(to, group))
    for ref, place in ((own_ref, core), (other_ref, 1 - core)):
        for start in range(0, rows, group):
            moved = matmul(order, ref[pl.ds(start * heads, size), :]).astype(BF16)
            first = pl.multiple_of(place * rows + start, group)
            for h in range(heads):
                out_ref[h, pl.ds(first, group), :] = moved[h * group : (h + 1) * group, :]


def partial_kernel(head_count, heads, owned, own_ref, other_ref, *refs):
    shard_refs, weight_ref, out_ref = refs[:-2], refs[-2], refs[-1]
    shards = len(shard_refs) + 1
    me = lax.axis_index("head")
    bits = head_count.bit_length() - 1
    rows = head_count * owned
    first = jnp.where(even_bits(me, bits) == 0, own_ref[...], other_ref[...])
    stacked = jnp.concatenate([first] + [ref[...] for ref in shard_refs], axis=0)
    size = shards * rows * heads
    to, at = iota((size, size), 0), iota((size, size), 1)
    i, j = rest(to, owned), rest(whole(to, owned), shards)
    position = rest(whole(to, owned * shards), head_count)
    token = (reverse_bits(position, bits) ^ me) * owned + i
    order = one_hot(at == (j * rows + token) * heads + whole(to, rows * shards))
    moved = matmul(order, stacked).astype(BF16)
    part = rows * shards
    total = matmul(moved[:part], weight_ref[0], 1, 1)
    for h in range(1, heads):
        total += matmul(moved[h * part : (h + 1) * part], weight_ref[h], 1, 1)
    out_ref[...] = total


def norm_kernel(columns, latent_ref, gain_ref, *out_refs):
    column = lax.axis_index("ctx") >> 1
    raw = latent_ref[...].astype(F32)
    rms = lax.rsqrt(jnp.mean(raw * raw, axis=1, keepdims=True) + 1e-06)
    normed = ((raw * rms) * gain_ref[...]).astype(BF16).astype(F32)
    width = normed.shape[1] // columns
    for j, ref in enumerate(out_refs):
        block = normed[:, :width]
        for b in range(1, columns):
            block = jnp.where((column ^ j) == b, normed[:, b * width : (b + 1) * width], block)
        ref[...] = block


def weight_grad_kernel(head_count, heads, owned, columns, own_ref, other_ref, *refs):
    shard_refs, (out_ref, spread_ref, total_ref, sems) = refs[:-4], refs[-4:]
    me = lax.axis_index("head")
    core = lax.axis_index("ctx") & 1
    role = core ^ even_bits(me, head_count.bit_length() - 1)
    groups = sems.shape[0]
    rows = out_ref.shape[0] // heads // groups
    tokens = head_count * owned
    normed = jnp.concatenate([own_ref[...], other_ref[...]], axis=0).astype(BF16)
    size = columns * tokens * heads
    at, to = iota((normed.shape[0], size), 0), iota((1, size), 1)
    token, j = rest(whole(to, heads), tokens), whole(to, heads * tokens)
    distance = whole(token, owned) ^ me
    turned = 1 ^ even_bits(distance, head_count.bit_length() - 1) ^ (j & 1)
    cots = []
    for side in range(2):
        held = jnp.where(j == 0, core, role) ^ side ^ core ^ turned
        place = ((held * head_count + distance) * columns + j) * owned + rest(token, owned)
        spread_ref[side] = matmul(normed, one_hot(at == place), 0, 0)
        cots.append(jnp.concatenate([r[...] for r in shard_refs[side * columns : (side + 1) * columns]], axis=0))
    keep = rest(iota((1, heads, size), 2), heads) == iota((1, heads, size), 1)
    copies = []
    for g in range(groups):
        total = None
        for side in range(2):
            block = spread_ref[side, g * rows : (g + 1) * rows, :]
            left = jnp.where(keep, block[:, None, :], 0.0).reshape(rows * heads, size).astype(BF16)
            part = matmul(left, cots[side])
            total = part if total is None else total + part
        place = pl.ds(g * rows * heads, rows * heads)
        total_ref[place, :] = total
        copies.append(pltpu.make_async_copy(total_ref.at[place], out_ref.at[place], sems.at[g]))
        copies[g].start()
    for copy in copies:
        copy.wait()


def latent_kernel(head_count, columns, latent_ref, gain_ref, other_ref, *refs):
    block_refs, out_ref = refs[:-1], refs[-1]
    column = lax.axis_index("ctx") >> 1
    crossed = even_bits(lax.axis_index("head"), head_count.bit_length() - 1)
    raw = latent_ref[...].astype(F32)
    rms = lax.rsqrt(jnp.mean(raw * raw, axis=1, keepdims=True) + 1e-06)
    hat = raw * rms
    relative = [ref[...] for ref in block_refs]
    count = raw.shape[0]
    for j in range(0, columns, 2):
        relative[j] = jnp.where(crossed == 0, relative[j], other_ref[j // 2 * count : (j // 2 + 1) * count, :])
    blocks = []
    for b in range(columns):
        block = relative[0]
        for j in range(1, columns):
            block = jnp.where((column ^ j) == b, relative[j], block)
        blocks.append(block)
    scaled = jnp.concatenate(blocks, axis=1) * gain_ref[...]
    inner = jnp.mean(scaled * hat, axis=1, keepdims=True)
    out_ref[...] = rms * (scaled - hat * inner)


def per_device(head_count, ctx_count, latent, gain, cotangent, weight):
    columns = ctx_count // 2
    owned, width = latent.shape[1:]
    _, tokens, heads, channels = cotangent.shape
    rows = weight.shape[0]
    bits = head_count.bit_length() - 1
    params = pltpu.CompilerParams(vmem_limit_bytes=48 * 1024 * 1024)

    def swap(value, partner):
        pairs = [
            (h * ctx_count + c, p * ctx_count + q)
            for h in range(head_count)
            for c in range(ctx_count)
            for p, q in [partner(h, c)]
        ]
        return lax.ppermute(value, ("head", "ctx"), pairs)

    def ctx_swap(value, mask):
        return swap(value, lambda h, c: (h, c ^ mask))

    def role_swap(value, mask):
        return swap(value, lambda h, c: (h, c ^ mask ^ even_bits(h, bits)))

    def head_swap(value, mask):
        return swap(value, lambda h, c: (h ^ mask, c ^ 1))

    def call(kernel, out, *args, scratch=(), flops=0, place=pltpu.VMEM):
        moved = sum(a.size * a.dtype.itemsize for a in args)
        return pl.pallas_call(
            kernel,
            out_shape=out,
            out_specs=jax.tree.map(lambda _: pl.BlockSpec(memory_space=place), out),
            scratch_shapes=scratch,
            compiler_params=params,
            cost_estimate=pl.CostEstimate(flops=flops, bytes_accessed=moved, transcendentals=0),
        )(*args)

    own = cotangent.reshape(tokens * heads, channels)
    far = [role_swap(own, 2)]
    other = ctx_swap(own, 1)
    if columns > 2:
        first = jnp.where(even_bits(lax.axis_index("head"), bits) == 0, own, other)
        shards = [first] + far
        mask = 4
        while mask < ctx_count:
            shards += [ctx_swap(s, mask) for s in shards]
            mask *= 2
        far = shards[1:]
    gain_row = gain.reshape(1, width)
    block = jax.ShapeDtypeStruct((owned, 2 * rows), F32)
    normed = list(call(functools.partial(norm_kernel, columns), [block] * columns, latent[0], gain_row, flops=4 * 10**8))

    weight_flat = weight.reshape(rows * heads, channels)
    weight_other = ctx_swap(weight_flat, 1)
    weight_flat, weight_other, *normed = lax.optimization_barrier((weight_flat, weight_other, *normed))
    chip_weight = call(
        functools.partial(weight_kernel, heads),
        jax.ShapeDtypeStruct((heads, 2 * rows, channels), BF16),
        weight_flat,
        weight_other,
    )

    mask = 2
    while mask < ctx_count:
        for j in range(columns):
            if j & (mask >> 1):
                normed[j] = ctx_swap(normed[j], mask | (mask == 2))
        mask *= 2
    normed = jnp.concatenate(normed, axis=0)

    sums = call(
        functools.partial(partial_kernel, head_count, heads, owned),
        jax.ShapeDtypeStruct((head_count * columns * owned, 2 * rows), F32),
        own,
        other,
        *far,
        chip_weight,
    )
    core = lax.axis_index("ctx") & 1
    far_other = [ctx_swap(s, 1) for s in far]
    mask = 1
    while mask < head_count:
        if mask == 2:
            sums, *far_other = lax.optimization_barrier((sums, *far_other))
        half = sums.shape[0] // 2
        count = normed.shape[0]
        if half >= count:
            got = head_swap(jnp.concatenate([sums[half:], normed], axis=0), mask)
            got_sums, got_normed = got[:half], got[half:]
        else:
            got = head_swap(jnp.concatenate([normed, sums[half:]], axis=0), mask)
            got_normed, got_sums = got[:count], got[count:]
        normed = jnp.concatenate([normed, got_normed], axis=0)
        sums = sums[:half] + got_sums
        mask *= 2

    blocks = [sums[j * owned : (j + 1) * owned] for j in range(columns)]
    mask = ctx_count // 2
    while mask > 2:
        for j in range(columns):
            if j & (mask >> 1):
                blocks[j] = ctx_swap(blocks[j], mask)
        mask //= 2
    normed_own = jnp.where(core == 0, normed[:, :rows], normed[:, rows:])
    sent = jnp.where(core == 0, normed[:, rows:], normed[:, :rows])
    count = sent.shape[0] // 2
    sent = [sent[:count], sent[count:]]
    both = ctx_swap(jnp.concatenate([jnp.concatenate(sent, axis=1)] + blocks[::2], axis=0), 1)
    normed_other = jnp.concatenate([both[:count, :rows], both[:count, rows:]], axis=0)
    for j in range(1, columns, 2):
        blocks[j] = role_swap(blocks[j], 2)

    weight_grad = call(
        functools.partial(weight_grad_kernel, head_count, heads, owned, columns),
        jax.ShapeDtypeStruct((rows * heads, channels), F32),
        normed_own,
        normed_other,
        own,
        *far,
        other,
        *far_other,
        scratch=[
            pltpu.VMEM((2, rows, columns * tokens * heads), F32),
            pltpu.VMEM((rows * heads, channels), F32),
            pltpu.SemaphoreType.DMA((4 if rows % 32 == 0 else 1,)),
        ],
        flops=2 * rows * heads * channels * ctx_count * tokens * heads,
        place=pl.ANY,
    )
    weight_grad, *blocks = lax.optimization_barrier((weight_grad, *blocks))
    latent_gradient = call(
        functools.partial(latent_kernel, head_count, columns),
        jax.ShapeDtypeStruct((owned, width), F32),
        latent[0],
        gain_row,
        both[count:],
        *blocks,
    )
    return latent_gradient[None], weight_grad.reshape(weight.shape)


def solution(mesh):
    return jax.shard_map(
        functools.partial(per_device, mesh.shape["head"], mesh.shape["ctx"]),
        mesh=mesh,
        in_specs=(
            P("ctx", "head", None),
            P(),
            P("ctx", None, "head", None),
            P("ctx", "head", None),
        ),
        out_specs=(P("ctx", "head", None), P("ctx", "head", None)),
        check_vma=False,
    )
```

```python
import functools

import jax
import jax.numpy as jnp
from jax import lax
from jax.experimental import pallas as pl
from jax.experimental.pallas import tpu as pltpu
from jax.sharding import PartitionSpec as P


F32 = jnp.float32
BF16 = jnp.bfloat16


def iota(shape, axis):
    return lax.broadcasted_iota(jnp.int32, shape, axis)


def one_hot(condition):
    return jnp.where(condition, 1.0, 0.0).astype(BF16)


def matmul(a, b, a_axis=1, b_axis=0):
    return lax.dot_general(a, b, (((a_axis,), (b_axis,)), ((), ())), preferred_element_type=F32)


def whole(value, step):
    return value >> (step.bit_length() - 1) if step & (step - 1) == 0 else value // step


def rest(value, step):
    return value & (step - 1) if step & (step - 1) == 0 else value % step


def reverse_bits(value, count):
    out = 0
    for bit in range(count):
        out = out | (((value >> bit) & 1) << (count - 1 - bit))
    return out


def even_bits(value, count):
    out = 1 ^ (value & 1)
    for bit in range(1, count):
        out = out ^ ((value >> bit) & 1)
    return out


def weight_kernel(head_count, heads, owned, shards, own_ref, other_ref, out_ref, order_ref):
    rows = own_ref.shape[0] // heads
    group = min(rows, max(256 // heads, 1))
    size = group * heads
    to, at = iota((size, size), 0), iota((size, size), 1)
    order = one_hot(at == rest(to, group) * heads + whole(to, group))
    parts = [[] for _ in range(heads)]
    for ref in (own_ref, other_ref):
        for start in range(0, rows, group):
            moved = matmul(order, ref[pl.ds(start * heads, size), :])
            for h in range(heads):
                parts[h].append(moved[h * group : (h + 1) * group, :])
    for h in range(heads):
        out_ref[h] = jnp.concatenate(parts[h], axis=0).T.astype(BF16)
    me = lax.axis_index("head")
    bits = head_count.bit_length() - 1
    tokens = head_count * owned
    size = order_ref.shape[0]
    to, at = iota((size, size), 0), iota((size, size), 1)
    i, j = rest(to, owned), rest(whole(to, owned), shards)
    position = rest(whole(to, owned * shards), head_count)
    token = (reverse_bits(position, bits) ^ me) * owned + i
    order_ref[...] = one_hot(at == (j * tokens + token) * heads + whole(to, tokens * shards))


def partial_kernel(head_count, order_ref, weight_ref, *refs):
    shard_refs, (own_ref, other_ref, out_ref) = refs[:-3], refs[-3:]
    core = lax.axis_index("ctx") & 1
    crossed = even_bits(lax.axis_index("head"), head_count.bit_length() - 1)
    first = jnp.where(crossed == 0, own_ref[...], other_ref[...])
    stacked = jnp.concatenate([first] + [ref[...] for ref in shard_refs], axis=0)
    moved = matmul(order_ref[...], stacked).astype(BF16)
    part, rows = out_ref.shape[0], out_ref.shape[1] // 2
    total = matmul(moved[:part], weight_ref[0])
    for h in range(1, weight_ref.shape[0]):
        total += matmul(moved[h * part : (h + 1) * part], weight_ref[h])
    turned = jnp.concatenate([total[:, rows:], total[:, :rows]], axis=1)
    out_ref[...] = jnp.where(core == 0, total, turned)


def norm_kernel(columns, latent_ref, gain_ref, *out_refs):
    column = lax.axis_index("ctx") >> 1
    raw = latent_ref[...].astype(F32)
    rms = lax.rsqrt(jnp.mean(raw * raw, axis=1, keepdims=True) + 1e-06)
    normed = ((raw * rms) * gain_ref[...]).astype(BF16).astype(F32)
    width = normed.shape[1] // columns
    for j, ref in enumerate(out_refs):
        block = normed[:, :width]
        for b in range(1, columns):
            block = jnp.where((column ^ j) == b, normed[:, b * width : (b + 1) * width], block)
        ref[...] = block


def weight_grad_kernel(head_count, heads, owned, columns, own_ref, other_ref, *refs):
    shard_refs, (out_ref, spread_ref, total_ref, sems) = refs[:-4], refs[-4:]
    me = lax.axis_index("head")
    core = lax.axis_index("ctx") & 1
    role = core ^ even_bits(me, head_count.bit_length() - 1)
    groups = sems.shape[0]
    rows = out_ref.shape[0] // heads // groups
    tokens = head_count * owned
    normed = jnp.concatenate([own_ref[...], other_ref[...]], axis=0).astype(BF16)
    size = columns * tokens * heads
    at, to = iota((normed.shape[0], size), 0), iota((1, size), 1)
    token, j = rest(whole(to, heads), tokens), whole(to, heads * tokens)
    distance = whole(token, owned) ^ me
    turned = 1 ^ even_bits(distance, head_count.bit_length() - 1) ^ (j & 1)
    cots = []
    for side in range(2):
        held = jnp.where(j == 0, core, role) ^ side ^ core ^ turned
        place = ((held * head_count + distance) * columns + j) * owned + rest(token, owned)
        spread_ref[side] = matmul(normed, one_hot(at == place), 0, 0)
        cots.append(jnp.concatenate([r[...] for r in shard_refs[side * columns : (side + 1) * columns]], axis=0))
    keep = rest(iota((1, heads, size), 2), heads) == iota((1, heads, size), 1)
    copies = []
    for g in range(groups):
        total = None
        for side in range(2):
            block = spread_ref[side, g * rows : (g + 1) * rows, :]
            left = jnp.where(keep, block[:, None, :], 0.0).reshape(rows * heads, size).astype(BF16)
            part = matmul(left, cots[side])
            total = part if total is None else total + part
        place = pl.ds(g * rows * heads, rows * heads)
        total_ref[place, :] = total
        copies.append(pltpu.make_async_copy(total_ref.at[place], out_ref.at[place], sems.at[g]))
        copies[g].start()
    for copy in copies:
        copy.wait()


def latent_kernel(head_count, columns, latent_ref, gain_ref, other_ref, *refs):
    block_refs, out_ref = refs[:-1], refs[-1]
    column = lax.axis_index("ctx") >> 1
    crossed = even_bits(lax.axis_index("head"), head_count.bit_length() - 1)
    raw = latent_ref[...].astype(F32)
    rms = lax.rsqrt(jnp.mean(raw * raw, axis=1, keepdims=True) + 1e-06)
    hat = raw * rms
    relative = [ref[...] for ref in block_refs]
    count = raw.shape[0]
    for j in range(0, columns, 2):
        relative[j] = jnp.where(crossed == 0, relative[j], other_ref[j // 2 * count : (j // 2 + 1) * count, :])
    blocks = []
    for b in range(columns):
        block = relative[0]
        for j in range(1, columns):
            block = jnp.where((column ^ j) == b, relative[j], block)
        blocks.append(block)
    scaled = jnp.concatenate(blocks, axis=1) * gain_ref[...]
    inner = jnp.mean(scaled * hat, axis=1, keepdims=True)
    out_ref[...] = rms * (scaled - hat * inner)


def per_device(head_count, ctx_count, latent, gain, cotangent, weight):
    columns = ctx_count // 2
    owned, width = latent.shape[1:]
    _, tokens, heads, channels = cotangent.shape
    rows = weight.shape[0]
    bits = head_count.bit_length() - 1
    params = pltpu.CompilerParams(vmem_limit_bytes=48 * 1024 * 1024)

    def swap(value, partner):
        pairs = [
            (h * ctx_count + c, p * ctx_count + q)
            for h in range(head_count)
            for c in range(ctx_count)
            for p, q in [partner(h, c)]
        ]
        return lax.ppermute(value, ("head", "ctx"), pairs)

    def ctx_swap(value, mask):
        return swap(value, lambda h, c: (h, c ^ mask))

    def role_swap(value, mask):
        return swap(value, lambda h, c: (h, c ^ mask ^ even_bits(h, bits)))

    def head_swap(value, mask):
        return swap(value, lambda h, c: (h ^ mask, c ^ 1))

    def call(kernel, out, *args, scratch=(), flops=0, place=pltpu.VMEM):
        moved = sum(a.size * a.dtype.itemsize for a in args)
        return pl.pallas_call(
            kernel,
            out_shape=out,
            out_specs=jax.tree.map(lambda _: pl.BlockSpec(memory_space=place), out),
            scratch_shapes=scratch,
            compiler_params=params,
            cost_estimate=pl.CostEstimate(flops=flops, bytes_accessed=moved, transcendentals=0),
        )(*args)

    own = cotangent.reshape(tokens * heads, channels)
    far = [role_swap(own, 2)]
    other = ctx_swap(own, 1)
    if columns > 2:
        first = jnp.where(even_bits(lax.axis_index("head"), bits) == 0, own, other)
        shards = [first] + far
        mask = 4
        while mask < ctx_count:
            shards += [ctx_swap(s, mask) for s in shards]
            mask *= 2
        far = shards[1:]
    gain_row = gain.reshape(1, width)
    block = jax.ShapeDtypeStruct((owned, 2 * rows), F32)
    normed = list(call(functools.partial(norm_kernel, columns), [block] * columns, latent[0], gain_row, flops=4 * 10**8))

    weight_flat = weight.reshape(rows * heads, channels)
    weight_other = ctx_swap(weight_flat, 1)
    weight_flat, weight_other, _ = lax.optimization_barrier((weight_flat, weight_other, normed[0]))
    size = columns * tokens * heads
    chip_weight, order = call(
        functools.partial(weight_kernel, head_count, heads, owned, columns),
        [jax.ShapeDtypeStruct((heads, channels, 2 * rows), BF16), jax.ShapeDtypeStruct((size, size), BF16)],
        weight_flat,
        weight_other,
    )

    mask = 2
    while mask < ctx_count:
        for j in range(columns):
            if j & (mask >> 1):
                normed[j] = ctx_swap(normed[j], mask | (mask == 2))
        mask *= 2
    normed = jnp.concatenate(normed, axis=0)

    sums = call(
        functools.partial(partial_kernel, head_count),
        jax.ShapeDtypeStruct((head_count * columns * owned, 2 * rows), F32),
        order,
        chip_weight,
        *far,
        own,
        other,
    )
    core = lax.axis_index("ctx") & 1
    far_other = [ctx_swap(s, 1) for s in far]
    mask = 1
    while mask < head_count:
        if mask == 2:
            sums, *far_other = lax.optimization_barrier((sums, *far_other))
        half = sums.shape[0] // 2
        count = normed.shape[0]
        if half >= count:
            got = head_swap(jnp.concatenate([sums[half:], normed], axis=0), mask)
            got_sums, got_normed = got[:half], got[half:]
        else:
            got = head_swap(jnp.concatenate([normed, sums[half:]], axis=0), mask)
            got_normed, got_sums = got[:count], got[count:]
        normed = jnp.concatenate([normed, got_normed], axis=0)
        sums = sums[:half] + got_sums
        mask *= 2

    blocks = [sums[j * owned : (j + 1) * owned] for j in range(columns)]
    mask = ctx_count // 2
    while mask > 2:
        for j in range(columns):
            if j & (mask >> 1):
                blocks[j] = ctx_swap(blocks[j], mask)
        mask //= 2
    normed_own = jnp.where(core == 0, normed[:, :rows], normed[:, rows:])
    sent = jnp.where(core == 0, normed[:, rows:], normed[:, :rows])
    count = sent.shape[0] // 2
    sent = [sent[:count], sent[count:]]
    both = ctx_swap(jnp.concatenate([jnp.concatenate(sent, axis=1)] + blocks[::2], axis=0), 1)
    normed_other = jnp.concatenate([both[:count, :rows], both[:count, rows:]], axis=0)
    for j in range(1, columns, 2):
        blocks[j] = role_swap(blocks[j], 2)

    weight_grad = call(
        functools.partial(weight_grad_kernel, head_count, heads, owned, columns),
        jax.ShapeDtypeStruct((rows * heads, channels), F32),
        normed_own,
        normed_other,
        own,
        *far,
        other,
        *far_other,
        scratch=[
            pltpu.VMEM((2, rows, columns * tokens * heads), F32),
            pltpu.VMEM((rows * heads, channels), F32),
            pltpu.SemaphoreType.DMA((4 if rows % 32 == 0 else 1,)),
        ],
        flops=2 * rows * heads * channels * ctx_count * tokens * heads,
        place=pl.ANY,
    )
    weight_grad, *blocks = lax.optimization_barrier((weight_grad, *blocks))
    latent_gradient = call(
        functools.partial(latent_kernel, head_count, columns),
        jax.ShapeDtypeStruct((owned, width), F32),
        latent[0],
        gain_row,
        both[count:],
        *blocks,
    )
    return latent_gradient[None], weight_grad.reshape(weight.shape)


def solution(mesh):
    return jax.shard_map(
        functools.partial(per_device, mesh.shape["head"], mesh.shape["ctx"]),
        mesh=mesh,
        in_specs=(
            P("ctx", "head", None),
            P(),
            P("ctx", None, "head", None),
            P("ctx", "head", None),
        ),
        out_specs=(P("ctx", "head", None), P("ctx", "head", None)),
        check_vma=False,
    )
```

```python
import functools

import jax
import jax.numpy as jnp
from jax import lax
from jax.experimental import pallas as pl
from jax.experimental.pallas import tpu as pltpu
from jax.sharding import PartitionSpec as P


F32 = jnp.float32
BF16 = jnp.bfloat16


PLANE = ((1, 1), (3, 2), (2, 0))


def iota(shape, axis):
    return lax.broadcasted_iota(jnp.int32, shape, axis)


def one_hot(condition):
    return jnp.where(condition, 1.0, 0.0).astype(BF16)


def matmul(a, b, a_axis=1, b_axis=0):
    return lax.dot_general(a, b, (((a_axis,), (b_axis,)), ((), ())), preferred_element_type=F32)


def whole(value, step):
    return value >> (step.bit_length() - 1) if step & (step - 1) == 0 else value // step


def rest(value, step):
    return value & (step - 1) if step & (step - 1) == 0 else value % step


def reverse_bits(value, count):
    out = 0
    for bit in range(count):
        out = out | (((value >> bit) & 1) << (count - 1 - bit))
    return out


def even_bits(value, count):
    out = 1 ^ (value & 1)
    for bit in range(1, count):
        out = out ^ ((value >> bit) & 1)
    return out


def weight_kernel(head_count, heads, owned, shards, own_ref, other_ref, out_ref, order_ref):
    rows = own_ref.shape[0] // heads
    group = min(rows, max(256 // heads, 1))
    size = group * heads
    to, at = iota((size, size), 0), iota((size, size), 1)
    order = one_hot(at == rest(to, group) * heads + whole(to, group))
    parts = [[] for _ in range(heads)]
    for ref in (own_ref, other_ref):
        for start in range(0, rows, group):
            moved = matmul(order, ref[pl.ds(start * heads, size), :])
            for h in range(heads):
                parts[h].append(moved[h * group : (h + 1) * group, :])
    for h in range(heads):
        out_ref[h] = jnp.concatenate(parts[h], axis=0).T.astype(BF16)
    me = lax.axis_index("head")
    bits = head_count.bit_length() - 1
    tokens = head_count * owned
    size = order_ref.shape[0]
    to, at = iota((size, size), 0), iota((size, size), 1)
    i, j = rest(to, owned), rest(whole(to, owned), shards)
    position = rest(whole(to, owned * shards), head_count)
    token = (reverse_bits(position, bits) ^ me) * owned + i
    order_ref[...] = one_hot(at == (j * tokens + token) * heads + whole(to, tokens * shards))


def partial_kernel(head_count, count, order_ref, weight_ref, *refs):
    shard_refs, (own_ref, other_ref), out_refs = refs[: -count - 2], refs[-count - 2 : -count], refs[-count:]
    core = lax.axis_index("ctx") & 1
    crossed = even_bits(lax.axis_index("head"), head_count.bit_length() - 1)
    first = jnp.where(crossed == 0, own_ref[...], other_ref[...])
    stacked = jnp.concatenate([first] + [ref[...] for ref in shard_refs], axis=0)
    moved = matmul(order_ref[...], stacked).astype(BF16)
    size, rows = out_refs[0].shape[0], out_refs[0].shape[1] // 2
    part = count * size
    total = matmul(moved[:part], weight_ref[0])
    for h in range(1, weight_ref.shape[0]):
        total += matmul(moved[h * part : (h + 1) * part], weight_ref[h])
    turned = jnp.concatenate([total[:, rows:], total[:, :rows]], axis=1)
    total = jnp.where(core == 0, total, turned)
    for n, ref in enumerate(out_refs):
        ref[...] = total[n * size : (n + 1) * size]


def norm_kernel(columns, latent_ref, gain_ref, *out_refs):
    column = lax.axis_index("ctx") >> 1
    raw = latent_ref[...].astype(F32)
    rms = lax.rsqrt(jnp.mean(raw * raw, axis=1, keepdims=True) + 1e-06)
    normed = ((raw * rms) * gain_ref[...]).astype(BF16).astype(F32)
    width = normed.shape[1] // columns
    for j, ref in enumerate(out_refs):
        block = normed[:, :width]
        for b in range(1, columns):
            block = jnp.where((column ^ j) == b, normed[:, b * width : (b + 1) * width], block)
        ref[...] = block


def weight_grad_kernel(head_count, heads, owned, columns, own_ref, other_ref, *refs):
    shard_refs, (out_ref, spread_ref, total_ref, sems) = refs[:-4], refs[-4:]
    me = lax.axis_index("head")
    core = lax.axis_index("ctx") & 1
    role = core ^ even_bits(me, head_count.bit_length() - 1)
    groups = sems.shape[0]
    rows = out_ref.shape[0] // heads // groups
    tokens = head_count * owned
    normed = jnp.concatenate([own_ref[...], other_ref[...]], axis=0).astype(BF16)
    size = columns * tokens * heads
    at, to = iota((normed.shape[0], size), 0), iota((1, size), 1)
    token, j = rest(whole(to, heads), tokens), whole(to, heads * tokens)
    distance = whole(token, owned) ^ me
    slot = distance ^ ((distance >> 1) & 1) if head_count >= 4 else distance
    turned = 1 ^ even_bits(distance, head_count.bit_length() - 1) ^ (j & 1)
    cots = []
    for side in range(2):
        held = jnp.where(j == 0, core, role) ^ side ^ core ^ turned
        place = ((held * head_count + slot) * columns + j) * owned + rest(token, owned)
        spread_ref[side] = matmul(normed, one_hot(at == place), 0, 0)
        cots.append(jnp.concatenate([r[...] for r in shard_refs[side * columns : (side + 1) * columns]], axis=0))
    keep = rest(iota((1, heads, size), 2), heads) == iota((1, heads, size), 1)
    copies = []
    for g in range(groups):
        total = None
        for side in range(2):
            block = spread_ref[side, g * rows : (g + 1) * rows, :]
            left = jnp.where(keep, block[:, None, :], 0.0).reshape(rows * heads, size).astype(BF16)
            part = matmul(left, cots[side])
            total = part if total is None else total + part
        place = pl.ds(g * rows * heads, rows * heads)
        total_ref[place, :] = total
        copies.append(pltpu.make_async_copy(total_ref.at[place], out_ref.at[place], sems.at[g]))
        copies[g].start()
    for copy in copies:
        copy.wait()


def latent_kernel(head_count, columns, latent_ref, gain_ref, other_ref, *refs):
    block_refs, out_ref = refs[:-1], refs[-1]
    column = lax.axis_index("ctx") >> 1
    crossed = even_bits(lax.axis_index("head"), head_count.bit_length() - 1)
    raw = latent_ref[...].astype(F32)
    rms = lax.rsqrt(jnp.mean(raw * raw, axis=1, keepdims=True) + 1e-06)
    hat = raw * rms
    relative = [ref[...] for ref in block_refs]
    count = raw.shape[0]
    for j in range(0, columns, 2):
        relative[j] = jnp.where(crossed == 0, relative[j], other_ref[j // 2 * count : (j // 2 + 1) * count, :])
    blocks = []
    for b in range(columns):
        block = relative[0]
        for j in range(1, columns):
            block = jnp.where((column ^ j) == b, relative[j], block)
        blocks.append(block)
    scaled = jnp.concatenate(blocks, axis=1) * gain_ref[...]
    inner = jnp.mean(scaled * hat, axis=1, keepdims=True)
    out_ref[...] = rms * (scaled - hat * inner)


def per_device(head_count, ctx_count, latent, gain, cotangent, weight):
    columns = ctx_count // 2
    owned, width = latent.shape[1:]
    _, tokens, heads, channels = cotangent.shape
    rows = weight.shape[0]
    bits = head_count.bit_length() - 1
    params = pltpu.CompilerParams(vmem_limit_bytes=48 * 1024 * 1024)

    def swap(value, partner):
        pairs = [
            (h * ctx_count + c, p * ctx_count + q)
            for h in range(head_count)
            for c in range(ctx_count)
            for p, q in [partner(h, c)]
        ]
        return lax.ppermute(value, ("head", "ctx"), pairs)

    def ctx_swap(value, mask):
        return swap(value, lambda h, c: (h, c ^ mask))

    def role_swap(value, mask):
        return swap(value, lambda h, c: (h, c ^ mask ^ even_bits(h, bits)))

    def head_swap(value, mask):
        return swap(value, lambda h, c: (h ^ mask, c ^ 1 ^ even_bits(mask, bits)))

    def call(kernel, out, *args, scratch=(), flops=0, place=pltpu.VMEM):
        moved = sum(a.size * a.dtype.itemsize for a in args)
        return pl.pallas_call(
            kernel,
            out_shape=out,
            out_specs=jax.tree.map(lambda _: pl.BlockSpec(memory_space=place), out),
            scratch_shapes=scratch,
            compiler_params=params,
            cost_estimate=pl.CostEstimate(flops=flops, bytes_accessed=moved, transcendentals=0),
        )(*args)

    own = cotangent.reshape(tokens * heads, channels)
    far = [role_swap(own, 2)]
    other = ctx_swap(own, 1)
    if columns > 2:
        first = jnp.where(even_bits(lax.axis_index("head"), bits) == 0, own, other)
        shards = [first] + far
        mask = 4
        while mask < ctx_count:
            shards += [ctx_swap(s, mask) for s in shards]
            mask *= 2
        far = shards[1:]
    gain_row = gain.reshape(1, width)
    block = jax.ShapeDtypeStruct((owned, 2 * rows), F32)
    normed = list(call(functools.partial(norm_kernel, columns), [block] * columns, latent[0], gain_row, flops=4 * 10**8))

    weight_flat = weight.reshape(rows * heads, channels)
    weight_other = ctx_swap(weight_flat, 1)
    weight_flat, weight_other, _ = lax.optimization_barrier((weight_flat, weight_other, normed[0]))
    size = columns * tokens * heads
    chip_weight, order = call(
        functools.partial(weight_kernel, head_count, heads, owned, columns),
        [jax.ShapeDtypeStruct((heads, channels, 2 * rows), BF16), jax.ShapeDtypeStruct((size, size), BF16)],
        weight_flat,
        weight_other,
    )

    mask = 2
    while mask < ctx_count:
        for j in range(columns):
            if j & (mask >> 1):
                normed[j] = ctx_swap(normed[j], mask | (mask == 2))
        mask *= 2
    normed = jnp.concatenate(normed, axis=0)

    count = 4 if head_count >= 4 else 1
    sums, *sent = call(
        functools.partial(partial_kernel, head_count, count),
        [jax.ShapeDtypeStruct((head_count * columns * owned // count, 2 * rows), F32)] * count,
        order,
        chip_weight,
        *far,
        own,
        other,
    )
    core = lax.axis_index("ctx") & 1
    far_other = [ctx_swap(s, 1) for s in far]
    mask = 1
    if count == 4:
        got = {m: head_swap(jnp.concatenate([sent[n], normed], axis=0), m) for m, n in PLANE}
        half = sums.shape[0]
        sums = sums + got[1][:half] + got[3][:half] + got[2][:half]
        sums, *far_other = lax.optimization_barrier((sums, *far_other))
        normed = jnp.concatenate([normed] + [got[m][half:] for m in (1, 3, 2)], axis=0)
        mask = 4
    while mask < head_count:
        half, count = sums.shape[0] // 2, normed.shape[0]
        if half >= count:
            got = head_swap(jnp.concatenate([sums[half:], normed], axis=0), mask)
            got_sums, got_normed = got[:half], got[half:]
        else:
            got = head_swap(jnp.concatenate([normed, sums[half:]], axis=0), mask)
            got_normed, got_sums = got[:count], got[count:]
        normed = jnp.concatenate([normed, got_normed], axis=0)
        sums = sums[:half] + got_sums
        mask *= 2

    blocks = [sums[j * owned : (j + 1) * owned] for j in range(columns)]
    mask = ctx_count // 2
    while mask > 2:
        for j in range(columns):
            if j & (mask >> 1):
                blocks[j] = ctx_swap(blocks[j], mask)
        mask //= 2
    normed_own = jnp.where(core == 0, normed[:, :rows], normed[:, rows:])
    sent = jnp.where(core == 0, normed[:, rows:], normed[:, :rows])
    count = sent.shape[0] // 2
    sent = [sent[:count], sent[count:]]
    both = ctx_swap(jnp.concatenate([jnp.concatenate(sent, axis=1)] + blocks[::2], axis=0), 1)
    normed_other = jnp.concatenate([both[:count, :rows], both[:count, rows:]], axis=0)
    for j in range(1, columns, 2):
        blocks[j] = role_swap(blocks[j], 2)

    weight_grad = call(
        functools.partial(weight_grad_kernel, head_count, heads, owned, columns),
        jax.ShapeDtypeStruct((rows * heads, channels), F32),
        normed_own,
        normed_other,
        own,
        *far,
        other,
        *far_other,
        scratch=[
            pltpu.VMEM((2, rows, columns * tokens * heads), F32),
            pltpu.VMEM((rows * heads, channels), F32),
            pltpu.SemaphoreType.DMA((4 if rows % 32 == 0 else 1,)),
        ],
        flops=2 * rows * heads * channels * ctx_count * tokens * heads,
        place=pl.ANY,
    )
    weight_grad, *blocks = lax.optimization_barrier((weight_grad, *blocks))
    latent_gradient = call(
        functools.partial(latent_kernel, head_count, columns),
        jax.ShapeDtypeStruct((owned, width), F32),
        latent[0],
        gain_row,
        both[count:],
        *blocks,
    )
    return latent_gradient[None], weight_grad.reshape(weight.shape)


def solution(mesh):
    return jax.shard_map(
        functools.partial(per_device, mesh.shape["head"], mesh.shape["ctx"]),
        mesh=mesh,
        in_specs=(
            P("ctx", "head", None),
            P(),
            P("ctx", None, "head", None),
            P("ctx", "head", None),
        ),
        out_specs=(P("ctx", "head", None), P("ctx", "head", None)),
        check_vma=False,
    )
```

```python
import functools

import jax
import jax.numpy as jnp
from jax import lax
from jax.experimental import pallas as pl
from jax.experimental.pallas import tpu as pltpu
from jax.sharding import PartitionSpec as P


F32 = jnp.float32
BF16 = jnp.bfloat16


PLANE = ((1, 1), (3, 2), (2, 0))


def iota(shape, axis):
    return lax.broadcasted_iota(jnp.int32, shape, axis)


def one_hot(condition):
    return jnp.where(condition, 1.0, 0.0).astype(BF16)


def matmul(a, b, a_axis=1, b_axis=0):
    return lax.dot_general(a, b, (((a_axis,), (b_axis,)), ((), ())), preferred_element_type=F32)


def whole(value, step):
    return value >> (step.bit_length() - 1) if step & (step - 1) == 0 else value // step


def rest(value, step):
    return value & (step - 1) if step & (step - 1) == 0 else value % step


def reverse_bits(value, count):
    out = 0
    for bit in range(count):
        out = out | (((value >> bit) & 1) << (count - 1 - bit))
    return out


def two_terms(value):
    high = lax.reduce_precision(value, 8, 7)
    return [high.astype(BF16), (value - high).astype(BF16)]


def even_bits(value, count):
    out = 1 ^ (value & 1)
    for bit in range(1, count):
        out = out ^ ((value >> bit) & 1)
    return out


def weight_kernel(head_count, heads, owned, shards, own_ref, other_ref, out_ref, order_ref):
    rows = own_ref.shape[0] // heads
    group = min(rows, max(256 // heads, 1))
    size = group * heads
    to, at = iota((size, size), 0), iota((size, size), 1)
    order = one_hot(at == rest(to, group) * heads + whole(to, group))
    parts = [[] for _ in range(heads)]
    for ref in (own_ref, other_ref):
        for start in range(0, rows, group):
            moved = matmul(order, ref[pl.ds(start * heads, size), :])
            for h in range(heads):
                parts[h].append(moved[h * group : (h + 1) * group, :])
    for h in range(heads):
        out_ref[h] = jnp.concatenate(parts[h], axis=0).T.astype(BF16)
    me = lax.axis_index("head")
    bits = head_count.bit_length() - 1
    tokens = head_count * owned
    size = order_ref.shape[0]
    to, at = iota((size, size), 0), iota((size, size), 1)
    i, j = rest(to, owned), rest(whole(to, owned), shards)
    position = rest(whole(to, owned * shards), head_count)
    token = (reverse_bits(position, bits) ^ me) * owned + i
    order_ref[...] = one_hot(at == (j * tokens + token) * heads + whole(to, tokens * shards))


def partial_kernel(head_count, count, order_ref, weight_ref, *refs):
    shard_refs, (own_ref, other_ref), out_refs = refs[: -count - 2], refs[-count - 2 : -count], refs[-count:]
    core = lax.axis_index("ctx") & 1
    crossed = even_bits(lax.axis_index("head"), head_count.bit_length() - 1)
    first = jnp.where(crossed == 0, own_ref[...], other_ref[...])
    stacked = jnp.concatenate([first] + [ref[...] for ref in shard_refs], axis=0)
    moved = matmul(order_ref[...], stacked).astype(BF16)
    size, rows = out_refs[0].shape[0], out_refs[0].shape[1] // 2
    part = count * size
    total = matmul(moved[:part], weight_ref[0])
    for h in range(1, weight_ref.shape[0]):
        total += matmul(moved[h * part : (h + 1) * part], weight_ref[h])
    turned = jnp.concatenate([total[:, rows:], total[:, :rows]], axis=1)
    total = jnp.where(core == 0, total, turned)
    for n, ref in enumerate(out_refs):
        ref[...] = total[n * size : (n + 1) * size]


def norm_kernel(columns, latent_ref, gain_ref, *out_refs):
    column = lax.axis_index("ctx") >> 1
    raw = latent_ref[...].astype(F32)
    rms = lax.rsqrt(jnp.mean(raw * raw, axis=1, keepdims=True) + 1e-06)
    normed = ((raw * rms) * gain_ref[...]).astype(BF16)
    width = normed.shape[1] // columns
    for j, ref in enumerate(out_refs):
        block = normed[:, :width]
        for b in range(1, columns):
            block = jnp.where((column ^ j) == b, normed[:, b * width : (b + 1) * width], block)
        ref[...] = block


def weight_grad_kernel(head_count, heads, owned, columns, own_ref, other_ref, *refs):
    shard_refs, (out_ref, spread_ref, total_ref, sems) = refs[:-4], refs[-4:]
    me = lax.axis_index("head")
    core = lax.axis_index("ctx") & 1
    role = core ^ even_bits(me, head_count.bit_length() - 1)
    groups = sems.shape[0]
    rows = out_ref.shape[0] // heads // groups
    tokens = head_count * owned
    normed = jnp.concatenate([own_ref[...], other_ref[...]], axis=0).astype(BF16)
    size = columns * tokens * heads
    at, to = iota((normed.shape[0], size), 0), iota((1, size), 1)
    token, j = rest(whole(to, heads), tokens), whole(to, heads * tokens)
    distance = whole(token, owned) ^ me
    slot = distance ^ ((distance >> 1) & 1) if head_count >= 4 else distance
    turned = 1 ^ even_bits(distance, head_count.bit_length() - 1) ^ (j & 1)
    cots = []
    for side in range(2):
        held = jnp.where(j == 0, core, role) ^ side ^ core ^ turned
        place = ((held * head_count + slot) * columns + j) * owned + rest(token, owned)
        spread_ref[side] = matmul(normed, one_hot(at == place), 0, 0)
        cots.append(jnp.concatenate([r[...] for r in shard_refs[side * columns : (side + 1) * columns]], axis=0))
    keep = rest(iota((1, heads, size), 2), heads) == iota((1, heads, size), 1)
    copies = []
    for g in range(groups):
        total = None
        for side in range(2):
            block = spread_ref[side, g * rows : (g + 1) * rows, :]
            left = jnp.where(keep, block[:, None, :], 0.0).reshape(rows * heads, size).astype(BF16)
            part = matmul(left, cots[side])
            total = part if total is None else total + part
        place = pl.ds(g * rows * heads, rows * heads)
        total_ref[place, :] = total
        copies.append(pltpu.make_async_copy(total_ref.at[place], out_ref.at[place], sems.at[g]))
        copies[g].start()
    for copy in copies:
        copy.wait()


def latent_kernel(head_count, columns, latent_ref, gain_ref, other_ref, *refs):
    block_refs, out_ref = refs[:-1], refs[-1]
    column = lax.axis_index("ctx") >> 1
    crossed = even_bits(lax.axis_index("head"), head_count.bit_length() - 1)
    raw = latent_ref[...].astype(F32)
    rms = lax.rsqrt(jnp.mean(raw * raw, axis=1, keepdims=True) + 1e-06)
    hat = raw * rms
    relative = [ref[...] for ref in block_refs]
    count = raw.shape[0]
    for j in range(0, columns, 2):
        relative[j] = jnp.where(crossed == 0, relative[j], other_ref[j // 2 * count : (j // 2 + 1) * count, :])
    blocks = []
    for b in range(columns):
        block = relative[0]
        for j in range(1, columns):
            block = jnp.where((column ^ j) == b, relative[j], block)
        blocks.append(block)
    scaled = jnp.concatenate(blocks, axis=1) * gain_ref[...]
    inner = jnp.mean(scaled * hat, axis=1, keepdims=True)
    out_ref[...] = rms * (scaled - hat * inner)


def per_device(head_count, ctx_count, latent, gain, cotangent, weight):
    columns = ctx_count // 2
    owned, width = latent.shape[1:]
    _, tokens, heads, channels = cotangent.shape
    rows = weight.shape[0]
    bits = head_count.bit_length() - 1
    params = pltpu.CompilerParams(vmem_limit_bytes=48 * 1024 * 1024)

    def swap(value, partner):
        pairs = [
            (h * ctx_count + c, p * ctx_count + q)
            for h in range(head_count)
            for c in range(ctx_count)
            for p, q in [partner(h, c)]
        ]
        return lax.ppermute(value, ("head", "ctx"), pairs)

    def ctx_swap(value, mask):
        return swap(value, lambda h, c: (h, c ^ mask))

    def role_swap(value, mask):
        return swap(value, lambda h, c: (h, c ^ mask ^ even_bits(h, bits)))

    def head_swap(value, mask):
        return swap(value, lambda h, c: (h ^ mask, c ^ 1 ^ even_bits(mask, bits)))

    def call(kernel, out, *args, scratch=(), flops=0, place=pltpu.VMEM):
        moved = sum(a.size * a.dtype.itemsize for a in args)
        return pl.pallas_call(
            kernel,
            out_shape=out,
            out_specs=jax.tree.map(lambda _: pl.BlockSpec(memory_space=place), out),
            scratch_shapes=scratch,
            compiler_params=params,
            cost_estimate=pl.CostEstimate(flops=flops, bytes_accessed=moved, transcendentals=0),
        )(*args)

    own = cotangent.reshape(tokens * heads, channels)
    far = [role_swap(own, 2)]
    other = ctx_swap(own, 1)
    if columns > 2:
        first = jnp.where(even_bits(lax.axis_index("head"), bits) == 0, own, other)
        shards = [first] + far
        mask = 4
        while mask < ctx_count:
            shards += [ctx_swap(s, mask) for s in shards]
            mask *= 2
        far = shards[1:]
    gain_row = gain.reshape(1, width)
    block = jax.ShapeDtypeStruct((owned, 2 * rows), BF16)
    normed = list(call(functools.partial(norm_kernel, columns), [block] * columns, latent[0], gain_row, flops=4 * 10**8))

    weight_flat = weight.reshape(rows * heads, channels)
    weight_other = ctx_swap(weight_flat, 1)
    weight_flat, weight_other, _ = lax.optimization_barrier((weight_flat, weight_other, normed[0]))
    size = columns * tokens * heads
    chip_weight, order = call(
        functools.partial(weight_kernel, head_count, heads, owned, columns),
        [jax.ShapeDtypeStruct((heads, channels, 2 * rows), BF16), jax.ShapeDtypeStruct((size, size), BF16)],
        weight_flat,
        weight_other,
    )

    mask = 2
    while mask < ctx_count:
        for j in range(columns):
            if j & (mask >> 1):
                normed[j] = ctx_swap(normed[j], mask | (mask == 2))
        mask *= 2
    normed = jnp.concatenate(normed, axis=0)

    count = 4 if head_count >= 4 else 1
    sums, *sent = call(
        functools.partial(partial_kernel, head_count, count),
        [jax.ShapeDtypeStruct((head_count * columns * owned // count, 2 * rows), F32)] * count,
        order,
        chip_weight,
        *far,
        own,
        other,
    )
    core = lax.axis_index("ctx") & 1
    far_other = [ctx_swap(s, 1) for s in far]
    mask = 1
    if count == 4:
        got = {m: head_swap(jnp.concatenate(two_terms(sent[n]) + [normed], axis=0), m) for m, n in PLANE}
        half = sums.shape[0]
        for m in (1, 3, 2):
            sums = sums + (got[m][:half].astype(F32) + got[m][half : 2 * half].astype(F32))
        sums, *far_other = lax.optimization_barrier((sums, *far_other))
        normed = jnp.concatenate([normed] + [got[m][2 * half :] for m in (1, 3, 2)], axis=0)
        mask = 4
    while mask < head_count:
        half, count = sums.shape[0] // 2, normed.shape[0]
        got = head_swap(jnp.concatenate([normed] + two_terms(sums[half:]), axis=0), mask)
        normed = jnp.concatenate([normed, got[:count]], axis=0)
        got = got[count:].astype(F32)
        sums = sums[:half] + (got[:half] + got[half:])
        mask *= 2

    blocks = [sums[j * owned : (j + 1) * owned] for j in range(columns)]
    mask = ctx_count // 2
    while mask > 2:
        for j in range(columns):
            if j & (mask >> 1):
                blocks[j] = ctx_swap(blocks[j], mask)
        mask //= 2
    normed_own = jnp.where(core == 0, normed[:, :rows], normed[:, rows:])
    sent = jnp.where(core == 0, normed[:, rows:], normed[:, :rows])
    count = sent.shape[0] // 2
    sent = [sent[:count], sent[count:]]
    both = ctx_swap(jnp.concatenate([jnp.concatenate(sent, axis=1)] + blocks[::2], axis=0), 1)
    normed_other = jnp.concatenate([both[:count, :rows], both[:count, rows:]], axis=0)
    for j in range(1, columns, 2):
        blocks[j] = role_swap(blocks[j], 2)

    weight_grad = call(
        functools.partial(weight_grad_kernel, head_count, heads, owned, columns),
        jax.ShapeDtypeStruct((rows * heads, channels), F32),
        normed_own,
        normed_other,
        own,
        *far,
        other,
        *far_other,
        scratch=[
            pltpu.VMEM((2, rows, columns * tokens * heads), F32),
            pltpu.VMEM((rows * heads, channels), F32),
            pltpu.SemaphoreType.DMA((4 if rows % 32 == 0 else 1,)),
        ],
        flops=2 * rows * heads * channels * ctx_count * tokens * heads,
        place=pl.ANY,
    )
    weight_grad, *blocks = lax.optimization_barrier((weight_grad, *blocks))
    latent_gradient = call(
        functools.partial(latent_kernel, head_count, columns),
        jax.ShapeDtypeStruct((owned, width), F32),
        latent[0],
        gain_row,
        both[count:],
        *blocks,
    )
    return latent_gradient[None], weight_grad.reshape(weight.shape)


def solution(mesh):
    return jax.shard_map(
        functools.partial(per_device, mesh.shape["head"], mesh.shape["ctx"]),
        mesh=mesh,
        in_specs=(
            P("ctx", "head", None),
            P(),
            P("ctx", None, "head", None),
            P("ctx", "head", None),
        ),
        out_specs=(P("ctx", "head", None), P("ctx", "head", None)),
        check_vma=False,
    )
```

```python
import functools

import jax
import jax.numpy as jnp
from jax import lax
from jax.experimental import pallas as pl
from jax.experimental.pallas import tpu as pltpu
from jax.sharding import PartitionSpec as P


F32 = jnp.float32
BF16 = jnp.bfloat16


PLANE = ((1, 1), (3, 2), (2, 0))


def iota(shape, axis):
    return lax.broadcasted_iota(jnp.int32, shape, axis)


def one_hot(condition):
    return jnp.where(condition, 1.0, 0.0).astype(BF16)


def matmul(a, b, a_axis=1, b_axis=0):
    return lax.dot_general(a, b, (((a_axis,), (b_axis,)), ((), ())), preferred_element_type=F32)


def whole(value, step):
    return value >> (step.bit_length() - 1) if step & (step - 1) == 0 else value // step


def rest(value, step):
    return value & (step - 1) if step & (step - 1) == 0 else value % step


def reverse_bits(value, count):
    out = 0
    for bit in range(count):
        out = out | (((value >> bit) & 1) << (count - 1 - bit))
    return out


def two_terms(value):
    high = value.astype(BF16).astype(F32)
    return jnp.concatenate([high, (value - high).astype(BF16).astype(F32)], axis=0)


def even_bits(value, count):
    out = 1 ^ (value & 1)
    for bit in range(1, count):
        out = out ^ ((value >> bit) & 1)
    return out


def weight_kernel(head_count, heads, owned, shards, own_ref, other_ref, out_ref, order_ref):
    rows = own_ref.shape[0] // heads
    group = min(rows, max(256 // heads, 1))
    size = group * heads
    to, at = iota((size, size), 0), iota((size, size), 1)
    order = one_hot(at == rest(to, group) * heads + whole(to, group))
    parts = [[] for _ in range(heads)]
    for ref in (own_ref, other_ref):
        for start in range(0, rows, group):
            moved = matmul(order, ref[pl.ds(start * heads, size), :])
            for h in range(heads):
                parts[h].append(moved[h * group : (h + 1) * group, :])
    for h in range(heads):
        out_ref[h] = jnp.concatenate(parts[h], axis=0).T.astype(BF16)
    me = lax.axis_index("head")
    bits = head_count.bit_length() - 1
    tokens = head_count * owned
    size = order_ref.shape[0]
    to, at = iota((size, size), 0), iota((size, size), 1)
    i, j = rest(to, owned), rest(whole(to, owned), shards)
    position = rest(whole(to, owned * shards), head_count)
    token = (reverse_bits(position, bits) ^ me) * owned + i
    order_ref[...] = one_hot(at == (j * tokens + token) * heads + whole(to, tokens * shards))


def partial_kernel(head_count, count, order_ref, weight_ref, *refs):
    shard_refs, (own_ref, other_ref), out_refs = refs[: -count - 2], refs[-count - 2 : -count], refs[-count:]
    core = lax.axis_index("ctx") & 1
    crossed = even_bits(lax.axis_index("head"), head_count.bit_length() - 1)
    first = jnp.where(crossed == 0, own_ref[...], other_ref[...])
    stacked = jnp.concatenate([first] + [ref[...] for ref in shard_refs], axis=0)
    moved = matmul(order_ref[...], stacked).astype(BF16)
    size, rows = out_refs[0].shape[0], out_refs[0].shape[1] // 2
    part = count * size
    total = matmul(moved[:part], weight_ref[0])
    for h in range(1, weight_ref.shape[0]):
        total += matmul(moved[h * part : (h + 1) * part], weight_ref[h])
    turned = jnp.concatenate([total[:, rows:], total[:, :rows]], axis=1)
    total = jnp.where(core == 0, total, turned)
    out_refs[0][...] = total[:size]
    for n, ref in enumerate(out_refs[1:]):
        ref[...] = two_terms(total[(n + 1) * size : (n + 2) * size]).astype(BF16)


def merge_kernel(skip, sums_ref, normed_ref, *refs):
    got_refs, keep_ref, message_ref = refs[:-2], refs[-2], refs[-1]
    total, rows = merged(skip, sums_ref, normed_ref, got_refs)
    half = keep_ref.shape[0]
    keep_ref[...] = total[:half]
    message_ref[...] = jnp.concatenate([two_terms(total[half:]), rows], axis=0).astype(BF16)


def last_merge_kernel(skip, columns, sums_ref, normed_ref, *refs):
    got_refs, block_refs, own_ref, sent_ref = refs[: -columns - 2], refs[-columns - 2 : -2], refs[-2], refs[-1]
    total, rows = merged(skip, sums_ref, normed_ref, got_refs)
    owned = total.shape[0] // columns
    for j, ref in enumerate(block_refs):
        ref[...] = total[j * owned : (j + 1) * owned]
    core = lax.axis_index("ctx") & 1
    count, width = rows.shape[0] // 2, rows.shape[1] // 2
    own_ref[...] = jnp.where(core == 0, rows[:, :width], rows[:, width:])
    sent = jnp.where(core == 0, rows[:, width:], rows[:, :width])
    sent = jnp.concatenate([sent[:count], sent[count:]], axis=1)
    sent_ref[...] = jnp.concatenate([sent, total[:owned]], axis=0) if columns == 2 else sent


def merged(skip, sums_ref, normed_ref, got_refs):
    total, half = sums_ref[...], sums_ref.shape[0]
    rows = [normed_ref[...].astype(F32)[skip:]]
    for ref in got_refs:
        got = ref[...].astype(F32)
        total = total + (got[:half] + got[half : 2 * half])
        rows.append(got[2 * half :])
    return total, jnp.concatenate(rows, axis=0)


def norm_kernel(columns, latent_ref, gain_ref, rms_ref, hat_ref, *out_refs):
    column = lax.axis_index("ctx") >> 1
    raw = latent_ref[...].astype(F32)
    rms = lax.rsqrt(jnp.mean(raw * raw, axis=1, keepdims=True) + 1e-06)
    hat = raw * rms
    rms_ref[...] = jnp.broadcast_to(rms, raw.shape)
    hat_ref[...] = hat
    normed = (hat * gain_ref[...]).astype(BF16)
    width = normed.shape[1] // columns
    for j, ref in enumerate(out_refs):
        block = normed[:, :width]
        for b in range(1, columns):
            block = jnp.where((column ^ j) == b, normed[:, b * width : (b + 1) * width], block)
        ref[...] = block


def weight_grad_kernel(head_count, heads, owned, columns, own_ref, other_ref, *refs):
    shard_refs, (out_ref, spread_ref, total_ref, sems) = refs[:-4], refs[-4:]
    me = lax.axis_index("head")
    core = lax.axis_index("ctx") & 1
    role = core ^ even_bits(me, head_count.bit_length() - 1)
    groups = sems.shape[0]
    rows = out_ref.shape[0] // heads // groups
    tokens = head_count * owned
    count, width = own_ref.shape[0] // 2, own_ref.shape[1]
    other = other_ref[...]
    normed = jnp.concatenate([own_ref[...], other[:count, :width], other[:count, width:]], axis=0).astype(BF16)
    size = columns * tokens * heads
    at, to = iota((normed.shape[0], size), 0), iota((1, size), 1)
    token, j = rest(whole(to, heads), tokens), whole(to, heads * tokens)
    distance = whole(token, owned) ^ me
    slot = distance ^ ((distance >> 1) & 1) if head_count >= 4 else distance
    turned = 1 ^ even_bits(distance, head_count.bit_length() - 1) ^ (j & 1)
    cots = []
    for side in range(2):
        held = jnp.where(j == 0, core, role) ^ side ^ core ^ turned
        place = ((held * head_count + slot) * columns + j) * owned + rest(token, owned)
        spread_ref[side] = matmul(normed, one_hot(at == place), 0, 0)
        cots.append(jnp.concatenate([r[...] for r in shard_refs[side * columns : (side + 1) * columns]], axis=0))
    keep = rest(iota((1, heads, size), 2), heads) == iota((1, heads, size), 1)
    copies = []
    for g in range(groups):
        total = None
        for side in range(2):
            block = spread_ref[side, g * rows : (g + 1) * rows, :]
            left = jnp.where(keep, block[:, None, :], 0.0).reshape(rows * heads, size).astype(BF16)
            part = matmul(left, cots[side])
            total = part if total is None else total + part
        place = pl.ds(g * rows * heads, rows * heads)
        total_ref[place, :] = total
        copies.append(pltpu.make_async_copy(total_ref.at[place], out_ref.at[place], sems.at[g]))
        copies[g].start()
    for copy in copies:
        copy.wait()


def latent_kernel(head_count, columns, rms_ref, hat_ref, gain_ref, other_ref, *refs):
    block_refs, out_ref = refs[:-1], refs[-1]
    column = lax.axis_index("ctx") >> 1
    crossed = even_bits(lax.axis_index("head"), head_count.bit_length() - 1)
    relative = [ref[...] for ref in block_refs]
    count = out_ref.shape[0]
    first = other_ref.shape[0] - count * columns // 2
    for j in range(0, columns, 2):
        place = first + j // 2 * count
        relative[j] = jnp.where(crossed == 0, relative[j], other_ref[place : place + count, :])
    blocks = []
    for b in range(columns):
        block = relative[0]
        for j in range(1, columns):
            block = jnp.where((column ^ j) == b, relative[j], block)
        blocks.append(block)
    scaled = jnp.concatenate(blocks, axis=1) * gain_ref[...]
    hat = hat_ref[...]
    inner = jnp.mean(scaled * hat, axis=1, keepdims=True)
    out_ref[...] = rms_ref[...] * (scaled - hat * inner)


def per_device(head_count, ctx_count, latent, gain, cotangent, weight):
    columns = ctx_count // 2
    owned, width = latent.shape[1:]
    _, tokens, heads, channels = cotangent.shape
    rows = weight.shape[0]
    bits = head_count.bit_length() - 1
    params = pltpu.CompilerParams(vmem_limit_bytes=48 * 1024 * 1024)

    def swap(value, partner):
        pairs = [
            (h * ctx_count + c, p * ctx_count + q)
            for h in range(head_count)
            for c in range(ctx_count)
            for p, q in [partner(h, c)]
        ]
        return lax.ppermute(value, ("head", "ctx"), pairs)

    def ctx_swap(value, mask):
        return swap(value, lambda h, c: (h, c ^ mask))

    def role_swap(value, mask):
        return swap(value, lambda h, c: (h, c ^ mask ^ even_bits(h, bits)))

    def head_swap(value, mask):
        return swap(value, lambda h, c: (h ^ mask, c ^ 1 ^ even_bits(mask, bits)))

    def call(kernel, out, *args, scratch=(), flops=0, place=pltpu.VMEM):
        moved = sum(a.size * a.dtype.itemsize for a in args)
        return pl.pallas_call(
            kernel,
            out_shape=out,
            out_specs=jax.tree.map(lambda _: pl.BlockSpec(memory_space=place), out),
            scratch_shapes=scratch,
            compiler_params=params,
            cost_estimate=pl.CostEstimate(flops=flops, bytes_accessed=moved, transcendentals=0),
        )(*args)

    own = cotangent.reshape(tokens * heads, channels)
    far = [role_swap(own, 2)]
    other = ctx_swap(own, 1)
    if columns > 2:
        first = jnp.where(even_bits(lax.axis_index("head"), bits) == 0, own, other)
        shards = [first] + far
        mask = 4
        while mask < ctx_count:
            shards += [ctx_swap(s, mask) for s in shards]
            mask *= 2
        far = shards[1:]
    gain_row = gain.reshape(1, width)
    block = jax.ShapeDtypeStruct((owned, 2 * rows), BF16)
    row = jax.ShapeDtypeStruct((owned, width), F32)
    rms, hat, *normed = call(
        functools.partial(norm_kernel, columns), [row] * 2 + [block] * columns, latent[0], gain_row, flops=4 * 10**8
    )

    weight_flat = weight.reshape(rows * heads, channels)
    weight_other = ctx_swap(weight_flat, 1)
    weight_flat, weight_other, _ = lax.optimization_barrier((weight_flat, weight_other, normed[0]))
    size = columns * tokens * heads
    chip_weight, order = call(
        functools.partial(weight_kernel, head_count, heads, owned, columns),
        [jax.ShapeDtypeStruct((heads, channels, 2 * rows), BF16), jax.ShapeDtypeStruct((size, size), BF16)],
        weight_flat,
        weight_other,
    )

    mask = 2
    while mask < ctx_count:
        for j in range(columns):
            if j & (mask >> 1):
                normed[j] = ctx_swap(normed[j], mask | (mask == 2))
        mask *= 2
    normed = jnp.concatenate(normed, axis=0)

    size = head_count * columns * owned // 4
    sums, *sent = call(
        functools.partial(partial_kernel, head_count, 4),
        [jax.ShapeDtypeStruct((size, 2 * rows), F32)] + [jax.ShapeDtypeStruct((2 * size, 2 * rows), BF16)] * 3,
        order,
        chip_weight,
        *far,
        own,
        other,
    )
    sums, *far = lax.optimization_barrier((sums, *far))
    far_other = [ctx_swap(s, 1) for s in far]
    got = {m: head_swap(jnp.concatenate([sent[n], normed], axis=0), m) for m, n in PLANE}
    got = [got[m] for m in (1, 3, 2)]
    skip, count, mask = 0, 4 * normed.shape[0], 4
    while mask < head_count:
        half = sums.shape[0] // 2
        sums, normed = call(
            functools.partial(merge_kernel, skip),
            [jax.ShapeDtypeStruct((half, 2 * rows), F32), jax.ShapeDtypeStruct((2 * half + count, 2 * rows), BF16)],
            sums,
            normed,
            *got,
        )
        if mask == 4:
            normed, *far_other = lax.optimization_barrier((normed, *far_other))
        got = [head_swap(normed, mask)]
        skip, count, mask = 2 * half, 2 * count, 2 * mask
    short = jax.ShapeDtypeStruct((owned, 2 * rows), F32)
    kept = owned if columns == 2 else 0
    *blocks, normed_own, sent = call(
        functools.partial(last_merge_kernel, skip, columns),
        [short] * columns
        + [jax.ShapeDtypeStruct((count, rows), F32), jax.ShapeDtypeStruct((count // 2 + kept, 2 * rows), F32)],
        sums,
        normed,
        *got,
    )
    mask = ctx_count // 2
    while mask > 2:
        for j in range(columns):
            if j & (mask >> 1):
                blocks[j] = ctx_swap(blocks[j], mask)
        mask //= 2
    if columns > 2:
        sent = jnp.concatenate([sent] + blocks[::2], axis=0)
    both = ctx_swap(sent, 1)
    for j in range(1, columns, 2):
        blocks[j] = role_swap(blocks[j], 2)

    weight_grad = call(
        functools.partial(weight_grad_kernel, head_count, heads, owned, columns),
        jax.ShapeDtypeStruct((rows * heads, channels), F32),
        normed_own,
        both,
        own,
        *far,
        other,
        *far_other,
        scratch=[
            pltpu.VMEM((2, rows, columns * tokens * heads), F32),
            pltpu.VMEM((rows * heads, channels), F32),
            pltpu.SemaphoreType.DMA((4 if rows % 32 == 0 else 1,)),
        ],
        flops=2 * rows * heads * channels * ctx_count * tokens * heads,
        place=pl.ANY,
    )
    weight_grad, *blocks = lax.optimization_barrier((weight_grad, *blocks))
    latent_gradient = call(
        functools.partial(latent_kernel, head_count, columns),
        jax.ShapeDtypeStruct((owned, width), F32),
        rms,
        hat,
        gain_row,
        both,
        *blocks,
    )
    return latent_gradient[None], weight_grad.reshape(weight.shape)


def solution(mesh):
    return jax.shard_map(
        functools.partial(per_device, mesh.shape["head"], mesh.shape["ctx"]),
        mesh=mesh,
        in_specs=(
            P("ctx", "head", None),
            P(),
            P("ctx", None, "head", None),
            P("ctx", "head", None),
        ),
        out_specs=(P("ctx", "head", None), P("ctx", "head", None)),
        check_vma=False,
    )
```

```python
import functools

import jax
import jax.numpy as jnp
from jax import lax
from jax.experimental import pallas as pl
from jax.experimental.pallas import tpu as pltpu
from jax.sharding import PartitionSpec as P


F32 = jnp.float32
BF16 = jnp.bfloat16


PLANE = ((1, 1), (3, 2), (2, 0))


def iota(shape, axis):
    return lax.broadcasted_iota(jnp.int32, shape, axis)


def one_hot(condition):
    return jnp.where(condition, 1.0, 0.0).astype(BF16)


def matmul(a, b, a_axis=1, b_axis=0):
    return lax.dot_general(a, b, (((a_axis,), (b_axis,)), ((), ())), preferred_element_type=F32)


def whole(value, step):
    return value >> (step.bit_length() - 1) if step & (step - 1) == 0 else value // step


def rest(value, step):
    return value & (step - 1) if step & (step - 1) == 0 else value % step


def reverse_bits(value, count):
    out = 0
    for bit in range(count):
        out = out | (((value >> bit) & 1) << (count - 1 - bit))
    return out


def two_terms(value):
    high = value.astype(BF16).astype(F32)
    return jnp.concatenate([high, (value - high).astype(BF16).astype(F32)], axis=0)


def even_bits(value, count):
    out = 1 ^ (value & 1)
    for bit in range(1, count):
        out = out ^ ((value >> bit) & 1)
    return out


def crossing(head, column, bits):
    return even_bits(head, bits) ^ (column & 1) ^ 1


def weight_kernel(head_count, heads, owned, shards, own_ref, other_ref, out_ref, order_ref):
    rows = own_ref.shape[0] // heads
    group = min(rows, max(256 // heads, 1))
    size = group * heads
    to, at = iota((size, size), 0), iota((size, size), 1)
    order = one_hot(at == rest(to, group) * heads + whole(to, group))
    parts = [[] for _ in range(heads)]
    for ref in (own_ref, other_ref):
        for start in range(0, rows, group):
            moved = matmul(order, ref[pl.ds(start * heads, size), :])
            for h in range(heads):
                parts[h].append(moved[h * group : (h + 1) * group, :])
    for h in range(heads):
        out_ref[h] = jnp.concatenate(parts[h], axis=0).T.astype(BF16)
    me = lax.axis_index("head")
    bits = head_count.bit_length() - 1
    tokens = head_count * owned
    size = order_ref.shape[0]
    to, at = iota((size, size), 0), iota((size, size), 1)
    i, j = rest(to, owned), rest(whole(to, owned), shards)
    position = rest(whole(to, owned * shards), head_count)
    token = (reverse_bits(position, bits) ^ me) * owned + i
    order_ref[...] = one_hot(at == (j * tokens + token) * heads + whole(to, tokens * shards))


def partial_kernel(head_count, count, order_ref, weight_ref, *refs):
    shard_refs, (own_ref, other_ref), out_refs = refs[: -count - 2], refs[-count - 2 : -count], refs[-count:]
    core = lax.axis_index("ctx") & 1
    crossed = crossing(lax.axis_index("head"), lax.axis_index("ctx") >> 1, head_count.bit_length() - 1)
    first = jnp.where(crossed == 0, own_ref[...], other_ref[...])
    stacked = jnp.concatenate([first] + [ref[...] for ref in shard_refs], axis=0)
    moved = matmul(order_ref[...], stacked).astype(BF16)
    size, rows = out_refs[0].shape[0], out_refs[0].shape[1] // 2
    part = count * size
    total = matmul(moved[:part], weight_ref[0])
    for h in range(1, weight_ref.shape[0]):
        total += matmul(moved[h * part : (h + 1) * part], weight_ref[h])
    turned = jnp.concatenate([total[:, rows:], total[:, :rows]], axis=1)
    total = jnp.where(core == 0, total, turned)
    out_refs[0][...] = total[:size]
    for n, ref in enumerate(out_refs[1:]):
        ref[...] = two_terms(total[(n + 1) * size : (n + 2) * size]).astype(BF16)


def merge_kernel(skip, sums_ref, normed_ref, *refs):
    got_refs, keep_ref, message_ref = refs[:-2], refs[-2], refs[-1]
    total, rows = merged(skip, sums_ref, normed_ref, got_refs)
    half = keep_ref.shape[0]
    keep_ref[...] = total[:half]
    message_ref[...] = jnp.concatenate([two_terms(total[half:]), rows], axis=0).astype(BF16)


def last_merge_kernel(skip, columns, sums_ref, normed_ref, *refs):
    got_refs, block_refs, own_ref, sent_ref = refs[: -columns - 2], refs[-columns - 2 : -2], refs[-2], refs[-1]
    total, rows = merged(skip, sums_ref, normed_ref, got_refs)
    owned = total.shape[0] // columns
    for j, ref in enumerate(block_refs):
        ref[...] = total[j * owned : (j + 1) * owned]
    core = lax.axis_index("ctx") & 1
    count, width = rows.shape[0] // 2, rows.shape[1] // 2
    own_ref[...] = jnp.where(core == 0, rows[:, :width], rows[:, width:])
    sent = jnp.where(core == 0, rows[:, width:], rows[:, :width])
    sent = jnp.concatenate([sent[:count], sent[count:]], axis=1)
    sent_ref[...] = jnp.concatenate([sent, total[:owned]], axis=0) if columns == 2 else sent


def merged(skip, sums_ref, normed_ref, got_refs):
    total, half = sums_ref[...], sums_ref.shape[0]
    rows = [normed_ref[...].astype(F32)[skip:]]
    for ref in got_refs:
        got = ref[...].astype(F32)
        total = total + (got[:half] + got[half : 2 * half])
        rows.append(got[2 * half :])
    return total, jnp.concatenate(rows, axis=0)


def norm_kernel(columns, latent_ref, gain_ref, rms_ref, hat_ref, *out_refs):
    column = lax.axis_index("ctx") >> 1
    raw = latent_ref[...].astype(F32)
    rms = lax.rsqrt(jnp.mean(raw * raw, axis=1, keepdims=True) + 1e-06)
    hat = raw * rms
    rms_ref[...] = jnp.broadcast_to(rms, raw.shape)
    hat_ref[...] = hat
    normed = (hat * gain_ref[...]).astype(BF16)
    width = normed.shape[1] // columns
    for j, ref in enumerate(out_refs):
        block = normed[:, :width]
        for b in range(1, columns):
            block = jnp.where((column ^ j) == b, normed[:, b * width : (b + 1) * width], block)
        ref[...] = block


def weight_grad_kernel(head_count, heads, owned, columns, own_ref, other_ref, *refs):
    shard_refs, (out_ref, spread_ref, total_ref, sems) = refs[:-4], refs[-4:]
    me = lax.axis_index("head")
    core = lax.axis_index("ctx") & 1
    role = core ^ crossing(me, lax.axis_index("ctx") >> 1, head_count.bit_length() - 1)
    groups = sems.shape[0]
    rows = out_ref.shape[0] // heads // groups
    tokens = head_count * owned
    count, width = own_ref.shape[0] // 2, own_ref.shape[1]
    other = other_ref[...]
    normed = jnp.concatenate([own_ref[...], other[:count, :width], other[:count, width:]], axis=0).astype(BF16)
    size = columns * tokens * heads
    at, to = iota((normed.shape[0], size), 0), iota((1, size), 1)
    token, j = rest(whole(to, heads), tokens), whole(to, heads * tokens)
    distance = whole(token, owned) ^ me
    slot = distance ^ ((distance >> 1) & 1) if head_count >= 4 else distance
    turned = 1 ^ even_bits(distance, head_count.bit_length() - 1) ^ (j & 1)
    cots = []
    for side in range(2):
        held = jnp.where(j == 0, core, role) ^ side ^ core ^ turned
        place = ((held * head_count + slot) * columns + j) * owned + rest(token, owned)
        spread_ref[side] = matmul(normed, one_hot(at == place), 0, 0)
        cots.append(jnp.concatenate([r[...] for r in shard_refs[side * columns : (side + 1) * columns]], axis=0))
    keep = rest(iota((1, heads, size), 2), heads) == iota((1, heads, size), 1)
    copies = []
    for g in range(groups):
        total = None
        for side in range(2):
            block = spread_ref[side, g * rows : (g + 1) * rows, :]
            left = jnp.where(keep, block[:, None, :], 0.0).reshape(rows * heads, size).astype(BF16)
            part = matmul(left, cots[side])
            total = part if total is None else total + part
        place = pl.ds(g * rows * heads, rows * heads)
        total_ref[place, :] = total
        copies.append(pltpu.make_async_copy(total_ref.at[place], out_ref.at[place], sems.at[g]))
        copies[g].start()
    for copy in copies:
        copy.wait()


def latent_kernel(head_count, columns, rms_ref, hat_ref, gain_ref, other_ref, *refs):
    block_refs, out_ref = refs[:-1], refs[-1]
    column = lax.axis_index("ctx") >> 1
    crossed = crossing(lax.axis_index("head"), lax.axis_index("ctx") >> 1, head_count.bit_length() - 1)
    relative = [ref[...] for ref in block_refs]
    count = out_ref.shape[0]
    first = other_ref.shape[0] - count * columns // 2
    for j in range(0, columns, 2):
        place = first + j // 2 * count
        relative[j] = jnp.where(crossed == 0, relative[j], other_ref[place : place + count, :])
    blocks = []
    for b in range(columns):
        block = relative[0]
        for j in range(1, columns):
            block = jnp.where((column ^ j) == b, relative[j], block)
        blocks.append(block)
    scaled = jnp.concatenate(blocks, axis=1) * gain_ref[...]
    hat = hat_ref[...]
    inner = jnp.mean(scaled * hat, axis=1, keepdims=True)
    out_ref[...] = rms_ref[...] * (scaled - hat * inner)


def per_device(head_count, ctx_count, latent, gain, cotangent, weight):
    columns = ctx_count // 2
    owned, width = latent.shape[1:]
    _, tokens, heads, channels = cotangent.shape
    rows = weight.shape[0]
    bits = head_count.bit_length() - 1
    params = pltpu.CompilerParams(vmem_limit_bytes=48 * 1024 * 1024)

    def swap(value, partner):
        pairs = [
            (h * ctx_count + c, p * ctx_count + q)
            for h in range(head_count)
            for c in range(ctx_count)
            for p, q in [partner(h, c)]
        ]
        return lax.ppermute(value, ("head", "ctx"), pairs)

    def ctx_swap(value, mask):
        return swap(value, lambda h, c: (h, c ^ mask))

    def to_role(value):
        return swap(value, lambda h, c: (h, c ^ 2 ^ crossing(h, (c ^ 2) >> 1, bits)))

    def to_owner(value):
        return swap(value, lambda h, c: (h, c ^ 2 ^ crossing(h, c >> 1, bits)))

    def head_swap(value, mask):
        return swap(value, lambda h, c: (h ^ mask, c ^ 1 ^ even_bits(mask, bits)))

    def call(kernel, out, *args, scratch=(), flops=0, place=pltpu.VMEM):
        moved = sum(a.size * a.dtype.itemsize for a in args)
        return pl.pallas_call(
            kernel,
            out_shape=out,
            out_specs=jax.tree.map(lambda _: pl.BlockSpec(memory_space=place), out),
            scratch_shapes=scratch,
            compiler_params=params,
            cost_estimate=pl.CostEstimate(flops=flops, bytes_accessed=moved, transcendentals=0),
        )(*args)

    own = cotangent.reshape(tokens * heads, channels)
    far = [to_role(own)]
    other = ctx_swap(own, 1)
    if columns > 2:
        first = jnp.where(crossing(lax.axis_index("head"), lax.axis_index("ctx") >> 1, bits) == 0, own, other)
        shards = [first] + far
        mask = 4
        while mask < ctx_count:
            shards += [ctx_swap(s, mask) for s in shards]
            mask *= 2
        far = shards[1:]
    gain_row = gain.reshape(1, width)
    block = jax.ShapeDtypeStruct((owned, 2 * rows), BF16)
    row = jax.ShapeDtypeStruct((owned, width), F32)
    rms, hat, *normed = call(
        functools.partial(norm_kernel, columns), [row] * 2 + [block] * columns, latent[0], gain_row, flops=4 * 10**8
    )

    weight_flat = weight.reshape(rows * heads, channels)
    weight_other = ctx_swap(weight_flat, 1)
    weight_flat, weight_other, _ = lax.optimization_barrier((weight_flat, weight_other, normed[0]))
    size = columns * tokens * heads
    chip_weight, order = call(
        functools.partial(weight_kernel, head_count, heads, owned, columns),
        [jax.ShapeDtypeStruct((heads, channels, 2 * rows), BF16), jax.ShapeDtypeStruct((size, size), BF16)],
        weight_flat,
        weight_other,
    )

    mask = 2
    while mask < ctx_count:
        for j in range(columns):
            if j & (mask >> 1):
                normed[j] = ctx_swap(normed[j], mask | (mask == 2))
        mask *= 2
    normed = jnp.concatenate(normed, axis=0)

    size = head_count * columns * owned // 4
    sums, *sent = call(
        functools.partial(partial_kernel, head_count, 4),
        [jax.ShapeDtypeStruct((size, 2 * rows), F32)] + [jax.ShapeDtypeStruct((2 * size, 2 * rows), BF16)] * 3,
        order,
        chip_weight,
        *far,
        own,
        other,
    )
    sums, *far = lax.optimization_barrier((sums, *far))
    far_other = [ctx_swap(s, 1) for s in far]
    got = {m: head_swap(jnp.concatenate([sent[n], normed], axis=0), m) for m, n in PLANE}
    got = [got[m] for m in (1, 3, 2)]
    skip, count, mask = 0, 4 * normed.shape[0], 4
    while mask < head_count:
        half = sums.shape[0] // 2
        sums, normed = call(
            functools.partial(merge_kernel, skip),
            [jax.ShapeDtypeStruct((half, 2 * rows), F32), jax.ShapeDtypeStruct((2 * half + count, 2 * rows), BF16)],
            sums,
            normed,
            *got,
        )
        if mask == 4:
            normed, *far_other = lax.optimization_barrier((normed, *far_other))
        got = [head_swap(normed, mask)]
        skip, count, mask = 2 * half, 2 * count, 2 * mask
    short = jax.ShapeDtypeStruct((owned, 2 * rows), F32)
    kept = owned if columns == 2 else 0
    *blocks, normed_own, sent = call(
        functools.partial(last_merge_kernel, skip, columns),
        [short] * columns
        + [jax.ShapeDtypeStruct((count, rows), F32), jax.ShapeDtypeStruct((count // 2 + kept, 2 * rows), F32)],
        sums,
        normed,
        *got,
    )
    mask = ctx_count // 2
    while mask > 2:
        for j in range(columns):
            if j & (mask >> 1):
                blocks[j] = ctx_swap(blocks[j], mask)
        mask //= 2
    if columns > 2:
        sent = jnp.concatenate([sent] + blocks[::2], axis=0)
    both = ctx_swap(sent, 1)
    for j in range(1, columns, 2):
        blocks[j] = to_owner(blocks[j])

    weight_grad = call(
        functools.partial(weight_grad_kernel, head_count, heads, owned, columns),
        jax.ShapeDtypeStruct((rows * heads, channels), F32),
        normed_own,
        both,
        own,
        *far,
        other,
        *far_other,
        scratch=[
            pltpu.VMEM((2, rows, columns * tokens * heads), F32),
            pltpu.VMEM((rows * heads, channels), F32),
            pltpu.SemaphoreType.DMA((4 if rows % 32 == 0 else 1,)),
        ],
        flops=2 * rows * heads * channels * ctx_count * tokens * heads,
        place=pl.ANY,
    )
    weight_grad, *blocks = lax.optimization_barrier((weight_grad, *blocks))
    latent_gradient = call(
        functools.partial(latent_kernel, head_count, columns),
        jax.ShapeDtypeStruct((owned, width), F32),
        rms,
        hat,
        gain_row,
        both,
        *blocks,
    )
    return latent_gradient[None], weight_grad.reshape(weight.shape)


def solution(mesh):
    return jax.shard_map(
        functools.partial(per_device, mesh.shape["head"], mesh.shape["ctx"]),
        mesh=mesh,
        in_specs=(
            P("ctx", "head", None),
            P(),
            P("ctx", None, "head", None),
            P("ctx", "head", None),
        ),
        out_specs=(P("ctx", "head", None), P("ctx", "head", None)),
        check_vma=False,
    )
```

```python
import functools

import jax
import jax.numpy as jnp
from jax import lax
from jax.experimental import pallas as pl
from jax.experimental.pallas import tpu as pltpu
from jax.sharding import PartitionSpec as P


F32 = jnp.float32
BF16 = jnp.bfloat16


PLANE = ((1, 1), (3, 2), (2, 0))


def iota(shape, axis):
    return lax.broadcasted_iota(jnp.int32, shape, axis)


def one_hot(condition):
    return jnp.where(condition, 1.0, 0.0).astype(BF16)


def matmul(a, b, a_axis=1, b_axis=0):
    return lax.dot_general(a, b, (((a_axis,), (b_axis,)), ((), ())), preferred_element_type=F32)


def whole(value, step):
    return value >> (step.bit_length() - 1) if step & (step - 1) == 0 else value // step


def rest(value, step):
    return value & (step - 1) if step & (step - 1) == 0 else value % step


def reverse_bits(value, count):
    out = 0
    for bit in range(count):
        out = out | (((value >> bit) & 1) << (count - 1 - bit))
    return out


def two_terms(value):
    high = value.astype(BF16).astype(F32)
    return jnp.concatenate([high, (value - high).astype(BF16).astype(F32)], axis=0)


def even_bits(value, count):
    out = 1 ^ (value & 1)
    for bit in range(1, count):
        out = out ^ ((value >> bit) & 1)
    return out


def crossing(head, column, bits):
    return even_bits(head, bits) ^ (column & 1) ^ 1


def weight_kernel(head_count, heads, owned, shards, own_ref, other_ref, out_ref, order_ref, place_ref):
    rows = own_ref.shape[0] // heads
    group = min(rows, max(256 // heads, 1))
    size = group * heads
    to, at = iota((size, size), 0), iota((size, size), 1)
    order = one_hot(at == rest(to, group) * heads + whole(to, group))
    parts = [[] for _ in range(heads)]
    for ref in (own_ref, other_ref):
        for start in range(0, rows, group):
            moved = matmul(order, ref[pl.ds(start * heads, size), :])
            for h in range(heads):
                parts[h].append(moved[h * group : (h + 1) * group, :])
    for h in range(heads):
        out_ref[h] = jnp.concatenate(parts[h], axis=0).T.astype(BF16)
    me = lax.axis_index("head")
    bits = head_count.bit_length() - 1
    tokens = head_count * owned
    size = order_ref.shape[0]
    to, at = iota((size, size), 0), iota((size, size), 1)
    i, j = rest(to, owned), rest(whole(to, owned), shards)
    position = rest(whole(to, owned * shards), head_count)
    token = (reverse_bits(position, bits) ^ me) * owned + i
    order_ref[...] = one_hot(at == (j * tokens + token) * heads + whole(to, tokens * shards))
    core = lax.axis_index("ctx") & 1
    role = core ^ crossing(me, lax.axis_index("ctx") >> 1, bits)
    size = place_ref.shape[2]
    at, to = iota(place_ref.shape[1:], 0), iota((1, size), 1)
    token, j = rest(whole(to, heads), tokens), whole(to, heads * tokens)
    distance = whole(token, owned) ^ me
    slot = distance ^ ((distance >> 1) & 1) if head_count >= 4 else distance
    turned = 1 ^ even_bits(distance, bits) ^ (j & 1)
    for side in range(2):
        held = jnp.where(j == 0, core, role) ^ side ^ core ^ turned
        place = ((held * head_count + slot) * shards + j) * owned + rest(token, owned)
        place_ref[side] = one_hot(at == place)


def partial_kernel(head_count, count, order_ref, weight_ref, *refs):
    shard_refs, (own_ref, other_ref), out_refs = refs[: -count - 2], refs[-count - 2 : -count], refs[-count:]
    core = lax.axis_index("ctx") & 1
    crossed = crossing(lax.axis_index("head"), lax.axis_index("ctx") >> 1, head_count.bit_length() - 1)
    first = jnp.where(crossed == 0, own_ref[...], other_ref[...])
    stacked = jnp.concatenate([first] + [ref[...] for ref in shard_refs], axis=0)
    moved = matmul(order_ref[...], stacked).astype(BF16)
    size, rows = out_refs[0].shape[0], out_refs[0].shape[1] // 2
    part = count * size
    total = matmul(moved[:part], weight_ref[0])
    for h in range(1, weight_ref.shape[0]):
        total += matmul(moved[h * part : (h + 1) * part], weight_ref[h])
    turned = jnp.concatenate([total[:, rows:], total[:, :rows]], axis=1)
    total = jnp.where(core == 0, total, turned)
    out_refs[0][...] = total[:size]
    for n, ref in enumerate(out_refs[1:]):
        ref[...] = two_terms(total[(n + 1) * size : (n + 2) * size]).astype(BF16)


def merge_kernel(skip, sums_ref, normed_ref, *refs):
    got_refs, keep_ref, message_ref = refs[:-2], refs[-2], refs[-1]
    total, rows = merged(skip, sums_ref, normed_ref, got_refs)
    half = keep_ref.shape[0]
    keep_ref[...] = total[:half]
    message_ref[...] = jnp.concatenate([two_terms(total[half:]), rows], axis=0).astype(BF16)


def last_merge_kernel(skip, columns, sums_ref, normed_ref, *refs):
    got_refs, block_refs, own_ref, sent_ref = refs[: -columns - 2], refs[-columns - 2 : -2], refs[-2], refs[-1]
    total, rows = merged(skip, sums_ref, normed_ref, got_refs)
    owned = total.shape[0] // columns
    for j, ref in enumerate(block_refs):
        ref[...] = total[j * owned : (j + 1) * owned]
    core = lax.axis_index("ctx") & 1
    count, width = rows.shape[0] // 2, rows.shape[1] // 2
    own_ref[...] = jnp.where(core == 0, rows[:, :width], rows[:, width:])
    sent = jnp.where(core == 0, rows[:, width:], rows[:, :width])
    sent = jnp.concatenate([sent[:count], sent[count:]], axis=1)
    sent_ref[...] = jnp.concatenate([sent, total[:owned]], axis=0) if columns == 2 else sent


def merged(skip, sums_ref, normed_ref, got_refs):
    total, half = sums_ref[...], sums_ref.shape[0]
    rows = [normed_ref[...].astype(F32)[skip:]]
    for ref in got_refs:
        got = ref[...].astype(F32)
        total = total + (got[:half] + got[half : 2 * half])
        rows.append(got[2 * half :])
    return total, jnp.concatenate(rows, axis=0)


def norm_kernel(columns, latent_ref, gain_ref, rms_ref, hat_ref, *out_refs):
    column = lax.axis_index("ctx") >> 1
    raw = latent_ref[...].astype(F32)
    rms = lax.rsqrt(jnp.mean(raw * raw, axis=1, keepdims=True) + 1e-06)
    hat = raw * rms
    rms_ref[...] = jnp.broadcast_to(rms, raw.shape)
    hat_ref[...] = hat
    normed = (hat * gain_ref[...]).astype(BF16)
    width = normed.shape[1] // columns
    for j, ref in enumerate(out_refs):
        block = normed[:, :width]
        for b in range(1, columns):
            block = jnp.where((column ^ j) == b, normed[:, b * width : (b + 1) * width], block)
        ref[...] = block


def weight_grad_kernel(heads, columns, place_ref, own_ref, other_ref, *refs):
    shard_refs, (out_ref, spread_ref, total_ref, sems) = refs[:-4], refs[-4:]
    groups = sems.shape[0]
    rows = out_ref.shape[0] // heads // groups
    count, width = own_ref.shape[0] // 2, own_ref.shape[1]
    other = other_ref[...]
    normed = jnp.concatenate([own_ref[...], other[:count, :width], other[:count, width:]], axis=0).astype(BF16)
    size = place_ref.shape[2]
    cots = []
    for side in range(2):
        spread_ref[side] = matmul(normed, place_ref[side], 0, 0)
        cots.append(jnp.concatenate([r[...] for r in shard_refs[side * columns : (side + 1) * columns]], axis=0))
    keep = rest(iota((1, heads, size), 2), heads) == iota((1, heads, size), 1)
    copies = []
    for g in range(groups):
        total = None
        for side in range(2):
            block = spread_ref[side, g * rows : (g + 1) * rows, :]
            left = jnp.where(keep, block[:, None, :], 0.0).reshape(rows * heads, size).astype(BF16)
            part = matmul(left, cots[side])
            total = part if total is None else total + part
        place = pl.ds(g * rows * heads, rows * heads)
        total_ref[place, :] = total
        copies.append(pltpu.make_async_copy(total_ref.at[place], out_ref.at[place], sems.at[g]))
        copies[g].start()
    for copy in copies:
        copy.wait()


def latent_kernel(head_count, columns, rms_ref, hat_ref, gain_ref, other_ref, *refs):
    block_refs, out_ref = refs[:-1], refs[-1]
    column = lax.axis_index("ctx") >> 1
    crossed = crossing(lax.axis_index("head"), lax.axis_index("ctx") >> 1, head_count.bit_length() - 1)
    relative = [ref[...] for ref in block_refs]
    count = out_ref.shape[0]
    first = other_ref.shape[0] - count * columns // 2
    for j in range(0, columns, 2):
        place = first + j // 2 * count
        relative[j] = jnp.where(crossed == 0, relative[j], other_ref[place : place + count, :])
    blocks = []
    for b in range(columns):
        block = relative[0]
        for j in range(1, columns):
            block = jnp.where((column ^ j) == b, relative[j], block)
        blocks.append(block)
    scaled = jnp.concatenate(blocks, axis=1) * gain_ref[...]
    hat = hat_ref[...]
    inner = jnp.mean(scaled * hat, axis=1, keepdims=True)
    out_ref[...] = rms_ref[...] * (scaled - hat * inner)


def per_device(head_count, ctx_count, latent, gain, cotangent, weight):
    columns = ctx_count // 2
    owned, width = latent.shape[1:]
    _, tokens, heads, channels = cotangent.shape
    rows = weight.shape[0]
    bits = head_count.bit_length() - 1
    params = pltpu.CompilerParams(vmem_limit_bytes=48 * 1024 * 1024)

    def swap(value, partner):
        pairs = [
            (h * ctx_count + c, p * ctx_count + q)
            for h in range(head_count)
            for c in range(ctx_count)
            for p, q in [partner(h, c)]
        ]
        return lax.ppermute(value, ("head", "ctx"), pairs)

    def ctx_swap(value, mask):
        return swap(value, lambda h, c: (h, c ^ mask))

    def to_role(value):
        return swap(value, lambda h, c: (h, c ^ 2 ^ crossing(h, (c ^ 2) >> 1, bits)))

    def to_owner(value):
        return swap(value, lambda h, c: (h, c ^ 2 ^ crossing(h, c >> 1, bits)))

    def head_swap(value, mask):
        return swap(value, lambda h, c: (h ^ mask, c ^ 1 ^ even_bits(mask, bits)))

    def call(kernel, out, *args, scratch=(), flops=0, place=pltpu.VMEM):
        moved = sum(a.size * a.dtype.itemsize for a in args)
        return pl.pallas_call(
            kernel,
            out_shape=out,
            out_specs=jax.tree.map(lambda _: pl.BlockSpec(memory_space=place), out),
            scratch_shapes=scratch,
            compiler_params=params,
            cost_estimate=pl.CostEstimate(flops=flops, bytes_accessed=moved, transcendentals=0),
        )(*args)

    own = cotangent.reshape(tokens * heads, channels)
    far = [to_role(own)]
    other = ctx_swap(own, 1)
    if columns > 2:
        first = jnp.where(crossing(lax.axis_index("head"), lax.axis_index("ctx") >> 1, bits) == 0, own, other)
        shards = [first] + far
        mask = 4
        while mask < ctx_count:
            shards += [ctx_swap(s, mask) for s in shards]
            mask *= 2
        far = shards[1:]
    gain_row = gain.reshape(1, width)
    block = jax.ShapeDtypeStruct((owned, 2 * rows), BF16)
    row = jax.ShapeDtypeStruct((owned, width), F32)
    rms, hat, *normed = call(
        functools.partial(norm_kernel, columns), [row] * 2 + [block] * columns, latent[0], gain_row, flops=4 * 10**8
    )

    weight_flat = weight.reshape(rows * heads, channels)
    weight_other = ctx_swap(weight_flat, 1)
    weight_flat, weight_other, _ = lax.optimization_barrier((weight_flat, weight_other, normed[0]))
    size = columns * tokens * heads
    chip_weight, order, place = call(
        functools.partial(weight_kernel, head_count, heads, owned, columns),
        [
            jax.ShapeDtypeStruct((heads, channels, 2 * rows), BF16),
            jax.ShapeDtypeStruct((size, size), BF16),
            jax.ShapeDtypeStruct((2, ctx_count * tokens, size), BF16),
        ],
        weight_flat,
        weight_other,
    )

    mask = 2
    while mask < ctx_count:
        for j in range(columns):
            if j & (mask >> 1):
                normed[j] = ctx_swap(normed[j], mask | (mask == 2))
        mask *= 2
    normed = jnp.concatenate(normed, axis=0)

    size = head_count * columns * owned // 4
    sums, *sent = call(
        functools.partial(partial_kernel, head_count, 4),
        [jax.ShapeDtypeStruct((size, 2 * rows), F32)] + [jax.ShapeDtypeStruct((2 * size, 2 * rows), BF16)] * 3,
        order,
        chip_weight,
        *far,
        own,
        other,
    )
    sums, *far = lax.optimization_barrier((sums, *far))
    far_other = [ctx_swap(s, 1) for s in far]
    got = {m: head_swap(jnp.concatenate([sent[n], normed], axis=0), m) for m, n in PLANE}
    got = [got[m] for m in (1, 3, 2)]
    skip, count, mask = 0, 4 * normed.shape[0], 4
    while mask < head_count:
        half = sums.shape[0] // 2
        sums, normed = call(
            functools.partial(merge_kernel, skip),
            [jax.ShapeDtypeStruct((half, 2 * rows), F32), jax.ShapeDtypeStruct((2 * half + count, 2 * rows), BF16)],
            sums,
            normed,
            *got,
        )
        if mask == 4:
            normed, *far_other = lax.optimization_barrier((normed, *far_other))
        got = [head_swap(normed, mask)]
        skip, count, mask = 2 * half, 2 * count, 2 * mask
    short = jax.ShapeDtypeStruct((owned, 2 * rows), F32)
    kept = owned if columns == 2 else 0
    *blocks, normed_own, sent = call(
        functools.partial(last_merge_kernel, skip, columns),
        [short] * columns
        + [jax.ShapeDtypeStruct((count, rows), F32), jax.ShapeDtypeStruct((count // 2 + kept, 2 * rows), F32)],
        sums,
        normed,
        *got,
    )
    mask = ctx_count // 2
    while mask > 2:
        for j in range(columns):
            if j & (mask >> 1):
                blocks[j] = ctx_swap(blocks[j], mask)
        mask //= 2
    if columns > 2:
        sent = jnp.concatenate([sent] + blocks[::2], axis=0)
    both = ctx_swap(sent, 1)
    for j in range(1, columns, 2):
        blocks[j] = to_owner(blocks[j])

    weight_grad = call(
        functools.partial(weight_grad_kernel, heads, columns),
        jax.ShapeDtypeStruct((rows * heads, channels), F32),
        place,
        normed_own,
        both,
        own,
        *far,
        other,
        *far_other,
        scratch=[
            pltpu.VMEM((2, rows, columns * tokens * heads), F32),
            pltpu.VMEM((rows * heads, channels), F32),
            pltpu.SemaphoreType.DMA((4 if rows % 32 == 0 else 1,)),
        ],
        flops=2 * rows * heads * channels * ctx_count * tokens * heads,
        place=pl.ANY,
    )
    weight_grad, *blocks = lax.optimization_barrier((weight_grad, *blocks))
    latent_gradient = call(
        functools.partial(latent_kernel, head_count, columns),
        jax.ShapeDtypeStruct((owned, width), F32),
        rms,
        hat,
        gain_row,
        both,
        *blocks,
    )
    return latent_gradient[None], weight_grad.reshape(weight.shape)


def solution(mesh):
    return jax.shard_map(
        functools.partial(per_device, mesh.shape["head"], mesh.shape["ctx"]),
        mesh=mesh,
        in_specs=(
            P("ctx", "head", None),
            P(),
            P("ctx", None, "head", None),
            P("ctx", "head", None),
        ),
        out_specs=(P("ctx", "head", None), P("ctx", "head", None)),
        check_vma=False,
    )
```

```python
import functools

import jax
import jax.numpy as jnp
from jax import lax
from jax.experimental import pallas as pl
from jax.experimental.pallas import tpu as pltpu
from jax.sharding import PartitionSpec as P


F32 = jnp.float32
BF16 = jnp.bfloat16


PLANE = ((1, 1), (3, 2), (2, 0))


def iota(shape, axis):
    return lax.broadcasted_iota(jnp.int32, shape, axis)


def one_hot(condition):
    return jnp.where(condition, 1.0, 0.0).astype(BF16)


def matmul(a, b, a_axis=1, b_axis=0):
    return lax.dot_general(a, b, (((a_axis,), (b_axis,)), ((), ())), preferred_element_type=F32)


def whole(value, step):
    return value >> (step.bit_length() - 1) if step & (step - 1) == 0 else value // step


def rest(value, step):
    return value & (step - 1) if step & (step - 1) == 0 else value % step


def reverse_bits(value, count):
    out = 0
    for bit in range(count):
        out = out | (((value >> bit) & 1) << (count - 1 - bit))
    return out


def two_terms(value):
    high = value.astype(BF16).astype(F32)
    return jnp.concatenate([high, (value - high).astype(BF16).astype(F32)], axis=0)


def even_bits(value, count):
    out = 1 ^ (value & 1)
    for bit in range(1, count):
        out = out ^ ((value >> bit) & 1)
    return out


def crossing(head, column, bits):
    return even_bits(head, bits) ^ (column & 1) ^ 1


def weight_kernel(head_count, heads, owned, shards, own_ref, other_ref, out_ref, order_ref):
    rows = own_ref.shape[0] // heads
    group = min(rows, max(256 // heads, 1))
    size = group * heads
    to, at = iota((size, size), 0), iota((size, size), 1)
    order = one_hot(at == rest(to, group) * heads + whole(to, group))
    parts = [[] for _ in range(heads)]
    for ref in (own_ref, other_ref):
        for start in range(0, rows, group):
            moved = matmul(order, ref[pl.ds(start * heads, size), :])
            for h in range(heads):
                parts[h].append(moved[h * group : (h + 1) * group, :])
    for h in range(heads):
        out_ref[h] = jnp.concatenate(parts[h], axis=0).T.astype(BF16)
    me = lax.axis_index("head")
    bits = head_count.bit_length() - 1
    tokens = head_count * owned
    size = order_ref.shape[0]
    to, at = iota((size, size), 0), iota((size, size), 1)
    i, j = rest(to, owned), rest(whole(to, owned), shards)
    position = rest(whole(to, owned * shards), head_count)
    token = (reverse_bits(position, bits) ^ me) * owned + i
    order_ref[...] = one_hot(at == (j * tokens + token) * heads + whole(to, tokens * shards))


def partial_kernel(head_count, count, order_ref, weight_ref, *refs):
    shard_refs, (own_ref, other_ref), out_refs = refs[: -count - 2], refs[-count - 2 : -count], refs[-count:]
    core = lax.axis_index("ctx") & 1
    crossed = crossing(lax.axis_index("head"), lax.axis_index("ctx") >> 1, head_count.bit_length() - 1)
    first = jnp.where(crossed == 0, own_ref[...], other_ref[...])
    stacked = jnp.concatenate([first] + [ref[...] for ref in shard_refs], axis=0)
    moved = matmul(order_ref[...], stacked).astype(BF16)
    size, rows = out_refs[0].shape[0], out_refs[0].shape[1] // 2
    part = count * size
    total = matmul(moved[:part], weight_ref[0])
    for h in range(1, weight_ref.shape[0]):
        total += matmul(moved[h * part : (h + 1) * part], weight_ref[h])
    turned = jnp.concatenate([total[:, rows:], total[:, :rows]], axis=1)
    total = jnp.where(core == 0, total, turned)
    out_refs[0][...] = total[:size]
    for n, ref in enumerate(out_refs[1:]):
        ref[...] = two_terms(total[(n + 1) * size : (n + 2) * size]).astype(BF16)


def merge_kernel(skip, sums_ref, normed_ref, *refs):
    got_refs, keep_ref, message_ref = refs[:-2], refs[-2], refs[-1]
    total, rows = merged(skip, sums_ref, normed_ref, got_refs)
    half = keep_ref.shape[0]
    keep_ref[...] = total[:half]
    message_ref[...] = jnp.concatenate([two_terms(total[half:]), rows], axis=0).astype(BF16)


def last_merge_kernel(skip, columns, sums_ref, normed_ref, *refs):
    got_refs, block_refs, own_ref, sent_ref = refs[: -columns - 2], refs[-columns - 2 : -2], refs[-2], refs[-1]
    total, rows = merged(skip, sums_ref, normed_ref, got_refs)
    owned = total.shape[0] // columns
    for j, ref in enumerate(block_refs):
        ref[...] = total[j * owned : (j + 1) * owned]
    core = lax.axis_index("ctx") & 1
    count, width = rows.shape[0] // 2, rows.shape[1] // 2
    own_ref[...] = jnp.where(core == 0, rows[:, :width], rows[:, width:])
    sent = jnp.where(core == 0, rows[:, width:], rows[:, :width])
    sent = jnp.concatenate([sent[:count], sent[count:]], axis=1)
    sent_ref[...] = jnp.concatenate([sent, total[:owned]], axis=0) if columns == 2 else sent


def merged(skip, sums_ref, normed_ref, got_refs):
    total, half = sums_ref[...], sums_ref.shape[0]
    rows = [normed_ref[...].astype(F32)[skip:]]
    for ref in got_refs:
        got = ref[...].astype(F32)
        total = total + (got[:half] + got[half : 2 * half])
        rows.append(got[2 * half :])
    return total, jnp.concatenate(rows, axis=0)


def norm_kernel(columns, latent_ref, gain_ref, rms_ref, hat_ref, *out_refs):
    column = lax.axis_index("ctx") >> 1
    raw = latent_ref[...].astype(F32)
    rms = lax.rsqrt(jnp.mean(raw * raw, axis=1, keepdims=True) + 1e-06)
    hat = raw * rms
    rms_ref[...] = jnp.broadcast_to(rms, raw.shape)
    hat_ref[...] = hat
    normed = (hat * gain_ref[...]).astype(BF16)
    width = normed.shape[1] // columns
    for j, ref in enumerate(out_refs):
        block = normed[:, :width]
        for b in range(1, columns):
            block = jnp.where((column ^ j) == b, normed[:, b * width : (b + 1) * width], block)
        ref[...] = block


def weight_grad_kernel(head_count, heads, owned, columns, own_ref, other_ref, *refs):
    shard_refs, (out_ref, spread_ref, total_ref, sems) = refs[:-4], refs[-4:]
    me = lax.axis_index("head")
    core = lax.axis_index("ctx") & 1
    role = core ^ crossing(me, lax.axis_index("ctx") >> 1, head_count.bit_length() - 1)
    groups = sems.shape[0]
    rows = out_ref.shape[0] // heads // groups
    tokens = head_count * owned
    count, width = own_ref.shape[0] // 2, own_ref.shape[1]
    other = other_ref[...]
    normed = jnp.concatenate([own_ref[...], other[:count, :width], other[:count, width:]], axis=0).astype(BF16)
    size = columns * tokens * heads
    at, to = iota((normed.shape[0], size), 0), iota((1, size), 1)
    token, j = rest(whole(to, heads), tokens), whole(to, heads * tokens)
    distance = whole(token, owned) ^ me
    slot = distance ^ ((distance >> 1) & 1) if head_count >= 4 else distance
    turned = 1 ^ even_bits(distance, head_count.bit_length() - 1) ^ (j & 1)
    cots = []
    for side in range(2):
        held = jnp.where(j == 0, core, role) ^ side ^ core ^ turned
        place = ((held * head_count + slot) * columns + j) * owned + rest(token, owned)
        spread_ref[side] = matmul(normed, one_hot(at == place), 0, 0)
        cots.append(jnp.concatenate([r[...] for r in shard_refs[side * columns : (side + 1) * columns]], axis=0))
    keep = rest(iota((1, heads, size), 2), heads) == iota((1, heads, size), 1)
    both_cots = jnp.concatenate(cots, axis=0)
    copies = []
    for g in range(groups):
        lefts = []
        for side in range(2):
            block = spread_ref[side, g * rows : (g + 1) * rows, :]
            lefts.append(jnp.where(keep, block[:, None, :], 0.0).reshape(rows * heads, size).astype(BF16))
        total = matmul(jnp.concatenate(lefts, axis=1), both_cots)
        place = pl.ds(g * rows * heads, rows * heads)
        total_ref[place, :] = total
        copies.append(pltpu.make_async_copy(total_ref.at[place], out_ref.at[place], sems.at[g]))
        copies[g].start()
    for copy in copies:
        copy.wait()


def latent_kernel(head_count, columns, rms_ref, hat_ref, gain_ref, other_ref, *refs):
    block_refs, out_ref = refs[:-1], refs[-1]
    column = lax.axis_index("ctx") >> 1
    crossed = crossing(lax.axis_index("head"), lax.axis_index("ctx") >> 1, head_count.bit_length() - 1)
    relative = [ref[...] for ref in block_refs]
    count = out_ref.shape[0]
    first = other_ref.shape[0] - count * columns // 2
    for j in range(0, columns, 2):
        place = first + j // 2 * count
        relative[j] = jnp.where(crossed == 0, relative[j], other_ref[place : place + count, :])
    blocks = []
    for b in range(columns):
        block = relative[0]
        for j in range(1, columns):
            block = jnp.where((column ^ j) == b, relative[j], block)
        blocks.append(block)
    scaled = jnp.concatenate(blocks, axis=1) * gain_ref[...]
    hat = hat_ref[...]
    inner = jnp.mean(scaled * hat, axis=1, keepdims=True)
    out_ref[...] = rms_ref[...] * (scaled - hat * inner)


def per_device(head_count, ctx_count, latent, gain, cotangent, weight):
    columns = ctx_count // 2
    owned, width = latent.shape[1:]
    _, tokens, heads, channels = cotangent.shape
    rows = weight.shape[0]
    bits = head_count.bit_length() - 1
    params = pltpu.CompilerParams(vmem_limit_bytes=48 * 1024 * 1024)

    def swap(value, partner):
        pairs = [
            (h * ctx_count + c, p * ctx_count + q)
            for h in range(head_count)
            for c in range(ctx_count)
            for p, q in [partner(h, c)]
        ]
        return lax.ppermute(value, ("head", "ctx"), pairs)

    def ctx_swap(value, mask):
        return swap(value, lambda h, c: (h, c ^ mask))

    def to_role(value):
        return swap(value, lambda h, c: (h, c ^ 2 ^ crossing(h, (c ^ 2) >> 1, bits)))

    def to_owner(value):
        return swap(value, lambda h, c: (h, c ^ 2 ^ crossing(h, c >> 1, bits)))

    def head_swap(value, mask):
        return swap(value, lambda h, c: (h ^ mask, c ^ 1 ^ even_bits(mask, bits)))

    def call(kernel, out, *args, scratch=(), flops=0, place=pltpu.VMEM):
        moved = sum(a.size * a.dtype.itemsize for a in args)
        return pl.pallas_call(
            kernel,
            out_shape=out,
            out_specs=jax.tree.map(lambda _: pl.BlockSpec(memory_space=place), out),
            scratch_shapes=scratch,
            compiler_params=params,
            cost_estimate=pl.CostEstimate(flops=flops, bytes_accessed=moved, transcendentals=0),
        )(*args)

    own = cotangent.reshape(tokens * heads, channels)
    far = [to_role(own)]
    other = ctx_swap(own, 1)
    if columns > 2:
        first = jnp.where(crossing(lax.axis_index("head"), lax.axis_index("ctx") >> 1, bits) == 0, own, other)
        shards = [first] + far
        mask = 4
        while mask < ctx_count:
            shards += [ctx_swap(s, mask) for s in shards]
            mask *= 2
        far = shards[1:]
    gain_row = gain.reshape(1, width)
    block = jax.ShapeDtypeStruct((owned, 2 * rows), BF16)
    row = jax.ShapeDtypeStruct((owned, width), F32)
    rms, hat, *normed = call(
        functools.partial(norm_kernel, columns), [row] * 2 + [block] * columns, latent[0], gain_row, flops=4 * 10**8
    )

    weight_flat = weight.reshape(rows * heads, channels)
    weight_other = ctx_swap(weight_flat, 1)
    weight_flat, weight_other, _ = lax.optimization_barrier((weight_flat, weight_other, normed[0]))
    size = columns * tokens * heads
    chip_weight, order = call(
        functools.partial(weight_kernel, head_count, heads, owned, columns),
        [jax.ShapeDtypeStruct((heads, channels, 2 * rows), BF16), jax.ShapeDtypeStruct((size, size), BF16)],
        weight_flat,
        weight_other,
    )

    mask = 2
    while mask < ctx_count:
        for j in range(columns):
            if j & (mask >> 1):
                normed[j] = ctx_swap(normed[j], mask | (mask == 2))
        mask *= 2
    normed = jnp.concatenate(normed, axis=0)

    size = head_count * columns * owned // 4
    sums, *sent = call(
        functools.partial(partial_kernel, head_count, 4),
        [jax.ShapeDtypeStruct((size, 2 * rows), F32)] + [jax.ShapeDtypeStruct((2 * size, 2 * rows), BF16)] * 3,
        order,
        chip_weight,
        *far,
        own,
        other,
    )
    sums, *far = lax.optimization_barrier((sums, *far))
    far_other = [ctx_swap(s, 1) for s in far]
    got = {m: head_swap(jnp.concatenate([sent[n], normed], axis=0), m) for m, n in PLANE}
    got = [got[m] for m in (1, 3, 2)]
    skip, count, mask = 0, 4 * normed.shape[0], 4
    while mask < head_count:
        half = sums.shape[0] // 2
        sums, normed = call(
            functools.partial(merge_kernel, skip),
            [jax.ShapeDtypeStruct((half, 2 * rows), F32), jax.ShapeDtypeStruct((2 * half + count, 2 * rows), BF16)],
            sums,
            normed,
            *got,
        )
        if mask == 4:
            normed, *far_other = lax.optimization_barrier((normed, *far_other))
        got = [head_swap(normed, mask)]
        skip, count, mask = 2 * half, 2 * count, 2 * mask
    short = jax.ShapeDtypeStruct((owned, 2 * rows), F32)
    kept = owned if columns == 2 else 0
    *blocks, normed_own, sent = call(
        functools.partial(last_merge_kernel, skip, columns),
        [short] * columns
        + [jax.ShapeDtypeStruct((count, rows), F32), jax.ShapeDtypeStruct((count // 2 + kept, 2 * rows), F32)],
        sums,
        normed,
        *got,
    )
    mask = ctx_count // 2
    while mask > 2:
        for j in range(columns):
            if j & (mask >> 1):
                blocks[j] = ctx_swap(blocks[j], mask)
        mask //= 2
    if columns > 2:
        sent = jnp.concatenate([sent] + blocks[::2], axis=0)
    both = ctx_swap(sent, 1)
    for j in range(1, columns, 2):
        blocks[j] = to_owner(blocks[j])

    weight_grad = call(
        functools.partial(weight_grad_kernel, head_count, heads, owned, columns),
        jax.ShapeDtypeStruct((rows * heads, channels), F32),
        normed_own,
        both,
        own,
        *far,
        other,
        *far_other,
        scratch=[
            pltpu.VMEM((2, rows, columns * tokens * heads), F32),
            pltpu.VMEM((rows * heads, channels), F32),
            pltpu.SemaphoreType.DMA((4 if rows % 32 == 0 else 1,)),
        ],
        flops=2 * rows * heads * channels * ctx_count * tokens * heads,
        place=pl.ANY,
    )
    weight_grad, *blocks = lax.optimization_barrier((weight_grad, *blocks))
    latent_gradient = call(
        functools.partial(latent_kernel, head_count, columns),
        jax.ShapeDtypeStruct((owned, width), F32),
        rms,
        hat,
        gain_row,
        both,
        *blocks,
    )
    return latent_gradient[None], weight_grad.reshape(weight.shape)


def solution(mesh):
    return jax.shard_map(
        functools.partial(per_device, mesh.shape["head"], mesh.shape["ctx"]),
        mesh=mesh,
        in_specs=(
            P("ctx", "head", None),
            P(),
            P("ctx", None, "head", None),
            P("ctx", "head", None),
        ),
        out_specs=(P("ctx", "head", None), P("ctx", "head", None)),
        check_vma=False,
    )
```

```python
import functools

import jax
import jax.numpy as jnp
from jax import lax
from jax.experimental import pallas as pl
from jax.experimental.pallas import tpu as pltpu
from jax.sharding import PartitionSpec as P


F32 = jnp.float32
BF16 = jnp.bfloat16


PLANE = ((1, 1), (3, 2), (2, 0))


def iota(shape, axis):
    return lax.broadcasted_iota(jnp.int32, shape, axis)


def one_hot(condition):
    return jnp.where(condition, 1.0, 0.0).astype(BF16)


def matmul(a, b, a_axis=1, b_axis=0):
    return lax.dot_general(a, b, (((a_axis,), (b_axis,)), ((), ())), preferred_element_type=F32)


def whole(value, step):
    return value >> (step.bit_length() - 1) if step & (step - 1) == 0 else value // step


def rest(value, step):
    return value & (step - 1) if step & (step - 1) == 0 else value % step


def reverse_bits(value, count):
    out = 0
    for bit in range(count):
        out = out | (((value >> bit) & 1) << (count - 1 - bit))
    return out


def two_terms(value):
    high = value.astype(BF16).astype(F32)
    return jnp.concatenate([high, (value - high).astype(BF16).astype(F32)], axis=0)


def even_bits(value, count):
    out = 1 ^ (value & 1)
    for bit in range(1, count):
        out = out ^ ((value >> bit) & 1)
    return out


def crossing(head, column, bits):
    return even_bits(head, bits) ^ (column & 1) ^ 1


def weight_kernel(head_count, heads, owned, shards, own_ref, other_ref, out_ref, order_ref):
    rows = own_ref.shape[0] // heads
    group = min(rows, max(256 // heads, 1))
    size = group * heads
    to, at = iota((size, size), 0), iota((size, size), 1)
    order = one_hot(at == rest(to, group) * heads + whole(to, group))
    parts = [[] for _ in range(heads)]
    for ref in (own_ref, other_ref):
        for start in range(0, rows, group):
            moved = matmul(order, ref[pl.ds(start * heads, size), :])
            for h in range(heads):
                parts[h].append(moved[h * group : (h + 1) * group, :])
    for h in range(heads):
        out_ref[h] = jnp.concatenate(parts[h], axis=0).T.astype(BF16)
    me = lax.axis_index("head")
    bits = head_count.bit_length() - 1
    tokens = head_count * owned
    size = order_ref.shape[0]
    to, at = iota((size, size), 0), iota((size, size), 1)
    i, j = rest(to, owned), rest(whole(to, owned), shards)
    position = rest(whole(to, owned * shards), head_count)
    token = (reverse_bits(position, bits) ^ me) * owned + i
    order_ref[...] = one_hot(at == (j * tokens + token) * heads + whole(to, tokens * shards))


def partial_kernel(head_count, count, order_ref, weight_ref, *refs):
    shard_refs, (own_ref, other_ref), out_refs = refs[: -count - 2], refs[-count - 2 : -count], refs[-count:]
    core = lax.axis_index("ctx") & 1
    crossed = crossing(lax.axis_index("head"), lax.axis_index("ctx") >> 1, head_count.bit_length() - 1)
    first = jnp.where(crossed == 0, own_ref[...], other_ref[...])
    stacked = jnp.concatenate([first] + [ref[...] for ref in shard_refs], axis=0)
    moved = matmul(order_ref[...], stacked).astype(BF16)
    size, rows = out_refs[0].shape[0], out_refs[0].shape[1] // 2
    part = count * size
    heads, channels, width = weight_ref.shape
    left = jnp.concatenate([moved[h * part : (h + 1) * part] for h in range(heads)], axis=1)
    total = matmul(left, weight_ref[...].reshape(heads * channels, width))
    turned = jnp.concatenate([total[:, rows:], total[:, :rows]], axis=1)
    total = jnp.where(core == 0, total, turned)
    out_refs[0][...] = total[:size]
    for n, ref in enumerate(out_refs[1:]):
        ref[...] = two_terms(total[(n + 1) * size : (n + 2) * size]).astype(BF16)


def merge_kernel(skip, sums_ref, normed_ref, *refs):
    got_refs, keep_ref, message_ref = refs[:-2], refs[-2], refs[-1]
    total, rows = merged(skip, sums_ref, normed_ref, got_refs)
    half = keep_ref.shape[0]
    keep_ref[...] = total[:half]
    message_ref[...] = jnp.concatenate([two_terms(total[half:]), rows], axis=0).astype(BF16)


def last_merge_kernel(skip, columns, sums_ref, normed_ref, *refs):
    got_refs, block_refs, own_ref, sent_ref = refs[: -columns - 2], refs[-columns - 2 : -2], refs[-2], refs[-1]
    total, rows = merged(skip, sums_ref, normed_ref, got_refs)
    owned = total.shape[0] // columns
    for j, ref in enumerate(block_refs):
        ref[...] = total[j * owned : (j + 1) * owned]
    core = lax.axis_index("ctx") & 1
    count, width = rows.shape[0] // 2, rows.shape[1] // 2
    own_ref[...] = jnp.where(core == 0, rows[:, :width], rows[:, width:])
    sent = jnp.where(core == 0, rows[:, width:], rows[:, :width])
    sent = jnp.concatenate([sent[:count], sent[count:]], axis=1)
    sent_ref[...] = jnp.concatenate([sent, total[:owned]], axis=0) if columns == 2 else sent


def merged(skip, sums_ref, normed_ref, got_refs):
    total, half = sums_ref[...], sums_ref.shape[0]
    rows = [normed_ref[...].astype(F32)[skip:]]
    for ref in got_refs:
        got = ref[...].astype(F32)
        total = total + (got[:half] + got[half : 2 * half])
        rows.append(got[2 * half :])
    return total, jnp.concatenate(rows, axis=0)


def norm_kernel(columns, latent_ref, gain_ref, rms_ref, hat_ref, *out_refs):
    column = lax.axis_index("ctx") >> 1
    raw = latent_ref[...].astype(F32)
    rms = lax.rsqrt(jnp.mean(raw * raw, axis=1, keepdims=True) + 1e-06)
    hat = raw * rms
    rms_ref[...] = jnp.broadcast_to(rms, raw.shape)
    hat_ref[...] = hat
    normed = (hat * gain_ref[...]).astype(BF16)
    width = normed.shape[1] // columns
    for j, ref in enumerate(out_refs):
        block = normed[:, :width]
        for b in range(1, columns):
            block = jnp.where((column ^ j) == b, normed[:, b * width : (b + 1) * width], block)
        ref[...] = block


def weight_grad_kernel(head_count, heads, owned, columns, own_ref, other_ref, *refs):
    shard_refs, (out_ref, spread_ref, total_ref, sems) = refs[:-4], refs[-4:]
    me = lax.axis_index("head")
    core = lax.axis_index("ctx") & 1
    role = core ^ crossing(me, lax.axis_index("ctx") >> 1, head_count.bit_length() - 1)
    groups = sems.shape[0]
    rows = out_ref.shape[0] // heads // groups
    tokens = head_count * owned
    count, width = own_ref.shape[0] // 2, own_ref.shape[1]
    other = other_ref[...]
    normed = jnp.concatenate([own_ref[...], other[:count, :width], other[:count, width:]], axis=0).astype(BF16)
    size = columns * tokens * heads
    at, to = iota((normed.shape[0], size), 0), iota((1, size), 1)
    token, j = rest(whole(to, heads), tokens), whole(to, heads * tokens)
    distance = whole(token, owned) ^ me
    slot = distance ^ ((distance >> 1) & 1) if head_count >= 4 else distance
    turned = 1 ^ even_bits(distance, head_count.bit_length() - 1) ^ (j & 1)
    cots = []
    for side in range(2):
        held = jnp.where(j == 0, core, role) ^ side ^ core ^ turned
        place = ((held * head_count + slot) * columns + j) * owned + rest(token, owned)
        spread_ref[side] = matmul(normed, one_hot(at == place), 0, 0)
        cots.append(jnp.concatenate([r[...] for r in shard_refs[side * columns : (side + 1) * columns]], axis=0))
    keep = rest(iota((1, heads, size), 2), heads) == iota((1, heads, size), 1)
    copies = []
    for g in range(groups):
        total = None
        for side in range(2):
            block = spread_ref[side, g * rows : (g + 1) * rows, :]
            left = jnp.where(keep, block[:, None, :], 0.0).reshape(rows * heads, size).astype(BF16)
            part = matmul(left, cots[side])
            total = part if total is None else total + part
        place = pl.ds(g * rows * heads, rows * heads)
        total_ref[place, :] = total
        copies.append(pltpu.make_async_copy(total_ref.at[place], out_ref.at[place], sems.at[g]))
        copies[g].start()
    for copy in copies:
        copy.wait()


def latent_kernel(head_count, columns, rms_ref, hat_ref, gain_ref, other_ref, *refs):
    block_refs, out_ref = refs[:-1], refs[-1]
    column = lax.axis_index("ctx") >> 1
    crossed = crossing(lax.axis_index("head"), lax.axis_index("ctx") >> 1, head_count.bit_length() - 1)
    relative = [ref[...] for ref in block_refs]
    count = out_ref.shape[0]
    first = other_ref.shape[0] - count * columns // 2
    for j in range(0, columns, 2):
        place = first + j // 2 * count
        relative[j] = jnp.where(crossed == 0, relative[j], other_ref[place : place + count, :])
    blocks = []
    for b in range(columns):
        block = relative[0]
        for j in range(1, columns):
            block = jnp.where((column ^ j) == b, relative[j], block)
        blocks.append(block)
    scaled = jnp.concatenate(blocks, axis=1) * gain_ref[...]
    hat = hat_ref[...]
    inner = jnp.mean(scaled * hat, axis=1, keepdims=True)
    out_ref[...] = rms_ref[...] * (scaled - hat * inner)


def per_device(head_count, ctx_count, latent, gain, cotangent, weight):
    columns = ctx_count // 2
    owned, width = latent.shape[1:]
    _, tokens, heads, channels = cotangent.shape
    rows = weight.shape[0]
    bits = head_count.bit_length() - 1
    params = pltpu.CompilerParams(vmem_limit_bytes=48 * 1024 * 1024)

    def swap(value, partner):
        pairs = [
            (h * ctx_count + c, p * ctx_count + q)
            for h in range(head_count)
            for c in range(ctx_count)
            for p, q in [partner(h, c)]
        ]
        return lax.ppermute(value, ("head", "ctx"), pairs)

    def ctx_swap(value, mask):
        return swap(value, lambda h, c: (h, c ^ mask))

    def to_role(value):
        return swap(value, lambda h, c: (h, c ^ 2 ^ crossing(h, (c ^ 2) >> 1, bits)))

    def to_owner(value):
        return swap(value, lambda h, c: (h, c ^ 2 ^ crossing(h, c >> 1, bits)))

    def head_swap(value, mask):
        return swap(value, lambda h, c: (h ^ mask, c ^ 1 ^ even_bits(mask, bits)))

    def call(kernel, out, *args, scratch=(), flops=0, place=pltpu.VMEM):
        moved = sum(a.size * a.dtype.itemsize for a in args)
        return pl.pallas_call(
            kernel,
            out_shape=out,
            out_specs=jax.tree.map(lambda _: pl.BlockSpec(memory_space=place), out),
            scratch_shapes=scratch,
            compiler_params=params,
            cost_estimate=pl.CostEstimate(flops=flops, bytes_accessed=moved, transcendentals=0),
        )(*args)

    own = cotangent.reshape(tokens * heads, channels)
    far = [to_role(own)]
    other = ctx_swap(own, 1)
    if columns > 2:
        first = jnp.where(crossing(lax.axis_index("head"), lax.axis_index("ctx") >> 1, bits) == 0, own, other)
        shards = [first] + far
        mask = 4
        while mask < ctx_count:
            shards += [ctx_swap(s, mask) for s in shards]
            mask *= 2
        far = shards[1:]
    gain_row = gain.reshape(1, width)
    block = jax.ShapeDtypeStruct((owned, 2 * rows), BF16)
    row = jax.ShapeDtypeStruct((owned, width), F32)
    rms, hat, *normed = call(
        functools.partial(norm_kernel, columns), [row] * 2 + [block] * columns, latent[0], gain_row, flops=4 * 10**8
    )

    weight_flat = weight.reshape(rows * heads, channels)
    weight_other = ctx_swap(weight_flat, 1)
    weight_flat, weight_other, _ = lax.optimization_barrier((weight_flat, weight_other, normed[0]))
    size = columns * tokens * heads
    chip_weight, order = call(
        functools.partial(weight_kernel, head_count, heads, owned, columns),
        [jax.ShapeDtypeStruct((heads, channels, 2 * rows), BF16), jax.ShapeDtypeStruct((size, size), BF16)],
        weight_flat,
        weight_other,
    )

    mask = 2
    while mask < ctx_count:
        for j in range(columns):
            if j & (mask >> 1):
                normed[j] = ctx_swap(normed[j], mask | (mask == 2))
        mask *= 2
    normed = jnp.concatenate(normed, axis=0)

    size = head_count * columns * owned // 4
    sums, *sent = call(
        functools.partial(partial_kernel, head_count, 4),
        [jax.ShapeDtypeStruct((size, 2 * rows), F32)] + [jax.ShapeDtypeStruct((2 * size, 2 * rows), BF16)] * 3,
        order,
        chip_weight,
        *far,
        own,
        other,
    )
    sums, *far = lax.optimization_barrier((sums, *far))
    far_other = [ctx_swap(s, 1) for s in far]
    got = {m: head_swap(jnp.concatenate([sent[n], normed], axis=0), m) for m, n in PLANE}
    got = [got[m] for m in (1, 3, 2)]
    skip, count, mask = 0, 4 * normed.shape[0], 4
    while mask < head_count:
        half = sums.shape[0] // 2
        sums, normed = call(
            functools.partial(merge_kernel, skip),
            [jax.ShapeDtypeStruct((half, 2 * rows), F32), jax.ShapeDtypeStruct((2 * half + count, 2 * rows), BF16)],
            sums,
            normed,
            *got,
        )
        if mask == 4:
            normed, *far_other = lax.optimization_barrier((normed, *far_other))
        got = [head_swap(normed, mask)]
        skip, count, mask = 2 * half, 2 * count, 2 * mask
    short = jax.ShapeDtypeStruct((owned, 2 * rows), F32)
    kept = owned if columns == 2 else 0
    *blocks, normed_own, sent = call(
        functools.partial(last_merge_kernel, skip, columns),
        [short] * columns
        + [jax.ShapeDtypeStruct((count, rows), F32), jax.ShapeDtypeStruct((count // 2 + kept, 2 * rows), F32)],
        sums,
        normed,
        *got,
    )
    mask = ctx_count // 2
    while mask > 2:
        for j in range(columns):
            if j & (mask >> 1):
                blocks[j] = ctx_swap(blocks[j], mask)
        mask //= 2
    if columns > 2:
        sent = jnp.concatenate([sent] + blocks[::2], axis=0)
    both = ctx_swap(sent, 1)
    for j in range(1, columns, 2):
        blocks[j] = to_owner(blocks[j])

    weight_grad = call(
        functools.partial(weight_grad_kernel, head_count, heads, owned, columns),
        jax.ShapeDtypeStruct((rows * heads, channels), F32),
        normed_own,
        both,
        own,
        *far,
        other,
        *far_other,
        scratch=[
            pltpu.VMEM((2, rows, columns * tokens * heads), F32),
            pltpu.VMEM((rows * heads, channels), F32),
            pltpu.SemaphoreType.DMA((4 if rows % 32 == 0 else 1,)),
        ],
        flops=2 * rows * heads * channels * ctx_count * tokens * heads,
        place=pl.ANY,
    )
    weight_grad, *blocks = lax.optimization_barrier((weight_grad, *blocks))
    latent_gradient = call(
        functools.partial(latent_kernel, head_count, columns),
        jax.ShapeDtypeStruct((owned, width), F32),
        rms,
        hat,
        gain_row,
        both,
        *blocks,
    )
    return latent_gradient[None], weight_grad.reshape(weight.shape)


def solution(mesh):
    return jax.shard_map(
        functools.partial(per_device, mesh.shape["head"], mesh.shape["ctx"]),
        mesh=mesh,
        in_specs=(
            P("ctx", "head", None),
            P(),
            P("ctx", None, "head", None),
            P("ctx", "head", None),
        ),
        out_specs=(P("ctx", "head", None), P("ctx", "head", None)),
        check_vma=False,
    )
```

```python
import functools

import jax
import jax.numpy as jnp
from jax import lax
from jax.experimental import pallas as pl
from jax.experimental.pallas import tpu as pltpu
from jax.sharding import PartitionSpec as P


F32 = jnp.float32
BF16 = jnp.bfloat16


PLANE = ((1, 1), (3, 2), (2, 0))


def iota(shape, axis):
    return lax.broadcasted_iota(jnp.int32, shape, axis)


def one_hot(condition):
    return jnp.where(condition, 1.0, 0.0).astype(BF16)


def matmul(a, b, a_axis=1, b_axis=0):
    return lax.dot_general(a, b, (((a_axis,), (b_axis,)), ((), ())), preferred_element_type=F32)


def whole(value, step):
    return value >> (step.bit_length() - 1) if step & (step - 1) == 0 else value // step


def rest(value, step):
    return value & (step - 1) if step & (step - 1) == 0 else value % step


def reverse_bits(value, count):
    out = 0
    for bit in range(count):
        out = out | (((value >> bit) & 1) << (count - 1 - bit))
    return out


def two_terms(value):
    high = value.astype(BF16).astype(F32)
    return jnp.concatenate([high, (value - high).astype(BF16).astype(F32)], axis=0)


def even_bits(value, count):
    out = 1 ^ (value & 1)
    for bit in range(1, count):
        out = out ^ ((value >> bit) & 1)
    return out


def crossing(head, column, bits):
    return even_bits(head, bits) ^ (column & 1) ^ 1


def weight_kernel(head_count, heads, owned, shards, own_ref, other_ref, out_ref, order_ref):
    rows = own_ref.shape[0] // heads
    group = min(rows, max(256 // heads, 1))
    size = group * heads
    to, at = iota((size, size), 0), iota((size, size), 1)
    order = one_hot(at == rest(to, group) * heads + whole(to, group))
    parts = [[] for _ in range(heads)]
    for ref in (own_ref, other_ref):
        for start in range(0, rows, group):
            moved = matmul(order, ref[pl.ds(start * heads, size), :])
            for h in range(heads):
                parts[h].append(moved[h * group : (h + 1) * group, :])
    for h in range(heads):
        out_ref[h] = jnp.concatenate(parts[h], axis=0).T.astype(BF16)
    me = lax.axis_index("head")
    bits = head_count.bit_length() - 1
    tokens = head_count * owned
    size = order_ref.shape[0]
    to, at = iota((size, size), 0), iota((size, size), 1)
    i, j = rest(to, owned), rest(whole(to, owned), shards)
    position = rest(whole(to, owned * shards), head_count)
    token = (reverse_bits(position, bits) ^ me) * owned + i
    order_ref[...] = one_hot(at == (j * tokens + token) * heads + whole(to, tokens * shards))


def partial_kernel(head_count, count, order_ref, weight_ref, *refs):
    shard_refs, (own_ref, other_ref), out_refs = refs[: -count - 2], refs[-count - 2 : -count], refs[-count:]
    core = lax.axis_index("ctx") & 1
    crossed = crossing(lax.axis_index("head"), lax.axis_index("ctx") >> 1, head_count.bit_length() - 1)
    first = jnp.where(crossed == 0, own_ref[...], other_ref[...])
    stacked = jnp.concatenate([first] + [ref[...] for ref in shard_refs], axis=0)
    moved = matmul(order_ref[...], stacked).astype(BF16)
    size, rows = out_refs[0].shape[0], out_refs[0].shape[1] // 2
    part = count * size
    heads, channels, width = weight_ref.shape
    left = jnp.concatenate([moved[h * part : (h + 1) * part] for h in range(heads)], axis=1)
    total = matmul(left, weight_ref[...].reshape(heads * channels, width))
    turned = jnp.concatenate([total[:, rows:], total[:, :rows]], axis=1)
    total = jnp.where(core == 0, total, turned)
    out_refs[0][...] = total[:size]
    for n, ref in enumerate(out_refs[1:]):
        ref[...] = two_terms(total[(n + 1) * size : (n + 2) * size]).astype(BF16)


def merge_kernel(skip, sums_ref, normed_ref, *refs):
    got_refs, keep_ref, message_ref = refs[:-2], refs[-2], refs[-1]
    total, rows = merged(skip, sums_ref, normed_ref, got_refs)
    half = keep_ref.shape[0]
    keep_ref[...] = total[:half]
    message_ref[...] = jnp.concatenate([two_terms(total[half:]), rows], axis=0).astype(BF16)


def last_merge_kernel(skip, columns, sums_ref, normed_ref, *refs):
    got_refs, block_refs, own_ref, sent_ref = refs[: -columns - 2], refs[-columns - 2 : -2], refs[-2], refs[-1]
    total, rows = merged(skip, sums_ref, normed_ref, got_refs)
    owned = total.shape[0] // columns
    for j, ref in enumerate(block_refs):
        ref[...] = total[j * owned : (j + 1) * owned]
    core = lax.axis_index("ctx") & 1
    count, width = rows.shape[0] // 2, rows.shape[1] // 2
    own_ref[...] = jnp.where(core == 0, rows[:, :width], rows[:, width:])
    sent = jnp.where(core == 0, rows[:, width:], rows[:, :width])
    sent = jnp.concatenate([sent[:count], sent[count:]], axis=1)
    sent_ref[...] = jnp.concatenate([sent, total[:owned]], axis=0) if columns == 2 else sent


def merged(skip, sums_ref, normed_ref, got_refs):
    total, half = sums_ref[...], sums_ref.shape[0]
    rows = [normed_ref[...].astype(F32)[skip:]]
    for ref in got_refs:
        got = ref[...].astype(F32)
        total = total + (got[:half] + got[half : 2 * half])
        rows.append(got[2 * half :])
    return total, jnp.concatenate(rows, axis=0)


def norm_kernel(columns, latent_ref, gain_ref, rms_ref, hat_ref, *out_refs):
    column = lax.axis_index("ctx") >> 1
    raw = latent_ref[...].astype(F32)
    rms = lax.rsqrt(jnp.mean(raw * raw, axis=1, keepdims=True) + 1e-06)
    hat = raw * rms
    rms_ref[...] = jnp.broadcast_to(rms, raw.shape)
    hat_ref[...] = hat
    normed = (hat * gain_ref[...]).astype(BF16)
    width = normed.shape[1] // columns
    for j, ref in enumerate(out_refs):
        block = normed[:, :width]
        for b in range(1, columns):
            block = jnp.where((column ^ j) == b, normed[:, b * width : (b + 1) * width], block)
        ref[...] = block


def weight_grad_kernel(head_count, heads, owned, columns, own_ref, other_ref, *refs):
    shard_refs, (out_ref, spread_ref, total_ref, sems) = refs[:-4], refs[-4:]
    me = lax.axis_index("head")
    core = lax.axis_index("ctx") & 1
    role = core ^ crossing(me, lax.axis_index("ctx") >> 1, head_count.bit_length() - 1)
    groups = sems.shape[0]
    rows = out_ref.shape[0] // heads // groups
    tokens = head_count * owned
    count, width = own_ref.shape[0] // 2, own_ref.shape[1]
    other = other_ref[...]
    normed = jnp.concatenate([own_ref[...], other[:count, :width], other[:count, width:]], axis=0).astype(BF16)
    size = columns * tokens * heads
    at, to = iota((normed.shape[0], size), 0), iota((1, size), 1)
    token, j = rest(whole(to, heads), tokens), whole(to, heads * tokens)
    distance = whole(token, owned) ^ me
    slot = distance ^ ((distance >> 1) & 1) if head_count >= 4 else distance
    turned = 1 ^ even_bits(distance, head_count.bit_length() - 1) ^ (j & 1)
    cots = []
    for side in range(2):
        held = jnp.where(j == 0, core, role) ^ side ^ core ^ turned
        place = ((held * head_count + slot) * columns + j) * owned + rest(token, owned)
        spread_ref[side] = matmul(normed, one_hot(at == place), 0, 0)
        cots.append(jnp.concatenate([r[...] for r in shard_refs[side * columns : (side + 1) * columns]], axis=0))
    keep = rest(iota((1, heads, size), 2), heads) == iota((1, heads, size), 1)
    both_cots = jnp.concatenate(cots, axis=0)
    copies = []
    for g in range(groups):
        lefts = []
        for side in range(2):
            block = spread_ref[side, g * rows : (g + 1) * rows, :]
            lefts.append(jnp.where(keep, block[:, None, :], 0.0).reshape(rows * heads, size).astype(BF16))
        total = matmul(jnp.concatenate(lefts, axis=1), both_cots)
        place = pl.ds(g * rows * heads, rows * heads)
        total_ref[place, :] = total
        copies.append(pltpu.make_async_copy(total_ref.at[place], out_ref.at[place], sems.at[g]))
        copies[g].start()
    for copy in copies:
        copy.wait()


def latent_kernel(head_count, columns, rms_ref, hat_ref, gain_ref, other_ref, *refs):
    block_refs, out_ref = refs[:-1], refs[-1]
    column = lax.axis_index("ctx") >> 1
    crossed = crossing(lax.axis_index("head"), lax.axis_index("ctx") >> 1, head_count.bit_length() - 1)
    relative = [ref[...] for ref in block_refs]
    count = out_ref.shape[0]
    first = other_ref.shape[0] - count * columns // 2
    for j in range(0, columns, 2):
        place = first + j // 2 * count
        relative[j] = jnp.where(crossed == 0, relative[j], other_ref[place : place + count, :])
    blocks = []
    for b in range(columns):
        block = relative[0]
        for j in range(1, columns):
            block = jnp.where((column ^ j) == b, relative[j], block)
        blocks.append(block)
    scaled = jnp.concatenate(blocks, axis=1) * gain_ref[...]
    hat = hat_ref[...]
    inner = jnp.mean(scaled * hat, axis=1, keepdims=True)
    out_ref[...] = rms_ref[...] * (scaled - hat * inner)


def per_device(head_count, ctx_count, latent, gain, cotangent, weight):
    columns = ctx_count // 2
    owned, width = latent.shape[1:]
    _, tokens, heads, channels = cotangent.shape
    rows = weight.shape[0]
    bits = head_count.bit_length() - 1
    params = pltpu.CompilerParams(vmem_limit_bytes=48 * 1024 * 1024)

    def swap(value, partner):
        pairs = [
            (h * ctx_count + c, p * ctx_count + q)
            for h in range(head_count)
            for c in range(ctx_count)
            for p, q in [partner(h, c)]
        ]
        return lax.ppermute(value, ("head", "ctx"), pairs)

    def ctx_swap(value, mask):
        return swap(value, lambda h, c: (h, c ^ mask))

    def to_role(value):
        return swap(value, lambda h, c: (h, c ^ 2 ^ crossing(h, (c ^ 2) >> 1, bits)))

    def to_owner(value):
        return swap(value, lambda h, c: (h, c ^ 2 ^ crossing(h, c >> 1, bits)))

    def head_swap(value, mask):
        return swap(value, lambda h, c: (h ^ mask, c ^ 1 ^ even_bits(mask, bits)))

    def call(kernel, out, *args, scratch=(), flops=0, place=pltpu.VMEM):
        moved = sum(a.size * a.dtype.itemsize for a in args)
        return pl.pallas_call(
            kernel,
            out_shape=out,
            out_specs=jax.tree.map(lambda _: pl.BlockSpec(memory_space=place), out),
            scratch_shapes=scratch,
            compiler_params=params,
            cost_estimate=pl.CostEstimate(flops=flops, bytes_accessed=moved, transcendentals=0),
        )(*args)

    own = cotangent.reshape(tokens * heads, channels)
    far = [to_role(own)]
    other = ctx_swap(own, 1)
    if columns > 2:
        first = jnp.where(crossing(lax.axis_index("head"), lax.axis_index("ctx") >> 1, bits) == 0, own, other)
        shards = [first] + far
        mask = 4
        while mask < ctx_count:
            shards += [ctx_swap(s, mask) for s in shards]
            mask *= 2
        far = shards[1:]
    gain_row = gain.reshape(1, width)
    block = jax.ShapeDtypeStruct((owned, 2 * rows), BF16)
    row = jax.ShapeDtypeStruct((owned, width), F32)
    rms, hat, *normed = call(
        functools.partial(norm_kernel, columns), [row] * 2 + [block] * columns, latent[0], gain_row, flops=4 * 10**8
    )

    weight_flat = weight.reshape(rows * heads, channels)
    weight_other = ctx_swap(weight_flat, 1)
    weight_flat, weight_other, _ = lax.optimization_barrier((weight_flat, weight_other, normed[0]))
    size = columns * tokens * heads
    chip_weight, order = call(
        functools.partial(weight_kernel, head_count, heads, owned, columns),
        [jax.ShapeDtypeStruct((heads, channels, 2 * rows), BF16), jax.ShapeDtypeStruct((size, size), BF16)],
        weight_flat,
        weight_other,
    )

    mask = 2
    while mask < ctx_count:
        for j in range(columns):
            if j & (mask >> 1):
                normed[j] = ctx_swap(normed[j], mask | (mask == 2))
        mask *= 2
    normed = jnp.concatenate(normed, axis=0)

    size = head_count * columns * owned // 4
    sums, *sent = call(
        functools.partial(partial_kernel, head_count, 4),
        [jax.ShapeDtypeStruct((size, 2 * rows), F32)] + [jax.ShapeDtypeStruct((2 * size, 2 * rows), BF16)] * 3,
        order,
        chip_weight,
        *far,
        own,
        other,
    )
    sums, *far = lax.optimization_barrier((sums, *far))
    far_other = [ctx_swap(s, 1) for s in far]
    got = {m: head_swap(jnp.concatenate([sent[n], normed], axis=0), m) for m, n in PLANE}
    got = [got[m] for m in (1, 3, 2)]
    skip, count, mask = 0, 4 * normed.shape[0], 4
    while mask < head_count:
        half = sums.shape[0] // 2
        sums, normed = call(
            functools.partial(merge_kernel, skip),
            [jax.ShapeDtypeStruct((half, 2 * rows), F32), jax.ShapeDtypeStruct((2 * half + count, 2 * rows), BF16)],
            sums,
            normed,
            *got,
        )
        if mask == 4:
            normed, *far_other = lax.optimization_barrier((normed, *far_other))
        got = [head_swap(normed, mask)]
        skip, count, mask = 2 * half, 2 * count, 2 * mask
    short = jax.ShapeDtypeStruct((owned, 2 * rows), F32)
    kept = owned if columns == 2 else 0
    *blocks, normed_own, sent = call(
        functools.partial(last_merge_kernel, skip, columns),
        [short] * columns
        + [jax.ShapeDtypeStruct((count, rows), F32), jax.ShapeDtypeStruct((count // 2 + kept, 2 * rows), F32)],
        sums,
        normed,
        *got,
    )
    mask = ctx_count // 2
    while mask > 2:
        for j in range(columns):
            if j & (mask >> 1):
                blocks[j] = ctx_swap(blocks[j], mask)
        mask //= 2
    if columns > 2:
        sent = jnp.concatenate([sent] + blocks[::2], axis=0)
    both = ctx_swap(sent, 1)
    for j in range(1, columns, 2):
        blocks[j] = to_owner(blocks[j])

    weight_grad = call(
        functools.partial(weight_grad_kernel, head_count, heads, owned, columns),
        jax.ShapeDtypeStruct((rows * heads, channels), F32),
        normed_own,
        both,
        own,
        *far,
        other,
        *far_other,
        scratch=[
            pltpu.VMEM((2, rows, columns * tokens * heads), F32),
            pltpu.VMEM((rows * heads, channels), F32),
            pltpu.SemaphoreType.DMA((4 if rows % 32 == 0 else 1,)),
        ],
        flops=2 * rows * heads * channels * ctx_count * tokens * heads,
        place=pl.ANY,
    )
    weight_grad, *blocks = lax.optimization_barrier((weight_grad, *blocks))
    latent_gradient = call(
        functools.partial(latent_kernel, head_count, columns),
        jax.ShapeDtypeStruct((owned, width), F32),
        rms,
        hat,
        gain_row,
        both,
        *blocks,
    )
    return latent_gradient[None], weight_grad.reshape(weight.shape)


def solution(mesh):
    return jax.shard_map(
        functools.partial(per_device, mesh.shape["head"], mesh.shape["ctx"]),
        mesh=mesh,
        in_specs=(
            P("ctx", "head", None),
            P(),
            P("ctx", None, "head", None),
            P("ctx", "head", None),
        ),
        out_specs=(P("ctx", "head", None), P("ctx", "head", None)),
        check_vma=False,
    )
```

```python
import functools

import jax
import jax.numpy as jnp
from jax import lax
from jax.experimental import pallas as pl
from jax.experimental.pallas import tpu as pltpu
from jax.sharding import PartitionSpec as P


F32 = jnp.float32
BF16 = jnp.bfloat16


PLANE = ((1, 1), (3, 2), (2, 0))


def iota(shape, axis):
    return lax.broadcasted_iota(jnp.int32, shape, axis)


def one_hot(condition):
    return jnp.where(condition, 1.0, 0.0).astype(BF16)


def matmul(a, b, a_axis=1, b_axis=0):
    return lax.dot_general(a, b, (((a_axis,), (b_axis,)), ((), ())), preferred_element_type=F32)


def whole(value, step):
    return value >> (step.bit_length() - 1) if step & (step - 1) == 0 else value // step


def rest(value, step):
    return value & (step - 1) if step & (step - 1) == 0 else value % step


def reverse_bits(value, count):
    out = 0
    for bit in range(count):
        out = out | (((value >> bit) & 1) << (count - 1 - bit))
    return out


def two_terms(value):
    high = value.astype(BF16).astype(F32)
    return jnp.concatenate([high, (value - high).astype(BF16).astype(F32)], axis=0)


def even_bits(value, count):
    out = 1 ^ (value & 1)
    for bit in range(1, count):
        out = out ^ ((value >> bit) & 1)
    return out


def crossing(head, column, bits):
    return even_bits(head, bits) ^ (column & 1) ^ 1


def weight_kernel(head_count, heads, owned, shards, own_ref, other_ref, out_ref, order_ref):
    rows = own_ref.shape[0] // heads
    group = min(rows, max(256 // heads, 1))
    size = group * heads
    to, at = iota((size, size), 0), iota((size, size), 1)
    order = one_hot(at == rest(to, group) * heads + whole(to, group))
    parts = [[] for _ in range(heads)]
    for ref in (own_ref, other_ref):
        for start in range(0, rows, group):
            moved = matmul(order, ref[pl.ds(start * heads, size), :])
            for h in range(heads):
                parts[h].append(moved[h * group : (h + 1) * group, :])
    for h in range(heads):
        out_ref[h] = jnp.concatenate(parts[h], axis=0).T.astype(BF16)
    me = lax.axis_index("head")
    bits = head_count.bit_length() - 1
    tokens = head_count * owned
    size = order_ref.shape[0]
    to, at = iota((size, size), 0), iota((size, size), 1)
    i, j = rest(to, owned), rest(whole(to, owned), shards)
    position = rest(whole(to, owned * shards), head_count)
    token = (reverse_bits(position, bits) ^ me) * owned + i
    order_ref[...] = one_hot(at == (j * tokens + token) * heads + whole(to, tokens * shards))


def partial_kernel(head_count, count, order_ref, weight_ref, *refs):
    shard_refs, (own_ref, other_ref), out_refs = refs[: -count - 2], refs[-count - 2 : -count], refs[-count:]
    core = lax.axis_index("ctx") & 1
    crossed = crossing(lax.axis_index("head"), lax.axis_index("ctx") >> 1, head_count.bit_length() - 1)
    first = jnp.where(crossed == 0, own_ref[...], other_ref[...])
    stacked = jnp.concatenate([first] + [ref[...] for ref in shard_refs], axis=0)
    moved = matmul(order_ref[...], stacked).astype(BF16)
    size, rows = out_refs[0].shape[0], out_refs[0].shape[1] // 2
    part = count * size
    total = matmul(moved[:part], weight_ref[0])
    for h in range(1, weight_ref.shape[0]):
        total += matmul(moved[h * part : (h + 1) * part], weight_ref[h])
    turned = jnp.concatenate([total[:, rows:], total[:, :rows]], axis=1)
    total = jnp.where(core == 0, total, turned)
    out_refs[0][...] = total[:size]
    for n, ref in enumerate(out_refs[1:]):
        ref[...] = two_terms(total[(n + 1) * size : (n + 2) * size]).astype(BF16)


def merge_kernel(skip, sums_ref, normed_ref, *refs):
    got_refs, keep_ref, message_ref = refs[:-2], refs[-2], refs[-1]
    total, rows = merged(skip, sums_ref, normed_ref, got_refs)
    half = keep_ref.shape[0]
    keep_ref[...] = total[:half]
    message_ref[...] = jnp.concatenate([two_terms(total[half:]), rows], axis=0).astype(BF16)


def last_merge_kernel(skip, columns, sums_ref, normed_ref, *refs):
    got_refs, block_refs, own_ref, sent_ref = refs[: -columns - 2], refs[-columns - 2 : -2], refs[-2], refs[-1]
    total, rows = merged(skip, sums_ref, normed_ref, got_refs)
    owned = total.shape[0] // columns
    for j, ref in enumerate(block_refs):
        ref[...] = total[j * owned : (j + 1) * owned]
    core = lax.axis_index("ctx") & 1
    count, width = rows.shape[0] // 2, rows.shape[1] // 2
    own_ref[...] = jnp.where(core == 0, rows[:, :width], rows[:, width:])
    sent = jnp.where(core == 0, rows[:, width:], rows[:, :width])
    sent = jnp.concatenate([sent[:count], sent[count:]], axis=1)
    sent_ref[...] = jnp.concatenate([sent, total[:owned]], axis=0) if columns == 2 else sent


def merged(skip, sums_ref, normed_ref, got_refs):
    total, half = sums_ref[...], sums_ref.shape[0]
    rows = [normed_ref[...].astype(F32)[skip:]]
    for ref in got_refs:
        got = ref[...].astype(F32)
        total = total + (got[:half] + got[half : 2 * half])
        rows.append(got[2 * half :])
    return total, jnp.concatenate(rows, axis=0)


def norm_kernel(columns, latent_ref, gain_ref, rms_ref, hat_ref, *out_refs):
    column = lax.axis_index("ctx") >> 1
    raw = latent_ref[...].astype(F32)
    rms = lax.rsqrt(jnp.mean(raw * raw, axis=1, keepdims=True) + 1e-06)
    hat = raw * rms
    rms_ref[...] = jnp.broadcast_to(rms, raw.shape)
    hat_ref[...] = hat
    normed = (hat * gain_ref[...]).astype(BF16)
    width = normed.shape[1] // columns
    for j, ref in enumerate(out_refs):
        block = normed[:, :width]
        for b in range(1, columns):
            block = jnp.where((column ^ j) == b, normed[:, b * width : (b + 1) * width], block)
        ref[...] = block


def weight_grad_kernel(head_count, heads, owned, columns, own_ref, other_ref, *refs):
    shard_refs, (out_ref, spread_ref, total_ref, sems) = refs[:-4], refs[-4:]
    me = lax.axis_index("head")
    core = lax.axis_index("ctx") & 1
    role = core ^ crossing(me, lax.axis_index("ctx") >> 1, head_count.bit_length() - 1)
    groups = sems.shape[0]
    rows = out_ref.shape[0] // heads // groups
    tokens = head_count * owned
    count, width = own_ref.shape[0] // 2, own_ref.shape[1]
    other = other_ref[...]
    normed = jnp.concatenate([own_ref[...], other[:count, :width], other[:count, width:]], axis=0).astype(BF16)
    size = columns * tokens * heads
    at, to = iota((normed.shape[0], size), 0), iota((1, size), 1)
    token, j = rest(whole(to, heads), tokens), whole(to, heads * tokens)
    distance = whole(token, owned) ^ me
    slot = distance ^ ((distance >> 1) & 1) if head_count >= 4 else distance
    turned = 1 ^ even_bits(distance, head_count.bit_length() - 1) ^ (j & 1)
    cots = []
    for side in range(2):
        held = jnp.where(j == 0, core, role) ^ side ^ core ^ turned
        place = ((held * head_count + slot) * columns + j) * owned + rest(token, owned)
        spread_ref[side] = matmul(normed, one_hot(at == place), 0, 0)
        cots.append(jnp.concatenate([r[...] for r in shard_refs[side * columns : (side + 1) * columns]], axis=0))
    keep = rest(iota((1, heads, size), 2), heads) == iota((1, heads, size), 1)
    copies = []
    for g in range(groups):
        total = None
        for side in range(2):
            block = spread_ref[side, g * rows : (g + 1) * rows, :]
            left = jnp.where(keep, block[:, None, :], 0.0).reshape(rows * heads, size).astype(BF16)
            part = matmul(left, cots[side])
            total = part if total is None else total + part
        place = pl.ds(g * rows * heads, rows * heads)
        total_ref[place, :] = total
        copies.append(pltpu.make_async_copy(total_ref.at[place], out_ref.at[place], sems.at[g]))
        copies[g].start()
    for copy in copies:
        copy.wait()


def latent_kernel(head_count, columns, rms_ref, hat_ref, gain_ref, other_ref, *refs):
    block_refs, out_ref = refs[:-1], refs[-1]
    column = lax.axis_index("ctx") >> 1
    crossed = crossing(lax.axis_index("head"), lax.axis_index("ctx") >> 1, head_count.bit_length() - 1)
    relative = [ref[...] for ref in block_refs]
    count = out_ref.shape[0]
    first = other_ref.shape[0] - count * columns // 2
    for j in range(0, columns, 2):
        place = first + j // 2 * count
        relative[j] = jnp.where(crossed == 0, relative[j], other_ref[place : place + count, :])
    blocks = []
    for b in range(columns):
        block = relative[0]
        for j in range(1, columns):
            block = jnp.where((column ^ j) == b, relative[j], block)
        blocks.append(block)
    scaled = jnp.concatenate(blocks, axis=1) * gain_ref[...]
    hat = hat_ref[...]
    inner = jnp.mean(scaled * hat, axis=1, keepdims=True)
    out_ref[...] = rms_ref[...] * (scaled - hat * inner)


def per_device(head_count, ctx_count, latent, gain, cotangent, weight):
    columns = ctx_count // 2
    owned, width = latent.shape[1:]
    _, tokens, heads, channels = cotangent.shape
    rows = weight.shape[0]
    bits = head_count.bit_length() - 1
    params = pltpu.CompilerParams(vmem_limit_bytes=48 * 1024 * 1024)

    def swap(value, partner):
        pairs = [
            (h * ctx_count + c, p * ctx_count + q)
            for h in range(head_count)
            for c in range(ctx_count)
            for p, q in [partner(h, c)]
        ]
        return lax.ppermute(value, ("head", "ctx"), pairs)

    def ctx_swap(value, mask):
        return swap(value, lambda h, c: (h, c ^ mask))

    def to_role(value):
        return swap(value, lambda h, c: (h, c ^ 2 ^ crossing(h, (c ^ 2) >> 1, bits)))

    def to_owner(value):
        return swap(value, lambda h, c: (h, c ^ 2 ^ crossing(h, c >> 1, bits)))

    def head_swap(value, mask):
        return swap(value, lambda h, c: (h ^ mask, c ^ 1 ^ even_bits(mask, bits)))

    def call(kernel, out, *args, scratch=(), flops=0, place=pltpu.VMEM):
        moved = sum(a.size * a.dtype.itemsize for a in args)
        return pl.pallas_call(
            kernel,
            out_shape=out,
            out_specs=jax.tree.map(lambda _: pl.BlockSpec(memory_space=place), out),
            scratch_shapes=scratch,
            compiler_params=params,
            cost_estimate=pl.CostEstimate(flops=flops, bytes_accessed=moved, transcendentals=0),
        )(*args)

    own = cotangent.reshape(tokens * heads, channels)
    far = [to_role(own)]
    other = ctx_swap(own, 1)
    if columns > 2:
        first = jnp.where(crossing(lax.axis_index("head"), lax.axis_index("ctx") >> 1, bits) == 0, own, other)
        shards = [first] + far
        mask = 4
        while mask < ctx_count:
            shards += [ctx_swap(s, mask) for s in shards]
            mask *= 2
        far = shards[1:]
    gain_row = gain.reshape(1, width)
    block = jax.ShapeDtypeStruct((owned, 2 * rows), BF16)
    row = jax.ShapeDtypeStruct((owned, width), F32)
    rms, hat, *normed = call(
        functools.partial(norm_kernel, columns), [row] * 2 + [block] * columns, latent[0], gain_row, flops=4 * 10**8
    )

    weight_flat = weight.reshape(rows * heads, channels)
    weight_other = ctx_swap(weight_flat, 1)
    weight_flat, weight_other, _ = lax.optimization_barrier((weight_flat, weight_other, normed[0]))
    size = columns * tokens * heads
    chip_weight, order = call(
        functools.partial(weight_kernel, head_count, heads, owned, columns),
        [jax.ShapeDtypeStruct((heads, channels, 2 * rows), BF16), jax.ShapeDtypeStruct((size, size), BF16)],
        weight_flat,
        weight_other,
    )

    mask = 2
    while mask < ctx_count:
        for j in range(columns):
            if j & (mask >> 1):
                normed[j] = ctx_swap(normed[j], mask | (mask == 2))
        mask *= 2
    normed = jnp.concatenate(normed, axis=0)

    size = head_count * columns * owned // 4
    sums, *sent = call(
        functools.partial(partial_kernel, head_count, 4),
        [jax.ShapeDtypeStruct((size, 2 * rows), F32)] + [jax.ShapeDtypeStruct((2 * size, 2 * rows), BF16)] * 3,
        order,
        chip_weight,
        *far,
        own,
        other,
    )
    sums, *far = lax.optimization_barrier((sums, *far))
    far_other = [ctx_swap(s, 1) for s in far]
    got = {m: head_swap(jnp.concatenate([sent[n], normed], axis=0), m) for m, n in PLANE}
    got = [got[m] for m in (1, 3, 2)]
    skip, count, mask = 0, 4 * normed.shape[0], 4
    while mask < head_count:
        half = sums.shape[0] // 2
        sums, normed = call(
            functools.partial(merge_kernel, skip),
            [jax.ShapeDtypeStruct((half, 2 * rows), F32), jax.ShapeDtypeStruct((2 * half + count, 2 * rows), BF16)],
            sums,
            normed,
            *got,
        )
        if mask == 4:
            normed, *far_other = lax.optimization_barrier((normed, *far_other))
        got = [head_swap(normed, mask)]
        skip, count, mask = 2 * half, 2 * count, 2 * mask
    short = jax.ShapeDtypeStruct((owned, 2 * rows), F32)
    kept = owned if columns == 2 else 0
    *blocks, normed_own, sent = call(
        functools.partial(last_merge_kernel, skip, columns),
        [short] * columns
        + [jax.ShapeDtypeStruct((count, rows), F32), jax.ShapeDtypeStruct((count // 2 + kept, 2 * rows), F32)],
        sums,
        normed,
        *got,
    )
    mask = ctx_count // 2
    while mask > 2:
        for j in range(columns):
            if j & (mask >> 1):
                blocks[j] = ctx_swap(blocks[j], mask)
        mask //= 2
    if columns > 2:
        sent = jnp.concatenate([sent] + blocks[::2], axis=0)
    both = ctx_swap(sent, 1)
    for j in range(1, columns, 2):
        blocks[j] = to_owner(blocks[j])

    weight_grad = call(
        functools.partial(weight_grad_kernel, head_count, heads, owned, columns),
        jax.ShapeDtypeStruct((rows * heads, channels), F32),
        normed_own,
        both,
        own,
        *far,
        other,
        *far_other,
        scratch=[
            pltpu.VMEM((2, rows, columns * tokens * heads), F32),
            pltpu.VMEM((rows * heads, channels), F32),
            pltpu.SemaphoreType.DMA((8 if rows % 64 == 0 else 1,)),
        ],
        flops=2 * rows * heads * channels * ctx_count * tokens * heads,
        place=pl.ANY,
    )
    weight_grad, *blocks = lax.optimization_barrier((weight_grad, *blocks))
    latent_gradient = call(
        functools.partial(latent_kernel, head_count, columns),
        jax.ShapeDtypeStruct((owned, width), F32),
        rms,
        hat,
        gain_row,
        both,
        *blocks,
    )
    return latent_gradient[None], weight_grad.reshape(weight.shape)


def solution(mesh):
    return jax.shard_map(
        functools.partial(per_device, mesh.shape["head"], mesh.shape["ctx"]),
        mesh=mesh,
        in_specs=(
            P("ctx", "head", None),
            P(),
            P("ctx", None, "head", None),
            P("ctx", "head", None),
        ),
        out_specs=(P("ctx", "head", None), P("ctx", "head", None)),
        check_vma=False,
    )
```
